32 devices in a mesh: seq: 8 (over z, x), dp: 4 (over y, core).
Axes of the slice: x: 2, y: 2, z: 4, core: 2. Of those that a mesh axis runs over, the one named last changes fastest.
Arguments:
- tokens: bfloat16 [8, 1024, 2048], P('dp', 'seq'), may hold values from -6 to 6
- per_layer: bfloat16 [8, 1024, 256], P('dp', 'seq'), may hold values from -6 to 6
- positions: int32 [8, 1024], P('dp', 'seq'), may hold values from 0 to 1023, as said below
- span_start: int32 [8, 2], P('dp'), may hold values from 0 to 768, as said below
- cotangent: bfloat16 [8, 1024, 2048], P('dp', 'seq'), may hold values from -6 to 6
- query_weight: bfloat16 [2048, 2048], P(('seq', 'dp')), may hold values from -0.125 to 0.125
- key_weight: bfloat16 [2048, 512], P(('seq', 'dp')), may hold values from -0.125 to 0.125
- value_weight: bfloat16 [2048, 512], P(('seq', 'dp')), may hold values from -0.125 to 0.125
- output_weight: bfloat16 [2048, 2048], P(('seq', 'dp')), may hold values from -0.125 to 0.125
- laurel_left: bfloat16 [2048, 64], P(('seq', 'dp')), may hold values from -0.125 to 0.125
- laurel_right: bfloat16 [2048, 64], P(('seq', 'dp')), may hold values from -0.75 to 0.75
- gate_weight: bfloat16 [2048, 8192], P(('seq', 'dp')), may hold values from -0.125 to 0.125
- up_weight: bfloat16 [2048, 8192], P(('seq', 'dp')), may hold values from -0.125 to 0.125
- down_weight: bfloat16 [2048, 8192], P(('seq', 'dp')), may hold values from -0.0625 to 0.0625
- side_gate: bfloat16 [2048, 256], P(('seq', 'dp')), may hold values from -0.125 to 0.125
- side_output: bfloat16 [2048, 256], P(('seq', 'dp')), may hold values from -0.375 to 0.375
- norm_input: float32 [2048], replicated, may hold values from 0.25 to 1.75
- norm_attn: float32 [2048], replicated, may hold values from 0.25 to 1.75
- norm_laurel: float32 [2048], replicated, may hold values from 0.25 to 1.75
- norm_before: float32 [2048], replicated, may hold values from 0.25 to 1.75
- norm_after: float32 [2048], replicated, may hold values from 0.25 to 1.75
- norm_layer: float32 [2048], replicated, may hold values from 0.25 to 1.75
- norm_query: float32 [256], replicated, may hold values from 0.2 to 0.5
- norm_key: float32 [256], replicated, may hold values from 0.2 to 0.5
Outputs:
- output: bfloat16 [8, 1024, 2048], P('dp', 'seq')
- grad_tokens: float32 [8, 1024, 2048], P('dp', 'seq')
- grad_per_layer: float32 [8, 1024, 256], P('dp', 'seq')
- grad_query: float32 [2048, 2048], P(('seq', 'dp'))
- grad_key: float32 [2048, 512], P(('seq', 'dp'))
- grad_value: float32 [2048, 512], P(('seq', 'dp'))
- grad_output: float32 [2048, 2048], P(('seq', 'dp'))
- grad_left: float32 [2048, 64], P(('seq', 'dp'))
- grad_right: float32 [2048, 64], P(('seq', 'dp'))
- grad_gate: float32 [2048, 8192], P(('seq', 'dp'))
- grad_up: float32 [2048, 8192], P(('seq', 'dp'))
- grad_down: float32 [2048, 8192], P(('seq', 'dp'))
- grad_side_gate: float32 [2048, 256], P(('seq', 'dp'))
- grad_side_output: float32 [2048, 256], P(('seq', 'dp'))
- grad_norm_input: float32 [2048], replicated
- grad_norm_attn: float32 [2048], replicated
- grad_norm_laurel: float32 [2048], replicated
- grad_norm_before: float32 [2048], replicated
- grad_norm_after: float32 [2048], replicated
- grad_norm_layer: float32 [2048], replicated
- grad_norm_query: float32 [256], replicated
- grad_norm_key: float32 [256], replicated
The draws below stay inside these ranges and needn't reach their ends.
Inputs may be any that keep to these rules, and one draw needn't show every extreme that they name: Each sequence is a pack of documents: a token's position is the number of tokens before it in its own document, so positions rise by 1 and fall to 0 where a new document begins; the first token of a sequence has position 0, and one sequence is a single document. `span_start`: each sequence holds 2 picture spans of 256 tokens; span s starts within tokens [4 * s * 128, 4 * (s + 1) * 128 - 256], so spans never intersect.
All inputs are finite; a program needn't handle non-finite values.
Results may differ from the reference program's by a relative error of at most 0.019.
Values may be sent and summed in bfloat16 or wider, within the bound.
No kernel may reach another device: no remote copies, remote signals or barrier semaphores. Data moves between devices by JAX's collectives and lax.ppermute only.
A program may use at most 448 MiB of HBM per device.

```python
import math
import jax
import jax.numpy as jnp
from jax import lax

D = 2048
H = 8
KVH = 2
HD = 256
FF = 8192
R = 64
PL = 256
WINDOW = 512
SPAN = 256
L = 1024
NSEQ = 8
NSPAN = 2


def draw_positions(key, part):
    key_marks = jax.random.fold_in(key, 11)
    key_drawn = jax.random.fold_in(key, 12)
    marks = jax.random.randint(key_marks, (NSEQ, L), 0, WINDOW) == 0
    drawn = jax.random.randint(key_drawn, (), 0, NSEQ)
    seq_rows = jnp.arange(NSEQ, dtype=jnp.int32)
    places = jnp.arange(L, dtype=jnp.int32)
    marks = marks & (seq_rows != drawn)[:, None]
    marks = marks | (places == 0)[None, :]
    begins = jnp.where(marks, places[None, :], 0).astype(jnp.int32)
    latest = lax.cummax(begins, axis=1)
    return (places[None, :] - latest).astype(jnp.int32)


def draw_span_start(key, part):
    region = L // NSPAN
    within = jax.random.randint(key, (NSEQ, NSPAN), 0, region - SPAN + 1)
    return (within + region * jnp.arange(NSPAN, dtype=jnp.int32)[None, :]).astype(jnp.int32)


def spiked(values, rng, source, target, blocks, factor):
    def block_of(axis_at):
        return (jnp.arange(values.shape[axis_at]) // (values.shape[axis_at] // blocks)).reshape((-1,) + (1,) * (values.ndim - 1 - axis_at))

    one_side = jax.random.permutation(rng, blocks)[block_of(target)]
    other_side = (block_of(target) + blocks // 2) % blocks
    return jnp.where((block_of(source) == one_side) | (block_of(source) == other_side), factor * values, values)


def steps_of(rng, shape, pieces, smallest, largest):
    loudness, own = 1.0, jax.random.fold_in(rng, 6)
    for dim, parts in pieces:
        draws = jnp.exp(jax.random.uniform(jax.random.fold_in(own, dim), (parts,), jnp.float32, smallest / len(pieces), largest / len(pieces)))
        loudness = loudness * jnp.repeat(draws, shape[dim] // parts).reshape([-1 if axis == dim else 1 for axis in range(len(shape))])
    return loudness


def centred(rng, shape, scale, bound, shards=(), held_as=jnp.bfloat16):
    loudness = steps_of(rng, shape, shards, -0.22, 0.18) if shards else 1.0
    values = jax.random.normal(rng, shape, jnp.float32) * scale * loudness
    return jnp.minimum(jnp.maximum(values, -bound), bound).astype(held_as)


def gaussian_with(stream_key, dims, spread, reach, cuts, heavy, kind=jnp.bfloat16):
    drawn = spread * jax.random.normal(stream_key, dims, jnp.float32)
    if cuts:
        drawn = drawn * steps_of(stream_key, dims, cuts, -0.22, 0.18)
    return jnp.clip(spiked(drawn, jax.random.fold_in(stream_key, 3), *heavy), -reach, reach).astype(kind)


def setup_inputs(seed: int = 0) -> dict:
    key_of = jax.random.split(jax.random.key(seed), 25)
    tokens = gaussian_with(key_of[0], (NSEQ, L, D), 1.0, 6.0, ((0, 4), (1, 8)), (1, 2, 8, 2.0))
    per_layer = centred(key_of[1], (NSEQ, L, PL), 1.0, 6.0, ((0, 4), (1, 8)))
    positions = draw_positions(jax.random.fold_in(key_of[24], 71), 0)
    span_start = draw_span_start(jax.random.fold_in(key_of[24], 71), 0)
    cotangent = centred(key_of[4], (NSEQ, L, D), 1.0, 6.0, ((0, 4), (1, 8)))
    query_weight = centred(key_of[5], (D, H * HD), D ** -0.5, 0.125, ((0, 32),))
    key_weight = centred(key_of[6], (D, KVH * HD), D ** -0.5, 0.125, ((0, 32),))
    value_weight = centred(key_of[7], (D, KVH * HD), D ** -0.5, 0.125, ((0, 32),))
    output_weight = centred(key_of[8], (D, H * HD), (H * HD) ** -0.5, 0.125, ((0, 32),))
    laurel_left = centred(key_of[9], (D, R), D ** -0.5, 0.125, ((0, 32),))
    laurel_right = centred(key_of[10], (D, R), R ** -0.5, 0.75, ((0, 32),))
    gate_weight = centred(key_of[11], (D, FF), D ** -0.5, 0.125, ((0, 32),))
    up_weight = centred(key_of[12], (D, FF), D ** -0.5, 0.125, ((0, 32),))
    down_weight = centred(key_of[13], (D, FF), FF ** -0.5, 0.0625, ((0, 32),))
    side_gate = centred(key_of[14], (D, PL), D ** -0.5, 0.125, ((0, 32),))
    side_output = centred(key_of[15], (D, PL), PL ** -0.5, 0.375, ((0, 32),))
    norm_input = jnp.clip(1.0 + 0.15 * jax.random.normal(key_of[16], (D,), jnp.float32), 0.25, 1.75)
    norm_attn = jnp.clip(1.0 + 0.15 * jax.random.normal(key_of[17], (D,), jnp.float32), 0.25, 1.75)
    norm_laurel = jnp.clip(1.0 + 0.15 * jax.random.normal(key_of[18], (D,), jnp.float32), 0.25, 1.75)
    norm_before = jnp.clip(1.0 + 0.15 * jax.random.normal(key_of[19], (D,), jnp.float32), 0.25, 1.75)
    norm_after = jnp.clip(1.0 + 0.15 * jax.random.normal(key_of[20], (D,), jnp.float32), 0.25, 1.75)
    norm_layer = jnp.clip(1.0 + 0.15 * jax.random.normal(key_of[21], (D,), jnp.float32), 0.25, 1.75)
    norm_query = jnp.clip(jnp.exp(jax.random.uniform(key_of[22], (HD,), jnp.float32, math.log(0.2), math.log(0.5))), 0.2, 0.5)
    norm_key = jnp.clip(jnp.exp(jax.random.uniform(key_of[23], (HD,), jnp.float32, math.log(0.2), math.log(0.5))), 0.2, 0.5)
    return {"tokens": tokens, "per_layer": per_layer, "positions": positions, "span_start": span_start, "cotangent": cotangent, "query_weight": query_weight, "key_weight": key_weight, "value_weight": value_weight, "output_weight": output_weight, "laurel_left": laurel_left, "laurel_right": laurel_right, "gate_weight": gate_weight, "up_weight": up_weight, "down_weight": down_weight, "side_gate": side_gate, "side_output": side_output, "norm_input": norm_input, "norm_attn": norm_attn, "norm_laurel": norm_laurel, "norm_before": norm_before, "norm_after": norm_after, "norm_layer": norm_layer, "norm_query": norm_query, "norm_key": norm_key}


@jax.custom_vjp
def low(v):
    return lax.optimization_barrier(v.astype(jnp.bfloat16)).astype(jnp.float32)

@jax.custom_vjp
def low_back(v):
    return v

def low_keep(v):
    return (low(v), None)

def low_pass(kept, grad):
    return (grad,)

def back_keep(v):
    return (v, None)

def back_low(kept, grad):
    return (low(grad),)
low.defvjp(low_keep, low_pass)
low_back.defvjp(back_keep, back_low)
EPS = 1e-06
HALF_ROOT = 1.0 / math.sqrt(2.0)
HIGH = lax.Precision.HIGHEST

def rms(values, gain):
    return values * lax.rsqrt(lax.optimization_barrier(jnp.mean(values * values, axis=-1, keepdims=True)) + EPS) * gain

def gelu_tanh(values):
    return jax.nn.gelu(values, approximate=True)

def product(left, right):
    return jnp.dot(left, right, precision=HIGH, preferred_element_type=jnp.float32)

def product_nt(left, right):
    return lax.dot_general(left, right, (((1,), (1,)), ((), ())), precision=HIGH, preferred_element_type=jnp.float32)

def rotate(values, places):
    size = values.shape[-1]
    half = size // 2
    freq = 10000.0 ** (-(2.0 * jnp.arange(half, dtype=jnp.float32)) / size)
    angle = places.astype(jnp.float32)[..., None] * freq
    cosine = jnp.cos(angle)[..., None, :]
    sine = jnp.sin(angle)[..., None, :]
    first = values[..., :half]
    second = values[..., half:]
    return jnp.concatenate([first * cosine - second * sine, second * cosine + first * sine], axis=-1)

def attend(query_low, key_low, value_low, starts):
    length = query_low.shape[0]
    rows = min(512, length)
    kv_heads = key_low.shape[1]
    group = query_low.shape[1] // kv_heads
    head_size = query_low.shape[2]
    places = jnp.arange(length, dtype=jnp.int32)
    in_key = (places[:, None] >= starts[None, :]) & (places[:, None] < starts[None, :] + SPAN)

    def one_block(index):
        first = (index * rows).astype(jnp.int32)
        query_block = lax.dynamic_slice_in_dim(query_low, first, rows, 0).reshape(rows, kv_heads, group, head_size)
        query_places = first + jnp.arange(rows, dtype=jnp.int32)
        in_query = lax.dynamic_slice_in_dim(in_key, first, rows, 0)
        near = (places[None, :] <= query_places[:, None]) & (query_places[:, None] - places[None, :] < WINDOW)
        same = jnp.any(in_query[:, None, :] & in_key[None, :, :], axis=-1)
        allowed = near | same
        scores = low_back(jnp.einsum('tkgd,skd->kgts', query_block, key_low, precision=HIGH))
        masked = jnp.where(allowed[None, None], scores, -1e+30)
        top = lax.optimization_barrier(jnp.max(masked, axis=-1, keepdims=True))
        expo = jnp.exp(masked - top)
        probs = expo / lax.optimization_barrier(jnp.sum(expo, axis=-1, keepdims=True))
        probs_low = low(probs)
        attended = jnp.einsum('kgts,skd->tkgd', probs_low, value_low, precision=HIGH)
        return attended.reshape(rows, kv_heads * group * head_size)
    blocks = lax.map(jax.checkpoint(one_block), jnp.arange(length // rows, dtype=jnp.int32))
    return blocks.reshape(length, kv_heads * group * head_size)

def layer(inputs, side_in, params, places, starts):
    query_weight, key_weight, value_weight, output_weight, laurel_left, laurel_right, gate_weight, up_weight, down_weight, side_gate, side_output, norm_input, norm_attn, norm_laurel, norm_before, norm_after, norm_layer, norm_query, norm_key = params
    length = inputs.shape[0]
    head_size = norm_query.shape[0]
    normed = rms(inputs, norm_input)
    normed_low = low(normed)
    queries = low_back(product(normed_low, query_weight)).reshape(length, -1, head_size)
    keys = low_back(product(normed_low, key_weight)).reshape(length, -1, head_size)
    values = low_back(product(normed_low, value_weight)).reshape(length, -1, head_size)
    query_low = low(rotate(rms(queries, norm_query), places))
    key_low = low(rotate(rms(keys, norm_key), places))
    value_low = low(rms(values, 1.0))
    attended = attend(query_low, key_low, value_low, starts)
    attended_low = low_back(low(attended))
    attn_proj = low_back(product_nt(attended_low, output_weight))
    latent_low = low_back(low(product(normed_low, laurel_left)))
    laurel = low_back(product_nt(latent_low, laurel_right))
    resid_one = (inputs + rms(attn_proj, norm_attn) + normed + rms(laurel, norm_laurel)) * HALF_ROOT
    feed_low = low(rms(resid_one, norm_before))
    gate = low_back(product(feed_low, gate_weight))
    up_val = low_back(product(feed_low, up_weight))
    hidden_low = low(gelu_tanh(gate) * up_val)
    feed_out = low_back(product_nt(hidden_low, down_weight))
    resid_two = resid_one + rms(feed_out, norm_after)
    side_pre = low_back(product(low(resid_two), side_gate))
    side_low = low(gelu_tanh(side_pre) * side_in)
    side_out = low_back(product_nt(side_low, side_output))
    return resid_two + rms(side_out, norm_layer)

def reference(tokens, per_layer, positions, span_start, cotangent, query_weight, key_weight, value_weight, output_weight, laurel_left, laurel_right, gate_weight, up_weight, down_weight, side_gate, side_output, norm_input, norm_attn, norm_laurel, norm_before, norm_after, norm_layer, norm_query, norm_key):
    weights = tuple((matrix.astype(jnp.float32) for matrix in (query_weight, key_weight, value_weight, output_weight, laurel_left, laurel_right, gate_weight, up_weight, down_weight, side_gate, side_output)))
    gains = (norm_input, norm_attn, norm_laurel, norm_before, norm_after, norm_layer, norm_query, norm_key)
    params = weights + gains
    zeros = tuple((jnp.zeros_like(entry) for entry in params))

    def one_sequence(carry, item):
        seq_tokens, seq_side, seq_places, seq_starts, seq_upstream = item

        def forward(inputs, side_in, weights_in):
            return layer(inputs, side_in, weights_in, seq_places, seq_starts)
        result, pullback = jax.vjp(forward, seq_tokens.astype(jnp.float32), seq_side.astype(jnp.float32), params)
        grad_in, grad_side, grad_params = pullback(seq_upstream.astype(jnp.float32))
        carry = tuple((total + piece for total, piece in zip(carry, grad_params)))
        return (carry, (result.astype(jnp.bfloat16), grad_in, grad_side))
    totals, (outputs, grad_tokens, grad_side) = lax.scan(one_sequence, zeros, (tokens, per_layer, positions, span_start, cotangent))
    return (outputs, grad_tokens, grad_side, totals[0], totals[1], totals[2], totals[3], totals[4], totals[5], totals[6], totals[7], totals[8], totals[9], totals[10], totals[11], totals[12], totals[13], totals[14], totals[15], totals[16], totals[17], totals[18])
```

```python
import math

import jax
import jax.numpy as jnp
from jax import lax
from jax.sharding import Mesh
from jax.sharding import PartitionSpec as P

WINDOW = 512
SPAN = 256
EPS = 1e-06
HALF_ROOT = 1.0 / math.sqrt(2.0)
F32 = jnp.float32
BF16 = jnp.bfloat16


def rms(values, gain):
    return values * lax.rsqrt(jnp.mean(values * values, axis=-1, keepdims=True) + EPS) * gain


def gelu_tanh(values):
    return jax.nn.gelu(values, approximate=True)


def product(left, right):
    return jnp.dot(left, right, preferred_element_type=F32)


def product_nt(left, right):
    return lax.dot_general(left, right, (((1,), (1,)), ((), ())), preferred_element_type=F32)


def product_tn(left, right):
    return lax.dot_general(left, right, (((0,), (0,)), ((), ())), preferred_element_type=F32)


def rotate(values, places):
    size = values.shape[-1]
    half = size // 2
    freq = 10000.0 ** (-(2.0 * jnp.arange(half, dtype=F32)) / size)
    angle = places.astype(F32)[..., None] * freq
    cosine = jnp.cos(angle)[..., None, :]
    sine = jnp.sin(angle)[..., None, :]
    first = values[..., :half]
    second = values[..., half:]
    return jnp.concatenate(
        [first * cosine - second * sine, second * cosine + first * sine], axis=-1
    )


def middle(inputs, normed, attn_proj, laurel, gain_attn, gain_laurel, gain_before):
    resid = (inputs + rms(attn_proj, gain_attn) + normed + rms(laurel, gain_laurel)) * HALF_ROOT
    return (resid, rms(resid, gain_before))


def gate_act(gate_val, up_val):
    return gelu_tanh(gate_val) * up_val


def after_feed(resid_one, feed_out, gain_after):
    return resid_one + rms(feed_out, gain_after)


def side_act(side_pre, side_in):
    return gelu_tanh(side_pre) * side_in


def finish(resid_two, side_out, gain_layer):
    return resid_two + rms(side_out, gain_layer)


def swap(value, axis):
    return lax.ppermute(value, axis, [(0, 1), (1, 0)])


def split_columns(whole, widths):
    pieces = []
    offset = 0
    for width_one in widths:
        pieces.append(whole[..., offset : offset + width_one])
        offset = offset + width_one
    return pieces


class Plan:
    def __init__(self, seq_bits, dp_bits):
        self.seq = tuple("s%d" % i for i in range(seq_bits))
        self.dp = tuple("d%d" % i for i in range(dp_bits))
        self.every = self.seq + self.dp
        self.l, self.x = self.seq[-2:]
        self.c = self.dp[-1]
        self.team = (self.l, self.x, self.c)
        self.far_seq = self.seq[:-2]
        self.far_dp = self.dp[:-1]
        self.far = self.far_seq + self.far_dp

    def flips(self, value, first_dims):
        for axis, dim in zip(self.far, first_dims):
            value = jnp.where(lax.axis_index(axis) == 1, jnp.flip(value, dim), value)
        return value

    def to_relative(self, value):
        rows, width = value.shape
        n_seq, n_dp = len(self.far_seq), len(self.far_dp)
        parts = value.reshape((rows,) + (2,) * n_seq + (4,) + (2,) * n_dp + (-1,))
        dims = list(range(1, 1 + n_seq)) + list(range(2 + n_seq, 2 + n_seq + n_dp))
        parts = self.flips(parts, dims)
        order = [0] + dims + [1 + n_seq, 2 + n_seq + n_dp]
        return parts.transpose(order).reshape(rows, width)

    def from_relative(self, value):
        rows, width = value.shape
        n_seq, n_dp = len(self.far_seq), len(self.far_dp)
        parts = value.reshape((rows,) + (2,) * (n_seq + n_dp) + (4, -1))
        parts = self.flips(parts, list(range(1, 1 + n_seq + n_dp)))
        order = [0] + list(range(1, 1 + n_seq)) + [1 + n_seq + n_dp]
        order += list(range(1 + n_seq, 1 + n_seq + n_dp)) + [2 + n_seq + n_dp]
        return parts.transpose(order).reshape(rows, width)

    def far_gather(self, block):
        pieces = {(): block}
        for axis in self.far:
            pieces.update({key + (axis,): swap(piece, axis) for key, piece in list(pieces.items())})
        return [pieces[key] for key in self.far_keys()]

    def far_keys(self):
        keys = [()]
        for axis in self.far:
            keys = [key + extra for key in keys for extra in ((), (axis,))]
        return keys

    def far_scatter(self, pieces):
        held = dict(zip(self.far_keys(), pieces))
        for axis in reversed(self.far):
            for key in [key for key in held if axis in key]:
                into = tuple(one for one in key if one != axis)
                moved = swap(held.pop(key), axis).astype(F32)
                held[into] = (held[into].astype(F32) + moved).astype(BF16)
        return held[()]

    def team_gather(self, own):
        by_x, by_l = swap(own, self.x), swap(own, self.l)
        half = own.shape[0] // 2
        both = jnp.concatenate([swap(by_x[:half], self.l), swap(by_l[half:], self.x)], axis=0)
        return [jnp.concatenate([p, swap(p, self.c)], axis=0) for p in (own, by_x, by_l, both)]

    def team_scatter(self, chunks):
        sums = []
        for chunk in chunks:
            rows = chunk.shape[0] // 2
            other = swap(chunk[rows:].astype(BF16), self.c)
            sums.append(chunk[:rows].astype(F32) + other.astype(F32))
        own, by_x, by_l, both = sums
        half = own.shape[0] // 2
        both = both.astype(BF16)
        first = by_l[:half] + swap(both[:half], self.x).astype(F32)
        second = by_x[half:] + swap(both[half:], self.l).astype(F32)
        by_l = jnp.concatenate([first, by_l[half:]], axis=0).astype(BF16)
        by_x = jnp.concatenate([by_x[:half], second], axis=0).astype(BF16)
        return own + swap(by_l, self.l).astype(F32) + swap(by_x, self.x).astype(F32)


def passed_along(value, axes, count, steps):
    initial, last = (max(0, -steps), min(count, count - steps))
    return lax.ppermute(value, axes, [(source, source + steps) for source in range(initial, last)])


def body(
    plan,
    tokens,
    per_layer,
    positions,
    span_start,
    cotangent,
    query_weight,
    key_weight,
    value_weight,
    output_weight,
    laurel_left,
    laurel_right,
    gate_weight,
    up_weight,
    down_weight,
    side_gate,
    side_output,
    norm_input,
    norm_attn,
    norm_laurel,
    norm_before,
    norm_after,
    norm_layer,
    norm_query,
    norm_key,
):
    batch, block, width = tokens.shape
    rows = batch * block
    head_size = norm_query.shape[0]
    heads = query_weight.shape[1] // head_size
    kv_heads = key_weight.shape[1] // head_size
    group = heads // kv_heads
    seq_count = 2 ** len(plan.seq)
    local_rows = gate_weight.shape[0]
    team_size = 2 ** len(plan.team)
    hidden_own = gate_weight.shape[1] // team_size

    one_widths = [query_weight.shape[1], key_weight.shape[1], value_weight.shape[1], laurel_left.shape[1]]
    two_widths = [output_weight.shape[1], laurel_right.shape[1], side_gate.shape[1], side_output.shape[1]]
    one_local = jnp.concatenate([query_weight, key_weight, value_weight, laurel_left], axis=1)
    two_local = jnp.concatenate([output_weight, laurel_right, side_gate, side_output], axis=1)
    one_full = lax.all_gather(one_local, plan.every, axis=0, tiled=True)
    two_full = lax.all_gather(two_local, plan.every, axis=0, tiled=True)
    output_full, right_full, side_gate_full, side_output_full = split_columns(two_full, two_widths)

    feed_local = jnp.stack([gate_weight, up_weight, down_weight], axis=1)
    feed_local = feed_local.reshape(local_rows, 3, team_size, hidden_own).transpose(2, 0, 1, 3)
    feed_local = feed_local.reshape(team_size * local_rows, 3 * hidden_own)
    feed_team = lax.all_to_all(feed_local, plan.team, split_axis=0, concat_axis=0, tiled=True)
    gate_up_full = jnp.concatenate(
        [
            jnp.concatenate(plan.far_gather(feed_team[:, :hidden_own]), axis=0),
            jnp.concatenate(plan.far_gather(feed_team[:, hidden_own : 2 * hidden_own]), axis=0),
        ],
        axis=1,
    )
    down_full = jnp.concatenate(plan.far_gather(feed_team[:, 2 * hidden_own :]), axis=0)

    inputs = tokens.astype(F32).reshape(rows, width)
    side_in = per_layer.astype(F32).reshape(rows, -1)
    upstream = cotangent.astype(F32).reshape(rows, width)
    normed, pre_pull = jax.vjp(rms, inputs, norm_input)
    normed_low = normed.astype(BF16)
    one_out = product(normed_low, one_full)
    queries, keys, values, latent = split_columns(one_out, one_widths)
    queries = queries.reshape(batch, block, heads, head_size)
    keys = keys.reshape(batch, block, kv_heads, head_size)
    values = values.reshape(batch, block, kv_heads, head_size)
    latent_low = latent.astype(BF16)

    def head_prep(query_in, key_in, value_in, gain_query, gain_key):
        return (
            rotate(rms(query_in, gain_query), positions),
            rotate(rms(key_in, gain_key), positions),
            rms(value_in, 1.0),
        )

    (rot_query, rot_key, rot_value), prep_pull = jax.vjp(
        head_prep, queries, keys, values, norm_query, norm_key
    )
    query_low = rot_query.astype(BF16)
    pair_low = jnp.stack([rot_key.astype(BF16), rot_value.astype(BF16)])
    left_count = WINDOW // block
    right_count = (SPAN + block - 2) // block
    offsets = list(range(left_count, 0, -1)) + [0] + list(range(-1, -right_count - 1, -1))
    gathered = []
    for offset in offsets:
        if offset == 0:
            gathered.append(pair_low)
        else:
            gathered.append(passed_along(pair_low, plan.seq, seq_count, offset))
    pairs_all = jnp.concatenate(gathered, axis=2)
    keys_all = pairs_all[0]
    values_all = pairs_all[1]
    key_count = keys_all.shape[1]
    seq_index = lax.axis_index(plan.seq)
    total_length = block * seq_count
    query_places = seq_index * block + jnp.arange(block, dtype=jnp.int32)
    key_places = (seq_index - left_count) * block + jnp.arange(key_count, dtype=jnp.int32)
    in_query = (query_places[None, :, None] >= span_start[:, None, :]) & (
        query_places[None, :, None] < span_start[:, None, :] + SPAN
    )
    in_key = (key_places[None, :, None] >= span_start[:, None, :]) & (
        key_places[None, :, None] < span_start[:, None, :] + SPAN
    )
    same = jnp.any(in_query[:, :, None, :] & in_key[:, None, :, :], axis=-1)
    near = (key_places[None, :] <= query_places[:, None]) & (
        query_places[:, None] - key_places[None, :] < WINDOW
    )
    valid = (key_places >= 0) & (key_places < total_length)
    allowed = (valid[None, None, :] & (near[None] | same))[:, None, None]
    query_group = query_low.reshape(batch, block, kv_heads, group, head_size)
    scores = jnp.einsum("btkgd,bskd->bkgts", query_group, keys_all, preferred_element_type=F32)
    masked = jnp.where(allowed, scores, -1e30)
    top = jnp.max(masked, axis=-1, keepdims=True)
    expo = jnp.exp(masked - top)
    total = jnp.sum(expo, axis=-1, keepdims=True)
    probs = expo / total
    probs_low = probs.astype(BF16)
    attended = jnp.einsum("bkgts,bskd->btkgd", probs_low, values_all, preferred_element_type=F32)
    attended_low = attended.reshape(rows, heads * head_size).astype(BF16)
    attn_proj = product_nt(attended_low, output_full)
    laurel = product_nt(latent_low, right_full)
    (resid_one, feed_in), mid_pull = jax.vjp(
        middle, inputs, normed, attn_proj, laurel, norm_attn, norm_laurel, norm_before
    )

    feed_chunks = plan.team_gather(plan.to_relative(feed_in.astype(BF16)))
    pulls = []
    hidden_chunks = []
    feed_parts = []
    for chunk in feed_chunks:
        gate_up = product(chunk, gate_up_full)
        hidden, pull = jax.vjp(gate_act, gate_up[:, :hidden_own], gate_up[:, hidden_own:])
        hidden_low = hidden.astype(BF16)
        pulls.append(pull)
        hidden_chunks.append(hidden_low)
        feed_parts.append(product_nt(hidden_low, down_full).astype(BF16))
    feed_out = plan.from_relative(plan.team_scatter(feed_parts))

    resid_two, after_pull = jax.vjp(after_feed, resid_one, feed_out, norm_after)
    resid_low = resid_two.astype(BF16)
    side_pre = product(resid_low, side_gate_full)
    side_val, side_pull = jax.vjp(side_act, side_pre, side_in)
    side_low = side_val.astype(BF16)
    side_out = product_nt(side_low, side_output_full)
    result, final_pull = jax.vjp(finish, resid_two, side_out, norm_layer)
    output = result.astype(BF16).reshape(batch, block, width)

    d_resid_two, d_side_out, grad_norm_layer = final_pull(upstream)
    d_side_out_low = d_side_out.astype(BF16)
    d_side = product(d_side_out_low, side_output_full)
    d_side_pre, d_side_in = side_pull(d_side)
    d_side_pre_low = d_side_pre.astype(BF16)
    d_resid_two = d_resid_two + product_nt(d_side_pre_low, side_gate_full)
    d_resid_one, d_feed_out, grad_norm_after = after_pull(d_resid_two)

    d_out_chunks = plan.team_gather(plan.to_relative(d_feed_out.astype(BF16)))
    d_gate_up_chunks = []
    d_feed_parts = []
    for chunk, pull in zip(d_out_chunks, pulls):
        d_gate, d_up = pull(product(chunk, down_full))
        d_gate_up = jnp.concatenate([d_gate.astype(BF16), d_up.astype(BF16)], axis=1)
        d_gate_up_chunks.append(d_gate_up)
        d_feed_parts.append(product_nt(d_gate_up, gate_up_full).astype(BF16))
    d_feed_in = plan.from_relative(plan.team_scatter(d_feed_parts))

    far_count = 2 ** len(plan.far)
    piece_width = width // far_count
    feed_all = jnp.concatenate(feed_chunks, axis=0)
    hidden_all = jnp.concatenate(hidden_chunks, axis=0)
    d_out_all = jnp.concatenate(d_out_chunks, axis=0)
    d_gate_up_all = jnp.concatenate(d_gate_up_chunks, axis=0)
    down_pieces = []
    gate_up_pieces = []
    for index in range(far_count):
        part = slice(index * piece_width, (index + 1) * piece_width)
        down_pieces.append(product_tn(d_out_all[:, part], hidden_all).astype(BF16))
        gate_up_pieces.append(product_tn(feed_all[:, part], d_gate_up_all).astype(BF16))
    grad_down_team = plan.far_scatter(down_pieces)
    grad_gate_up_team = plan.far_scatter(gate_up_pieces)
    feed_grads = lax.all_to_all(
        jnp.concatenate([grad_gate_up_team, grad_down_team], axis=1),
        plan.team,
        split_axis=0,
        concat_axis=0,
        tiled=True,
    )
    feed_grads = feed_grads.reshape(team_size, local_rows, 3, hidden_own).transpose(2, 1, 0, 3)
    feed_grads = feed_grads.reshape(3, local_rows, team_size * hidden_own).astype(F32)

    (
        d_inputs,
        d_normed,
        d_attn_proj,
        d_laurel,
        grad_norm_attn,
        grad_norm_laurel,
        grad_norm_before,
    ) = mid_pull((d_resid_one, d_feed_in))
    d_attn_low = d_attn_proj.astype(BF16)
    d_laurel_low = d_laurel.astype(BF16)
    d_attended_low = product(d_attn_low, output_full).astype(BF16)
    d_latent_low = product(d_laurel_low, right_full).astype(BF16)
    two_terms = jnp.concatenate(
        [
            product_tn(d_attn_low, attended_low).astype(BF16),
            product_tn(d_laurel_low, latent_low).astype(BF16),
            product_tn(resid_low, d_side_pre_low).astype(BF16),
            product_tn(d_side_out_low, side_low).astype(BF16),
        ],
        axis=1,
    )
    two_sum = lax.psum_scatter(two_terms, plan.every, scatter_dimension=0, tiled=True).astype(F32)

    d_att = d_attended_low.reshape(batch, block, kv_heads, group, head_size)
    d_values_all = jnp.einsum("bkgts,btkgd->bskd", probs_low, d_att, preferred_element_type=F32)
    d_probs = jnp.einsum("btkgd,bskd->bkgts", d_att, values_all, preferred_element_type=F32)
    d_scores = probs * (d_probs - jnp.sum(probs * d_probs, axis=-1, keepdims=True))
    d_scores_low = d_scores.astype(BF16)
    d_query_rot = jnp.einsum("bkgts,bskd->btkgd", d_scores_low, keys_all, preferred_element_type=F32)
    d_keys_all = jnp.einsum(
        "bkgts,btkgd->bskd", d_scores_low, query_group, preferred_element_type=F32
    )
    d_pairs = jnp.stack([d_keys_all, d_values_all])
    d_pair_total = d_pairs[:, :, left_count * block : (left_count + 1) * block]
    for position, offset in enumerate(offsets):
        if offset != 0:
            piece = d_pairs[:, :, position * block : (position + 1) * block].astype(BF16)
            d_pair_total = d_pair_total + passed_along(piece, plan.seq, seq_count, -offset).astype(F32)
    d_queries, d_keys, d_values, grad_norm_query, grad_norm_key = prep_pull(
        (d_query_rot.reshape(batch, block, heads, head_size), d_pair_total[0], d_pair_total[1])
    )
    d_one_low = jnp.concatenate(
        [
            d_queries.reshape(rows, -1).astype(BF16),
            d_keys.reshape(rows, -1).astype(BF16),
            d_values.reshape(rows, -1).astype(BF16),
            d_latent_low,
        ],
        axis=1,
    )
    one_terms = product_tn(normed_low, d_one_low).astype(BF16)
    one_sum = lax.psum_scatter(one_terms, plan.every, scatter_dimension=0, tiled=True).astype(F32)
    d_normed = d_normed + product_nt(d_one_low, one_full)
    d_inputs_norm, grad_norm_input = pre_pull(d_normed)
    grad_tokens = (d_inputs + d_inputs_norm).reshape(batch, block, width)
    grad_side = d_side_in.reshape(batch, block, -1)
    gains = lax.psum(
        jnp.concatenate(
            [
                grad_norm_input,
                grad_norm_attn,
                grad_norm_laurel,
                grad_norm_before,
                grad_norm_after,
                grad_norm_layer,
                grad_norm_query,
                grad_norm_key,
            ]
        ),
        plan.every,
    )
    gain_parts = split_columns(gains, [width] * 6 + [head_size] * 2)
    one_parts = split_columns(one_sum, one_widths)
    two_parts = split_columns(two_sum, two_widths)
    return (
        output,
        grad_tokens,
        grad_side,
        one_parts[0],
        one_parts[1],
        one_parts[2],
        two_parts[0],
        one_parts[3],
        two_parts[1],
        feed_grads[0],
        feed_grads[1],
        feed_grads[2],
        two_parts[2],
        two_parts[3],
    ) + tuple(gain_parts)


def solution(mesh):
    seq_bits = int(math.log2(mesh.shape["seq"]))
    dp_bits = int(math.log2(mesh.shape["dp"]))
    plan = Plan(seq_bits, dp_bits)
    binary = Mesh(mesh.devices.reshape((2,) * (seq_bits + dp_bits)), plan.every)
    token_spec = P(plan.dp, plan.seq, None)
    weight_spec = P(plan.every, None)

    def step(*arrays):
        return body(plan, *arrays)

    return jax.shard_map(
        step,
        mesh=binary,
        in_specs=(token_spec, token_spec, P(plan.dp, plan.seq), P(plan.dp, None), token_spec)
        + (weight_spec,) * 11
        + (P(),) * 8,
        out_specs=(token_spec,) * 3 + (weight_spec,) * 11 + (P(),) * 8,
        check_vma=False,
    )
```

```python
import math

import jax
import jax.numpy as jnp
from jax import lax
from jax.sharding import Mesh
from jax.sharding import PartitionSpec as P

WINDOW = 512
SPAN = 256
EPS = 1e-06
HALF_ROOT = 1.0 / math.sqrt(2.0)
F32 = jnp.float32
BF16 = jnp.bfloat16


def rms(values, gain):
    return values * lax.rsqrt(jnp.mean(values * values, axis=-1, keepdims=True) + EPS) * gain


def gelu_tanh(values):
    return jax.nn.gelu(values, approximate=True)


def product(left, right):
    return jnp.dot(left, right, preferred_element_type=F32)


def product_nt(left, right):
    return lax.dot_general(left, right, (((1,), (1,)), ((), ())), preferred_element_type=F32)


def product_tn(left, right):
    return lax.dot_general(left, right, (((0,), (0,)), ((), ())), preferred_element_type=F32)


def rotate(values, places):
    size = values.shape[-1]
    half = size // 2
    freq = 10000.0 ** (-(2.0 * jnp.arange(half, dtype=F32)) / size)
    angle = places.astype(F32)[..., None] * freq
    cosine = jnp.cos(angle)[..., None, :]
    sine = jnp.sin(angle)[..., None, :]
    first = values[..., :half]
    second = values[..., half:]
    return jnp.concatenate(
        [first * cosine - second * sine, second * cosine + first * sine], axis=-1
    )


def middle(inputs, normed, attn_proj, laurel, gain_attn, gain_laurel, gain_before):
    resid = (inputs + rms(attn_proj, gain_attn) + normed + rms(laurel, gain_laurel)) * HALF_ROOT
    return (resid, rms(resid, gain_before))


def gate_act(gate_val, up_val):
    return gelu_tanh(gate_val) * up_val


def after_feed(resid_one, feed_out, gain_after):
    return resid_one + rms(feed_out, gain_after)


def side_act(side_pre, side_in):
    return gelu_tanh(side_pre) * side_in


def finish(resid_two, side_out, gain_layer):
    return resid_two + rms(side_out, gain_layer)


def swap(value, axis):
    return lax.ppermute(value, axis, [(0, 1), (1, 0)])


def split_columns(whole, widths):
    pieces = []
    offset = 0
    for width_one in widths:
        pieces.append(whole[..., offset : offset + width_one])
        offset = offset + width_one
    return pieces


class Plan:
    def __init__(self, seq_bits, dp_bits):
        self.seq = tuple("s%d" % i for i in range(seq_bits))
        self.dp = tuple("d%d" % i for i in range(dp_bits))
        self.every = self.seq + self.dp
        self.l, self.x = self.seq[-2:]
        self.c = self.dp[-1]
        self.team = (self.l, self.x, self.c)
        self.far_seq = self.seq[:-2]
        self.far_dp = self.dp[:-1]
        self.far = self.far_seq + self.far_dp

    def flips(self, value, first_dims):
        for axis, dim in zip(self.far, first_dims):
            value = jnp.where(lax.axis_index(axis) == 1, jnp.flip(value, dim), value)
        return value

    def to_relative(self, value):
        rows, width = value.shape
        n_seq, n_dp = len(self.far_seq), len(self.far_dp)
        parts = value.reshape((rows,) + (2,) * n_seq + (4,) + (2,) * n_dp + (-1,))
        dims = list(range(1, 1 + n_seq)) + list(range(2 + n_seq, 2 + n_seq + n_dp))
        parts = self.flips(parts, dims)
        order = [0] + dims + [1 + n_seq, 2 + n_seq + n_dp]
        return parts.transpose(order).reshape(rows, width)

    def from_relative(self, value):
        rows, width = value.shape
        n_seq, n_dp = len(self.far_seq), len(self.far_dp)
        parts = value.reshape((rows,) + (2,) * (n_seq + n_dp) + (4, -1))
        parts = self.flips(parts, list(range(1, 1 + n_seq + n_dp)))
        order = [0] + list(range(1, 1 + n_seq)) + [1 + n_seq + n_dp]
        order += list(range(1 + n_seq, 1 + n_seq + n_dp)) + [2 + n_seq + n_dp]
        return parts.transpose(order).reshape(rows, width)

    def source_in_natural(self, width):
        return self.to_relative(jnp.arange(width, dtype=jnp.int32)[None])[0]

    def spread_order(self, width):
        n_seq, n_dp = len(self.far_seq), len(self.far_dp)
        own = jnp.arange(width, dtype=jnp.int32).reshape((2,) * (n_seq + n_dp + 3) + (-1,))
        for dim, axis in enumerate(self.team):
            at = n_seq + n_dp + dim
            own = jnp.where(lax.axis_index(axis) == 1, jnp.flip(own, at), own)
        far_seq = list(range(n_seq))
        far_dp = list(range(n_seq, n_seq + n_dp))
        at_l, at_x, at_c = (n_seq + n_dp + dim for dim in range(3))
        return own.transpose([at_c] + far_dp + [at_x, at_l] + far_seq + [n_seq + n_dp + 3]).reshape(-1)

    def gather(self, block, x_first):
        canon = self.far_seq + self.far_dp + self.team
        middle_axes = (self.x,) + self.far_dp if x_first else self.far_dp + (self.x,)
        held = []
        for axis in self.far_seq + (self.l,) + middle_axes + (self.c,):
            other = swap(block, axis)
            place = sum(canon.index(one) < canon.index(axis) for one in held)
            held.append(axis)
            if axis in self.team:
                second = lax.axis_index(axis) == 1
                block, other = jnp.where(second, other, block), jnp.where(second, block, other)
            block = jnp.stack([block, other], axis=place)
        return block.reshape((-1, block.shape[-1]))

    def spread_sum(self, pairs, y_first):
        half = pairs[0][0].shape[1] // 2
        away = jnp.concatenate([product_tn(one[:, half:], two).astype(BF16) for one, two in pairs], axis=1)
        kept = jnp.concatenate([product_tn(one[:, :half], two).astype(BF16) for one, two in pairs], axis=1)
        total = (kept.astype(F32) + swap(away, self.c).astype(F32)).astype(BF16)
        names = list(self.far_dp) + [self.x, self.l] + list(self.far_seq)
        total = total.reshape((2,) * len(names) + (-1, total.shape[1]))
        order = list(self.far_dp) + [self.x] if y_first else [self.x] + list(self.far_dp)
        for axis in order + [self.l] + list(reversed(self.far_seq)):
            dim = names.index(axis)
            names.remove(axis)
            away = swap(lax.index_in_dim(total, 1, dim, False), axis).astype(F32)
            total = lax.index_in_dim(total, 0, dim, False).astype(F32) + away
            if names:
                total = total.astype(BF16)
        return total

    def total(self, value):
        for axis in reversed(self.every):
            value = value + swap(value, axis)
        return value

    def far_gather(self, block):
        pieces = {(): block}
        for axis in self.far:
            pieces.update({key + (axis,): swap(piece, axis) for key, piece in list(pieces.items())})
        return [pieces[key] for key in self.far_keys()]

    def far_keys(self):
        keys = [()]
        for axis in self.far:
            keys = [key + extra for key in keys for extra in ((), (axis,))]
        return keys

    def far_scatter(self, pieces):
        held = dict(zip(self.far_keys(), pieces))
        for axis in reversed(self.far):
            for key in [key for key in held if axis in key]:
                into = tuple(one for one in key if one != axis)
                moved = swap(held.pop(key), axis).astype(F32)
                held[into] = (held[into].astype(F32) + moved).astype(BF16)
        return held[()]

    def team_gather(self, own):
        by_x, by_l = swap(own, self.x), swap(own, self.l)
        half = own.shape[0] // 2
        both = jnp.concatenate([swap(by_x[:half], self.l), swap(by_l[half:], self.x)], axis=0)
        return [jnp.concatenate([p, swap(p, self.c)], axis=0) for p in (own, by_x, by_l, both)]

    def team_scatter(self, chunks):
        sums = []
        for chunk in chunks:
            rows = chunk.shape[0] // 2
            other = swap(chunk[rows:].astype(BF16), self.c)
            sums.append(chunk[:rows].astype(F32) + other.astype(F32))
        own, by_x, by_l, both = sums
        half = own.shape[0] // 2
        both = both.astype(BF16)
        first = by_l[:half] + swap(both[:half], self.x).astype(F32)
        second = by_x[half:] + swap(both[half:], self.l).astype(F32)
        by_l = jnp.concatenate([first, by_l[half:]], axis=0).astype(BF16)
        by_x = jnp.concatenate([by_x[:half], second], axis=0).astype(BF16)
        return own + swap(by_l, self.l).astype(F32) + swap(by_x, self.x).astype(F32)


def passed_along(value, axes, count, steps):
    initial, last = (max(0, -steps), min(count, count - steps))
    return lax.ppermute(value, axes, [(source, source + steps) for source in range(initial, last)])


def body(
    plan,
    tokens,
    per_layer,
    positions,
    span_start,
    cotangent,
    query_weight,
    key_weight,
    value_weight,
    output_weight,
    laurel_left,
    laurel_right,
    gate_weight,
    up_weight,
    down_weight,
    side_gate,
    side_output,
    norm_input,
    norm_attn,
    norm_laurel,
    norm_before,
    norm_after,
    norm_layer,
    norm_query,
    norm_key,
):
    batch, block, width = tokens.shape
    rows = batch * block
    head_size = norm_query.shape[0]
    heads = query_weight.shape[1] // head_size
    kv_heads = key_weight.shape[1] // head_size
    group = heads // kv_heads
    seq_count = 2 ** len(plan.seq)
    local_rows = gate_weight.shape[0]
    team_size = 2 ** len(plan.team)
    hidden_own = gate_weight.shape[1] // team_size

    kvl_widths = [key_weight.shape[1], value_weight.shape[1], laurel_left.shape[1]]
    rest_widths = [laurel_right.shape[1], side_gate.shape[1], side_output.shape[1]]
    query_full = plan.gather(query_weight, True)
    kvl_full = plan.gather(jnp.concatenate([key_weight, value_weight, laurel_left], axis=1), False)
    output_full = plan.gather(output_weight, False)
    rest_full = plan.gather(jnp.concatenate([laurel_right, side_gate, side_output], axis=1), True)
    right_full, side_gate_full, side_output_full = split_columns(rest_full, rest_widths)

    feed_local = jnp.concatenate(
        [
            one.reshape(local_rows, team_size, hidden_own).transpose(1, 0, 2)
            for one in (gate_weight, up_weight, down_weight)
        ],
        axis=1,
    )
    feed_team = lax.all_to_all(feed_local, plan.team, split_axis=0, concat_axis=0, tiled=True)
    feed_team = [
        feed_team[:, index * local_rows : (index + 1) * local_rows].reshape(-1, hidden_own)
        for index in range(3)
    ]
    feed_pieces = [plan.far_gather(one) for one in feed_team]

    places = jnp.arange(width, dtype=jnp.int32)
    natural = plan.source_in_natural(width)
    to_relative = (places[:, None] == natural[None, :]).astype(BF16)
    to_spread = (places[:, None] == plan.spread_order(width)[None, :]).astype(BF16)
    gains = jnp.stack([norm_input, norm_attn, norm_laurel, norm_before, norm_after, norm_layer])
    norm_input, norm_attn, norm_laurel, norm_before, norm_after, norm_layer = plan.to_relative(gains)
    inputs = product(tokens.reshape(rows, width), to_relative)
    upstream = product(cotangent.reshape(rows, width), to_relative)
    side_in = per_layer.astype(F32).reshape(rows, -1)
    normed, pre_pull = jax.vjp(rms, inputs, norm_input)
    normed_low = normed.astype(BF16)
    normed_spread = product(normed_low, to_spread).astype(BF16)
    queries = product(normed_low, query_full).reshape(batch, block, heads, head_size)
    keys, values, latent = split_columns(product(normed_low, kvl_full), kvl_widths)
    keys = keys.reshape(batch, block, kv_heads, head_size)
    values = values.reshape(batch, block, kv_heads, head_size)
    latent_low = latent.astype(BF16)

    def head_prep(query_in, key_in, value_in, gain_query, gain_key):
        return (
            rotate(rms(query_in, gain_query), positions),
            rotate(rms(key_in, gain_key), positions),
            rms(value_in, 1.0),
        )

    (rot_query, rot_key, rot_value), prep_pull = jax.vjp(
        head_prep, queries, keys, values, norm_query, norm_key
    )
    query_low = rot_query.astype(BF16)
    pair_low = jnp.stack([rot_key.astype(BF16), rot_value.astype(BF16)])
    left_count = WINDOW // block
    right_count = (SPAN + block - 2) // block
    offsets = list(range(left_count, 0, -1)) + [0] + list(range(-1, -right_count - 1, -1))
    gathered = []
    for offset in offsets:
        if offset == 0:
            gathered.append(pair_low)
        else:
            gathered.append(passed_along(pair_low, plan.seq, seq_count, offset))
    pairs_all, feed_pieces = lax.optimization_barrier(
        (jnp.concatenate(gathered, axis=2), feed_pieces)
    )
    gate_full, up_full, down_full = [jnp.concatenate(pieces, axis=0) for pieces in feed_pieces]
    keys_all = pairs_all[0]
    values_all = pairs_all[1]
    key_count = keys_all.shape[1]
    seq_index = lax.axis_index(plan.seq)
    total_length = block * seq_count
    query_places = seq_index * block + jnp.arange(block, dtype=jnp.int32)
    key_places = (seq_index - left_count) * block + jnp.arange(key_count, dtype=jnp.int32)
    in_query = (query_places[None, :, None] >= span_start[:, None, :]) & (
        query_places[None, :, None] < span_start[:, None, :] + SPAN
    )
    in_key = (key_places[None, :, None] >= span_start[:, None, :]) & (
        key_places[None, :, None] < span_start[:, None, :] + SPAN
    )
    same = jnp.any(in_query[:, :, None, :] & in_key[:, None, :, :], axis=-1)
    near = (key_places[None, :] <= query_places[:, None]) & (
        query_places[:, None] - key_places[None, :] < WINDOW
    )
    valid = (key_places >= 0) & (key_places < total_length)
    allowed = (valid[None, None, :] & (near[None] | same))[:, None, None]
    query_group = query_low.reshape(batch, block, kv_heads, group, head_size)
    scores = jnp.einsum("btkgd,bskd->bkgts", query_group, keys_all, preferred_element_type=F32)
    masked = jnp.where(allowed, scores, -1e30)
    top = jnp.max(masked, axis=-1, keepdims=True)
    expo = jnp.exp(masked - top)
    total = jnp.sum(expo, axis=-1, keepdims=True)
    probs = expo / total
    probs_low = probs.astype(BF16)
    attended = jnp.einsum("bkgts,bskd->btkgd", probs_low, values_all, preferred_element_type=F32)
    attended_low = attended.reshape(rows, heads * head_size).astype(BF16)
    attn_proj = product_nt(attended_low, output_full)
    laurel = product_nt(latent_low, right_full)
    (resid_one, feed_in), mid_pull = jax.vjp(
        middle, inputs, normed, attn_proj, laurel, norm_attn, norm_laurel, norm_before
    )

    feed_chunks = plan.team_gather(feed_in.astype(BF16))
    pulls = []
    hidden_chunks = []
    feed_parts = []
    for chunk in feed_chunks:
        hidden, pull = jax.vjp(gate_act, product(chunk, gate_full), product(chunk, up_full))
        hidden_low = hidden.astype(BF16)
        pulls.append(pull)
        hidden_chunks.append(hidden_low)
        feed_parts.append(product_nt(hidden_low, down_full).astype(BF16))
    feed_out = plan.team_scatter(feed_parts)

    resid_two, after_pull = jax.vjp(after_feed, resid_one, feed_out, norm_after)
    resid_low = resid_two.astype(BF16)
    side_pre = product(resid_low, side_gate_full)
    side_val, side_pull = jax.vjp(side_act, side_pre, side_in)
    side_low = side_val.astype(BF16)
    side_out = product_nt(side_low, side_output_full)
    result, final_pull = jax.vjp(finish, resid_two, side_out, norm_layer)
    output = product_nt(result.astype(BF16), to_relative).astype(BF16).reshape(batch, block, width)

    d_resid_two, d_side_out, grad_norm_layer = final_pull(upstream)
    d_side_out_low = d_side_out.astype(BF16)
    d_side = product(d_side_out_low, side_output_full)
    d_side_pre, d_side_in = side_pull(d_side)
    d_side_pre_low = d_side_pre.astype(BF16)
    d_resid_two = d_resid_two + product_nt(d_side_pre_low, side_gate_full)
    d_resid_one, d_feed_out, grad_norm_after = after_pull(d_resid_two)

    d_out_chunks = plan.team_gather(d_feed_out.astype(BF16))
    d_gate_chunks = []
    d_up_chunks = []
    d_feed_parts = []
    for chunk, pull in zip(d_out_chunks, pulls):
        d_gate, d_up = pull(product(chunk, down_full))
        d_gate_chunks.append(d_gate.astype(BF16))
        d_up_chunks.append(d_up.astype(BF16))
        part = product_nt(d_gate_chunks[-1], gate_full) + product_nt(d_up_chunks[-1], up_full)
        d_feed_parts.append(part.astype(BF16))
    d_feed_in = plan.team_scatter(d_feed_parts)

    far_count = 2 ** len(plan.far)
    piece_width = width // far_count
    feed_all = jnp.concatenate(feed_chunks, axis=0)
    d_out_all = jnp.concatenate(d_out_chunks, axis=0)
    pairs = (
        (d_out_all, jnp.concatenate(hidden_chunks, axis=0)),
        (feed_all, jnp.concatenate(d_gate_chunks, axis=0)),
        (feed_all, jnp.concatenate(d_up_chunks, axis=0)),
    )
    grad_pieces = [
        [
            product_tn(left[:, index * piece_width : (index + 1) * piece_width], right).astype(BF16)
            for index in range(far_count)
        ]
        for left, right in pairs
    ]
    d_feed_in, grad_pieces = lax.optimization_barrier((d_feed_in, grad_pieces))
    team_grads = [plan.far_scatter(pieces) for pieces in grad_pieces]
    feed_grads = lax.all_to_all(
        jnp.concatenate([one.reshape(team_size, local_rows, hidden_own) for one in team_grads], axis=1),
        plan.team,
        split_axis=0,
        concat_axis=0,
        tiled=True,
    )
    grad_down, grad_gate, grad_up = [
        jnp.concatenate(
            [feed_grads[at, index * local_rows : (index + 1) * local_rows] for at in range(team_size)],
            axis=1,
        ).astype(F32)
        for index in range(3)
    ]

    (
        d_inputs,
        d_normed,
        d_attn_proj,
        d_laurel,
        grad_norm_attn,
        grad_norm_laurel,
        grad_norm_before,
    ) = mid_pull((d_resid_one, d_feed_in))
    d_attn_low = d_attn_proj.astype(BF16)
    d_laurel_low = d_laurel.astype(BF16)
    d_attended_low = product(d_attn_low, output_full).astype(BF16)
    d_latent_low = product(d_laurel_low, right_full).astype(BF16)
    spread = product(
        jnp.concatenate([d_attn_low, d_laurel_low, resid_low, d_side_out_low], axis=0), to_spread
    ).astype(BF16)
    grad_output = plan.spread_sum([(spread[:rows], attended_low)], False)
    grad_right, grad_side_gate, grad_side_output = split_columns(
        plan.spread_sum(
            [
                (spread[rows : 2 * rows], latent_low),
                (spread[2 * rows : 3 * rows], d_side_pre_low),
                (spread[3 * rows :], side_low),
            ],
            True,
        ),
        rest_widths,
    )

    d_att = d_attended_low.reshape(batch, block, kv_heads, group, head_size)
    d_values_all = jnp.einsum("bkgts,btkgd->bskd", probs_low, d_att, preferred_element_type=F32)
    d_probs = jnp.einsum("btkgd,bskd->bkgts", d_att, values_all, preferred_element_type=F32)
    d_scores = probs * (d_probs - jnp.sum(probs * d_probs, axis=-1, keepdims=True))
    d_scores_low = d_scores.astype(BF16)
    d_query_rot = jnp.einsum("bkgts,bskd->btkgd", d_scores_low, keys_all, preferred_element_type=F32)
    d_keys_all = jnp.einsum(
        "bkgts,btkgd->bskd", d_scores_low, query_group, preferred_element_type=F32
    )
    d_pairs = jnp.stack([d_keys_all, d_values_all])
    d_pair_total = d_pairs[:, :, left_count * block : (left_count + 1) * block]
    for position, offset in enumerate(offsets):
        if offset != 0:
            piece = d_pairs[:, :, position * block : (position + 1) * block].astype(BF16)
            d_pair_total = d_pair_total + passed_along(piece, plan.seq, seq_count, -offset).astype(F32)
    d_queries, d_keys, d_values, grad_norm_query, grad_norm_key = prep_pull(
        (d_query_rot.reshape(batch, block, heads, head_size), d_pair_total[0], d_pair_total[1])
    )
    d_queries_low = d_queries.reshape(rows, -1).astype(BF16)
    d_kvl_low = jnp.concatenate(
        [
            d_keys.reshape(rows, -1).astype(BF16),
            d_values.reshape(rows, -1).astype(BF16),
            d_latent_low,
        ],
        axis=1,
    )
    grad_query = plan.spread_sum([(normed_spread, d_queries_low)], True)
    grad_key, grad_value, grad_left = split_columns(
        plan.spread_sum([(normed_spread, d_kvl_low)], False), kvl_widths
    )
    d_normed = d_normed + product_nt(d_queries_low, query_full) + product_nt(d_kvl_low, kvl_full)
    d_inputs_norm, grad_norm_input = pre_pull(d_normed)
    d_tokens = d_inputs + d_inputs_norm
    high = lax.reduce_precision(d_tokens, 8, 7)
    halves = jnp.concatenate([high.astype(BF16), (d_tokens - high).astype(BF16)], axis=0)
    halves = product_nt(halves, to_relative)
    grad_tokens = (halves[:rows] + halves[rows:]).reshape(batch, block, width)
    grad_side = d_side_in.reshape(batch, block, -1)
    early = jnp.stack(
        [grad_norm_attn, grad_norm_laurel, grad_norm_before, grad_norm_after, grad_norm_layer]
    )
    early = plan.total(plan.from_relative(early))
    late = jnp.concatenate([plan.from_relative(grad_norm_input[None])[0], grad_norm_query, grad_norm_key])
    late = plan.total(late)
    late_parts = split_columns(late, [width, head_size, head_size])
    return (
        output,
        grad_tokens,
        grad_side,
        grad_query,
        grad_key,
        grad_value,
        grad_output,
        grad_left,
        grad_right,
        grad_gate,
        grad_up,
        grad_down,
        grad_side_gate,
        grad_side_output,
        late_parts[0],
        early[0],
        early[1],
        early[2],
        early[3],
        early[4],
        late_parts[1],
        late_parts[2],
    )


def solution(mesh):
    seq_bits = int(math.log2(mesh.shape["seq"]))
    dp_bits = int(math.log2(mesh.shape["dp"]))
    plan = Plan(seq_bits, dp_bits)
    binary = Mesh(mesh.devices.reshape((2,) * (seq_bits + dp_bits)), plan.every)
    token_spec = P(plan.dp, plan.seq, None)
    weight_spec = P(plan.every, None)

    def step(*arrays):
        return body(plan, *arrays)

    return jax.shard_map(
        step,
        mesh=binary,
        in_specs=(token_spec, token_spec, P(plan.dp, plan.seq), P(plan.dp, None), token_spec)
        + (weight_spec,) * 11
        + (P(),) * 8,
        out_specs=(token_spec,) * 3 + (weight_spec,) * 11 + (P(),) * 8,
        check_vma=False,
    )
```

```python
import math

import jax
import jax.numpy as jnp
from jax import lax
from jax.sharding import Mesh
from jax.sharding import PartitionSpec as P

WINDOW = 512
SPAN = 256
EPS = 1e-06
HALF_ROOT = 1.0 / math.sqrt(2.0)
F32 = jnp.float32
BF16 = jnp.bfloat16


def rms(values, gain):
    return values * lax.rsqrt(jnp.mean(values * values, axis=-1, keepdims=True) + EPS) * gain


def gelu_tanh(values):
    return jax.nn.gelu(values, approximate=True)


def product(left, right):
    return jnp.dot(left, right, preferred_element_type=F32)


def product_nt(left, right):
    return lax.dot_general(left, right, (((1,), (1,)), ((), ())), preferred_element_type=F32)


def product_tn(left, right):
    return lax.dot_general(left, right, (((0,), (0,)), ((), ())), preferred_element_type=F32)


def rotate(values, places):
    size = values.shape[-1]
    half = size // 2
    freq = 10000.0 ** (-(2.0 * jnp.arange(half, dtype=F32)) / size)
    angle = places.astype(F32)[..., None] * freq
    cosine = jnp.cos(angle)[..., None, :]
    sine = jnp.sin(angle)[..., None, :]
    first = values[..., :half]
    second = values[..., half:]
    return jnp.concatenate(
        [first * cosine - second * sine, second * cosine + first * sine], axis=-1
    )


def middle(inputs, normed, attn_proj, laurel, gain_attn, gain_laurel, gain_before):
    resid = (inputs + rms(attn_proj, gain_attn) + normed + rms(laurel, gain_laurel)) * HALF_ROOT
    return (resid, rms(resid, gain_before))


def gate_act(gate_val, up_val):
    return gelu_tanh(gate_val) * up_val


def after_feed(resid_one, feed_out, gain_after):
    return resid_one + rms(feed_out, gain_after)


def side_act(side_pre, side_in):
    return gelu_tanh(side_pre) * side_in


def finish(resid_two, side_out, gain_layer):
    return resid_two + rms(side_out, gain_layer)


def swap(value, axis):
    return lax.ppermute(value, axis, [(0, 1), (1, 0)])


def split_columns(whole, widths):
    pieces = []
    offset = 0
    for width_one in widths:
        pieces.append(whole[..., offset : offset + width_one])
        offset = offset + width_one
    return pieces


class Plan:
    def __init__(self, seq_bits, dp_bits):
        self.seq = tuple("s%d" % i for i in range(seq_bits))
        self.dp = tuple("d%d" % i for i in range(dp_bits))
        self.every = self.seq + self.dp
        self.l, self.x = self.seq[-2:]
        self.c = self.dp[-1]
        self.team = (self.l, self.x, self.c)
        self.far_seq = self.seq[:-2]
        self.far_dp = self.dp[:-1]
        self.far = self.far_seq + self.far_dp
        self.canon = self.far + self.team
        self.order_x = self.far_seq + (self.l, self.x) + self.far_dp
        self.order_y = self.far_seq + (self.l,) + self.far_dp + (self.x,)

    def to_far_team(self, value):
        rows, width = value.shape
        parts = value.reshape((rows,) + (2,) * len(self.every) + (-1,))
        order = [0] + [1 + self.every.index(axis) for axis in self.canon] + [1 + len(self.every)]
        return parts.transpose(order).reshape(rows, width)

    def from_far_team(self, value):
        rows, width = value.shape
        parts = value.reshape((rows,) + (2,) * len(self.every) + (-1,))
        order = [0] + [1 + self.canon.index(axis) for axis in self.every] + [1 + len(self.every)]
        return parts.transpose(order).reshape(rows, width)

    def spread_order(self, width, order):
        own = jnp.arange(width, dtype=jnp.int32).reshape((2,) * len(self.canon) + (-1,))
        for at, axis in enumerate(self.canon):
            own = jnp.where(lax.axis_index(axis) == 1, jnp.flip(own, at), own)
        axes = (self.c,) + tuple(reversed(order))
        return own.transpose([self.canon.index(axis) for axis in axes] + [len(self.canon)]).reshape(-1)

    def grow(self, block, axes):
        for axis in axes:
            block = jnp.concatenate([block, swap(block, axis)], axis=0)
        return block

    def gather_pieces(self, block, axes):
        block = self.grow(block, axes[:-1])
        other = swap(block, axes[-1])
        return [block, other, swap(block, self.c), swap(other, self.c)]

    def gather(self, block, done, axes):
        held = list(reversed(done))
        block = block.reshape((2,) * len(held) + (-1, block.shape[-1]))
        for axis in axes:
            block = jnp.stack([block, swap(block, axis)], axis=0)
            held = [axis] + held
        block = block.transpose([held.index(axis) for axis in self.canon] + [len(held), len(held) + 1])
        for at, axis in enumerate(self.canon):
            block = jnp.where(lax.axis_index(axis) == 1, jnp.flip(block, at), block)
        return block.reshape((-1, block.shape[-1]))

    def spread_sum(self, pairs, order):
        half = pairs[0][0].shape[1] // 2
        away = jnp.concatenate([product_tn(one[:, half:], two).astype(BF16) for one, two in pairs], axis=1)
        kept = jnp.concatenate([product_tn(one[:, :half], two).astype(BF16) for one, two in pairs], axis=1)
        total = kept.astype(F32) + swap(away, self.c).astype(F32)
        for axis in reversed(order):
            half = total.shape[0] // 2
            total = total.astype(BF16)
            total = total[:half].astype(F32) + swap(total[half:], axis).astype(F32)
        return total

    def total(self, value):
        for axis in reversed(self.every):
            value = value + swap(value, axis)
        return value

    def team_gather(self, own):
        by_x, by_l = swap(own, self.x), swap(own, self.l)
        half = own.shape[0] // 2
        both = jnp.concatenate([swap(by_x[:half], self.l), swap(by_l[half:], self.x)], axis=0)
        return [jnp.concatenate([p, swap(p, self.c)], axis=0) for p in (own, by_x, by_l, both)]

    def team_scatter(self, chunks):
        sums = []
        for chunk in chunks:
            rows = chunk.shape[0] // 2
            other = swap(chunk[rows:].astype(BF16), self.c)
            sums.append(chunk[:rows].astype(F32) + other.astype(F32))
        own, by_x, by_l, both = sums
        half = own.shape[0] // 2
        both = both.astype(BF16)
        first = by_l[:half] + swap(both[:half], self.x).astype(F32)
        second = by_x[half:] + swap(both[half:], self.l).astype(F32)
        by_l = jnp.concatenate([first, by_l[half:]], axis=0).astype(BF16)
        by_x = jnp.concatenate([by_x[:half], second], axis=0).astype(BF16)
        return own + swap(by_l, self.l).astype(F32) + swap(by_x, self.x).astype(F32)


def product_split(left, pieces):
    width = left.shape[1] // len(pieces)
    return sum(product(left[:, i * width : (i + 1) * width], one) for i, one in enumerate(pieces))


def product_nt_split(left, pieces):
    return jnp.concatenate([product_nt(left, one) for one in pieces], axis=1)


def reorder(values, matrix):
    rows = values.shape[0]
    high = lax.reduce_precision(values, 8, 7)
    parts = jnp.concatenate([high.astype(BF16), (values - high).astype(BF16)], axis=0)
    parts = product_nt(parts, matrix)
    return parts[:rows] + parts[rows:]


def passed_along(value, axes, count, steps):
    initial, last = (max(0, -steps), min(count, count - steps))
    return lax.ppermute(value, axes, [(source, source + steps) for source in range(initial, last)])


def body(
    plan,
    tokens,
    per_layer,
    positions,
    span_start,
    cotangent,
    query_weight,
    key_weight,
    value_weight,
    output_weight,
    laurel_left,
    laurel_right,
    gate_weight,
    up_weight,
    down_weight,
    side_gate,
    side_output,
    norm_input,
    norm_attn,
    norm_laurel,
    norm_before,
    norm_after,
    norm_layer,
    norm_query,
    norm_key,
):
    batch, block, width = tokens.shape
    rows = batch * block
    head_size = norm_query.shape[0]
    heads = query_weight.shape[1] // head_size
    kv_heads = key_weight.shape[1] // head_size
    group = heads // kv_heads
    seq_count = 2 ** len(plan.seq)
    local_rows = gate_weight.shape[0]
    team_size = 2 ** len(plan.team)
    hidden_own = gate_weight.shape[1] // team_size

    kvl_widths = [key_weight.shape[1], value_weight.shape[1], laurel_left.shape[1]]
    rest_widths = [laurel_right.shape[1], side_gate.shape[1], side_output.shape[1]]
    feed_local = jnp.concatenate(
        [
            one.reshape(local_rows, team_size, hidden_own).transpose(1, 0, 2)
            for one in (gate_weight, up_weight, down_weight)
        ],
        axis=1,
    )
    feed_team = lax.all_to_all(feed_local, plan.team, split_axis=0, concat_axis=0, tiled=True)
    feed_team = feed_team.reshape(team_size, 3, local_rows, hidden_own).transpose(1, 0, 2, 3)
    blocks = (
        query_weight,
        jnp.concatenate([key_weight, value_weight, laurel_left], axis=1),
        output_weight,
        jnp.concatenate([laurel_right, side_gate, side_output], axis=1),
    )
    blocks = [plan.grow(block, plan.far_seq) for block in blocks]
    blocks, feed_team = lax.optimization_barrier((blocks, feed_team))
    feed_full = lax.all_gather(feed_team.reshape(-1, hidden_own), plan.far, axis=0, tiled=True)
    feed_full = feed_full.reshape(-1, 3, team_size * local_rows, hidden_own)
    steps_x, steps_y = plan.order_x[len(plan.far_seq) :], plan.order_y[len(plan.far_seq) :]
    query_full = plan.gather_pieces(blocks[0], steps_x)
    kvl_full = plan.gather_pieces(blocks[1], steps_y)
    output_full = plan.gather_pieces(blocks[2], steps_y)
    rest_full = plan.gather(blocks[3], plan.far_seq, steps_x + (plan.c,))
    right_full, side_gate_full, side_output_full = split_columns(rest_full, rest_widths)

    places = jnp.arange(width, dtype=jnp.int32)
    far_team = plan.to_far_team(places[None])[0]
    to_far_team = (places[:, None] == far_team[None, :]).astype(BF16)
    spread_x = (places[:, None] == plan.spread_order(width, plan.order_x)[None, :]).astype(BF16)
    spread_y = (places[:, None] == plan.spread_order(width, plan.order_y)[None, :]).astype(BF16)
    gains = jnp.stack([norm_input, norm_attn, norm_laurel, norm_before, norm_after, norm_layer])
    norm_input, norm_attn, norm_laurel, norm_before, norm_after, norm_layer = plan.to_far_team(gains)
    inputs = product(tokens.reshape(rows, width), to_far_team)
    upstream = product(cotangent.reshape(rows, width), to_far_team)
    side_in = per_layer.astype(F32).reshape(rows, -1)
    normed, pre_pull = jax.vjp(rms, inputs, norm_input)
    normed_low = normed.astype(BF16)
    normed_x = product(normed_low, spread_x).astype(BF16)
    normed_y = product(normed_low, spread_y).astype(BF16)
    queries = product_split(normed_x, query_full).reshape(batch, block, heads, head_size)
    keys, values, latent = split_columns(product_split(normed_y, kvl_full), kvl_widths)
    keys = keys.reshape(batch, block, kv_heads, head_size)
    values = values.reshape(batch, block, kv_heads, head_size)
    latent_low = latent.astype(BF16)

    def head_prep(query_in, key_in, value_in, gain_query, gain_key):
        return (
            rotate(rms(query_in, gain_query), positions),
            rotate(rms(key_in, gain_key), positions),
            rms(value_in, 1.0),
        )

    (rot_query, rot_key, rot_value), prep_pull = jax.vjp(
        head_prep, queries, keys, values, norm_query, norm_key
    )
    query_low = rot_query.astype(BF16)
    pair_low = jnp.stack([rot_key.astype(BF16), rot_value.astype(BF16)])
    left_count = WINDOW // block
    right_count = (SPAN + block - 2) // block
    offsets = list(range(left_count, 0, -1)) + [0] + list(range(-1, -right_count - 1, -1))
    gathered = []
    for offset in offsets:
        if offset == 0:
            gathered.append(pair_low)
        else:
            gathered.append(passed_along(pair_low, plan.seq, seq_count, offset))
    pairs_all = jnp.concatenate(gathered, axis=2)
    keys_all = pairs_all[0]
    values_all = pairs_all[1]
    key_count = keys_all.shape[1]
    seq_index = lax.axis_index(plan.seq)
    total_length = block * seq_count
    query_places = seq_index * block + jnp.arange(block, dtype=jnp.int32)
    key_places = (seq_index - left_count) * block + jnp.arange(key_count, dtype=jnp.int32)
    in_query = (query_places[None, :, None] >= span_start[:, None, :]) & (
        query_places[None, :, None] < span_start[:, None, :] + SPAN
    )
    in_key = (key_places[None, :, None] >= span_start[:, None, :]) & (
        key_places[None, :, None] < span_start[:, None, :] + SPAN
    )
    same = jnp.any(in_query[:, :, None, :] & in_key[:, None, :, :], axis=-1)
    near = (key_places[None, :] <= query_places[:, None]) & (
        query_places[:, None] - key_places[None, :] < WINDOW
    )
    valid = (key_places >= 0) & (key_places < total_length)
    allowed = (valid[None, None, :] & (near[None] | same))[:, None, None]
    query_group = query_low.reshape(batch, block, kv_heads, group, head_size)
    scores = jnp.einsum("btkgd,bskd->bkgts", query_group, keys_all, preferred_element_type=F32)
    masked = jnp.where(allowed, scores, -1e30)
    top = jnp.max(masked, axis=-1, keepdims=True)
    expo = jnp.exp(masked - top)
    total = jnp.sum(expo, axis=-1, keepdims=True)
    probs = expo / total
    probs_low = probs.astype(BF16)
    attended = jnp.einsum("bkgts,bskd->btkgd", probs_low, values_all, preferred_element_type=F32)
    attended_low = attended.reshape(rows, heads * head_size).astype(BF16)
    attn_proj = reorder(product_nt_split(attended_low, output_full), spread_y)
    laurel = product_nt(latent_low, right_full)
    (resid_one, feed_in), mid_pull = jax.vjp(
        middle, inputs, normed, attn_proj, laurel, norm_attn, norm_laurel, norm_before
    )

    feed_low = feed_in.astype(BF16)
    feed_full, feed_low = lax.optimization_barrier((feed_full, feed_low))
    gate_full, up_full, down_full = [feed_full[:, at].reshape(width, hidden_own) for at in range(3)]
    feed_chunks = plan.team_gather(feed_low)
    pulls = []
    hidden_chunks = []
    feed_parts = []
    for chunk in feed_chunks:
        hidden, pull = jax.vjp(gate_act, product(chunk, gate_full), product(chunk, up_full))
        hidden_low = hidden.astype(BF16)
        pulls.append(pull)
        hidden_chunks.append(hidden_low)
        feed_parts.append(product_nt(hidden_low, down_full).astype(BF16))
    feed_out = plan.team_scatter(feed_parts)

    resid_two, after_pull = jax.vjp(after_feed, resid_one, feed_out, norm_after)
    resid_low = resid_two.astype(BF16)
    side_pre = product(resid_low, side_gate_full)
    side_val, side_pull = jax.vjp(side_act, side_pre, side_in)
    side_low = side_val.astype(BF16)
    side_out = product_nt(side_low, side_output_full)
    result, final_pull = jax.vjp(finish, resid_two, side_out, norm_layer)
    output = product_nt(result.astype(BF16), to_far_team).astype(BF16).reshape(batch, block, width)

    d_resid_two, d_side_out, grad_norm_layer = final_pull(upstream)
    d_side_out_low = d_side_out.astype(BF16)
    d_side = product(d_side_out_low, side_output_full)
    d_side_pre, d_side_in = side_pull(d_side)
    d_side_pre_low = d_side_pre.astype(BF16)
    d_resid_two = d_resid_two + product_nt(d_side_pre_low, side_gate_full)
    d_resid_one, d_feed_out, grad_norm_after = after_pull(d_resid_two)

    d_out_chunks = plan.team_gather(d_feed_out.astype(BF16))
    d_gate_chunks = []
    d_up_chunks = []
    d_feed_parts = []
    for chunk, pull in zip(d_out_chunks, pulls):
        d_gate, d_up = pull(product(chunk, down_full))
        d_gate_chunks.append(d_gate.astype(BF16))
        d_up_chunks.append(d_up.astype(BF16))
        part = product_nt(d_gate_chunks[-1], gate_full) + product_nt(d_up_chunks[-1], up_full)
        d_feed_parts.append(part.astype(BF16))
    d_feed_in = plan.team_scatter(d_feed_parts)

    feed_all = jnp.concatenate(feed_chunks, axis=0)
    d_out_all = jnp.concatenate(d_out_chunks, axis=0)
    feed_terms = jnp.stack(
        [
            product_tn(left, jnp.concatenate(right, axis=0)).astype(BF16).reshape(-1, team_size * local_rows, hidden_own)
            for left, right in (
                (feed_all, d_gate_chunks),
                (feed_all, d_up_chunks),
                (d_out_all, hidden_chunks),
            )
        ],
        axis=1,
    )
    d_feed_in, feed_terms = lax.optimization_barrier((d_feed_in, feed_terms))
    feed_sum = lax.psum_scatter(
        feed_terms.reshape(-1, hidden_own), plan.far, scatter_dimension=0, tiled=True
    )
    feed_sum = feed_sum.reshape(3, team_size, local_rows, hidden_own).transpose(1, 0, 2, 3)
    feed_grads = lax.all_to_all(
        feed_sum.reshape(team_size, 3 * local_rows, hidden_own),
        plan.team,
        split_axis=0,
        concat_axis=0,
        tiled=True,
    )
    grad_gate, grad_up, grad_down = [
        jnp.concatenate(
            [feed_grads[at, index * local_rows : (index + 1) * local_rows] for at in range(team_size)],
            axis=1,
        ).astype(F32)
        for index in range(3)
    ]

    (
        d_inputs,
        d_normed,
        d_attn_proj,
        d_laurel,
        grad_norm_attn,
        grad_norm_laurel,
        grad_norm_before,
    ) = mid_pull((d_resid_one, d_feed_in))
    d_attn_low = d_attn_proj.astype(BF16)
    d_laurel_low = d_laurel.astype(BF16)
    d_attn_y = product(d_attn_low, spread_y).astype(BF16)
    d_attended_low = product_split(d_attn_y, output_full).astype(BF16)
    d_latent_low = product(d_laurel_low, right_full).astype(BF16)
    spread = jnp.concatenate([d_laurel_low, resid_low, d_side_out_low], axis=0)
    spread = product(spread, spread_x).astype(BF16)
    grad_output = plan.spread_sum([(d_attn_y, attended_low)], plan.order_y)
    grad_right, grad_side_gate, grad_side_output = split_columns(
        plan.spread_sum(
            [
                (spread[:rows], latent_low),
                (spread[rows : 2 * rows], d_side_pre_low),
                (spread[2 * rows :], side_low),
            ],
            plan.order_x,
        ),
        rest_widths,
    )

    d_att = d_attended_low.reshape(batch, block, kv_heads, group, head_size)
    d_values_all = jnp.einsum("bkgts,btkgd->bskd", probs_low, d_att, preferred_element_type=F32)
    d_probs = jnp.einsum("btkgd,bskd->bkgts", d_att, values_all, preferred_element_type=F32)
    d_scores = probs * (d_probs - jnp.sum(probs * d_probs, axis=-1, keepdims=True))
    d_scores_low = d_scores.astype(BF16)
    d_query_rot = jnp.einsum("bkgts,bskd->btkgd", d_scores_low, keys_all, preferred_element_type=F32)
    d_keys_all = jnp.einsum(
        "bkgts,btkgd->bskd", d_scores_low, query_group, preferred_element_type=F32
    )
    d_pairs = jnp.stack([d_keys_all, d_values_all])
    d_pair_total = d_pairs[:, :, left_count * block : (left_count + 1) * block]
    for position, offset in enumerate(offsets):
        if offset != 0:
            piece = d_pairs[:, :, position * block : (position + 1) * block].astype(BF16)
            d_pair_total = d_pair_total + passed_along(piece, plan.seq, seq_count, -offset).astype(F32)
    d_queries, d_keys, d_values, grad_norm_query, grad_norm_key = prep_pull(
        (d_query_rot.reshape(batch, block, heads, head_size), d_pair_total[0], d_pair_total[1])
    )
    d_queries_low = d_queries.reshape(rows, -1).astype(BF16)
    d_kvl_low = jnp.concatenate(
        [
            d_keys.reshape(rows, -1).astype(BF16),
            d_values.reshape(rows, -1).astype(BF16),
            d_latent_low,
        ],
        axis=1,
    )
    grad_query = plan.spread_sum([(normed_x, d_queries_low)], plan.order_x)
    grad_key, grad_value, grad_left = split_columns(
        plan.spread_sum([(normed_y, d_kvl_low)], plan.order_y), kvl_widths
    )
    d_normed = d_normed + reorder(product_nt_split(d_queries_low, query_full), spread_x)
    d_normed = d_normed + reorder(product_nt_split(d_kvl_low, kvl_full), spread_y)
    d_inputs_norm, grad_norm_input = pre_pull(d_normed)
    grad_tokens = reorder(d_inputs + d_inputs_norm, to_far_team).reshape(batch, block, width)
    grad_side = d_side_in.reshape(batch, block, -1)
    early = jnp.stack(
        [grad_norm_attn, grad_norm_laurel, grad_norm_before, grad_norm_after, grad_norm_layer]
    )
    early = plan.total(plan.from_far_team(early))
    late = jnp.concatenate([plan.from_far_team(grad_norm_input[None])[0], grad_norm_query, grad_norm_key])
    late = plan.total(late)
    late_parts = split_columns(late, [width, head_size, head_size])
    return (
        output,
        grad_tokens,
        grad_side,
        grad_query,
        grad_key,
        grad_value,
        grad_output,
        grad_left,
        grad_right,
        grad_gate,
        grad_up,
        grad_down,
        grad_side_gate,
        grad_side_output,
        late_parts[0],
        early[0],
        early[1],
        early[2],
        early[3],
        early[4],
        late_parts[1],
        late_parts[2],
    )


def solution(mesh):
    seq_bits = int(math.log2(mesh.shape["seq"]))
    dp_bits = int(math.log2(mesh.shape["dp"]))
    plan = Plan(seq_bits, dp_bits)
    binary = Mesh(mesh.devices.reshape((2,) * (seq_bits + dp_bits)), plan.every)
    token_spec = P(plan.dp, plan.seq, None)
    weight_spec = P(plan.every, None)

    def step(*arrays):
        return body(plan, *arrays)

    return jax.shard_map(
        step,
        mesh=binary,
        in_specs=(token_spec, token_spec, P(plan.dp, plan.seq), P(plan.dp, None), token_spec)
        + (weight_spec,) * 11
        + (P(),) * 8,
        out_specs=(token_spec,) * 3 + (weight_spec,) * 11 + (P(),) * 8,
        check_vma=False,
    )
```

```python
import math

import jax
import jax.numpy as jnp
from jax import lax
from jax.sharding import Mesh
from jax.sharding import PartitionSpec as P

WINDOW = 512
SPAN = 256
EPS = 1e-06
HALF_ROOT = 1.0 / math.sqrt(2.0)
F32 = jnp.float32
BF16 = jnp.bfloat16


def rms(values, gain):
    return values * lax.rsqrt(jnp.mean(values * values, axis=-1, keepdims=True) + EPS) * gain


def gelu_tanh(values):
    return jax.nn.gelu(values, approximate=True)


def product(left, right):
    return jnp.dot(left, right, preferred_element_type=F32)


def product_nt(left, right):
    return lax.dot_general(left, right, (((1,), (1,)), ((), ())), preferred_element_type=F32)


def product_tn(left, right):
    return lax.dot_general(left, right, (((0,), (0,)), ((), ())), preferred_element_type=F32)


def rotate(values, places):
    size = values.shape[-1]
    half = size // 2
    freq = 10000.0 ** (-(2.0 * jnp.arange(half, dtype=F32)) / size)
    angle = places.astype(F32)[..., None] * freq
    cosine = jnp.cos(angle)[..., None, :]
    sine = jnp.sin(angle)[..., None, :]
    first = values[..., :half]
    second = values[..., half:]
    return jnp.concatenate(
        [first * cosine - second * sine, second * cosine + first * sine], axis=-1
    )


def middle(inputs, normed, attn_proj, laurel, gain_attn, gain_laurel, gain_before):
    resid = (inputs + rms(attn_proj, gain_attn) + normed + rms(laurel, gain_laurel)) * HALF_ROOT
    return (resid, rms(resid, gain_before))


def gate_act(gate_val, up_val):
    return gelu_tanh(gate_val) * up_val


def after_feed(resid_one, feed_out, gain_after):
    return resid_one + rms(feed_out, gain_after)


def side_act(side_pre, side_in):
    return gelu_tanh(side_pre) * side_in


def finish(resid_two, side_out, gain_layer):
    return resid_two + rms(side_out, gain_layer)


def swap(value, axis):
    return lax.ppermute(value, axis, [(0, 1), (1, 0)])


def together(*values):
    return lax.optimization_barrier(values)


def split_columns(whole, widths):
    pieces = []
    offset = 0
    for width_one in widths:
        pieces.append(whole[..., offset : offset + width_one])
        offset = offset + width_one
    return pieces


class Plan:
    def __init__(self, seq_bits, dp_bits):
        self.seq = tuple("s%d" % i for i in range(seq_bits))
        self.dp = tuple("d%d" % i for i in range(dp_bits))
        self.every = self.seq + self.dp
        self.l, self.x = self.seq[-2:]
        self.c = self.dp[-1]
        self.team = (self.l, self.x, self.c)
        self.far_seq = self.seq[:-2]
        self.far_dp = self.dp[:-1]
        self.far = self.far_seq + self.far_dp
        self.canon = self.far + self.team
        self.order_x = self.far_seq + (self.l, self.x) + self.far_dp
        self.order_y = self.far_seq + (self.l,) + self.far_dp + (self.x,)

    def to_far_team(self, value):
        rows, width = value.shape
        parts = value.reshape((rows,) + (2,) * len(self.every) + (-1,))
        order = [0] + [1 + self.every.index(axis) for axis in self.canon] + [1 + len(self.every)]
        return parts.transpose(order).reshape(rows, width)

    def from_far_team(self, value):
        rows, width = value.shape
        parts = value.reshape((rows,) + (2,) * len(self.every) + (-1,))
        order = [0] + [1 + self.canon.index(axis) for axis in self.every] + [1 + len(self.every)]
        return parts.transpose(order).reshape(rows, width)

    def spread_order(self, width, order):
        own = jnp.arange(width, dtype=jnp.int32).reshape((2,) * len(self.canon) + (-1,))
        for at, axis in enumerate(self.canon):
            own = jnp.where(lax.axis_index(axis) == 1, jnp.flip(own, at), own)
        axes = (self.c,) + tuple(reversed(order))
        return own.transpose([self.canon.index(axis) for axis in axes] + [len(self.canon)]).reshape(-1)

    def grow(self, block, axes):
        for axis in axes:
            block = jnp.concatenate([block, swap(block, axis)], axis=0)
        return block

    def gather_pieces(self, block, axes):
        block = self.grow(block, axes[:-1])
        other = swap(block, axes[-1])
        return [block, other, swap(block, self.c), swap(other, self.c)]


    def gather(self, block, done, axes):
        held = list(reversed(done))
        block = block.reshape((2,) * len(held) + (-1, block.shape[-1]))
        for axis in axes:
            block = jnp.stack([block, swap(block, axis)], axis=0)
            held = [axis] + held
        block = block.transpose([held.index(axis) for axis in self.canon] + [len(held), len(held) + 1])
        for at, axis in enumerate(self.canon):
            block = jnp.where(lax.axis_index(axis) == 1, jnp.flip(block, at), block)
        return block.reshape((-1, block.shape[-1]))

    def spread_begin(self, pairs):
        half = pairs[0][0].shape[1] // 2
        away = jnp.concatenate([product_tn(one[:, half:], two).astype(BF16) for one, two in pairs], axis=1)
        kept = jnp.concatenate([product_tn(one[:, :half], two).astype(BF16) for one, two in pairs], axis=1)
        return (kept.astype(F32) + swap(away, self.c).astype(F32)).astype(BF16)

    def spread_end(self, total, order):
        for axis in reversed(order):
            half = total.shape[0] // 2
            total = total.astype(BF16)
            total = total[:half].astype(F32) + swap(total[half:], axis).astype(F32)
        return total

    def total(self, value):
        for axis in reversed(self.every):
            value = value + swap(value, axis)
        return value

    def team_map(self, own, function):
        def chunk_of(piece):
            return jnp.concatenate([piece, swap(piece, self.c)], axis=0)

        by_x, by_l = swap(own, self.x), swap(own, self.l)
        chunks = [chunk_of(own)]
        results = [function(chunks[0])]
        by_x, by_l, results = together(by_x, by_l, results)
        half = own.shape[0] // 2
        both = jnp.concatenate([swap(by_x[:half], self.l), swap(by_l[half:], self.x)], axis=0)
        for piece in (by_x, by_l, both):
            chunks.append(chunk_of(piece))
            results.append(function(chunks[-1]))
        return chunks, results

    def team_scatter(self, chunks):
        sums = []
        for chunk in chunks:
            rows = chunk.shape[0] // 2
            other = swap(chunk[rows:].astype(BF16), self.c)
            sums.append(chunk[:rows].astype(F32) + other.astype(F32))
        own, by_x, by_l, both = sums
        half = own.shape[0] // 2
        both = both.astype(BF16)
        first = by_l[:half] + swap(both[:half], self.x).astype(F32)
        second = by_x[half:] + swap(both[half:], self.l).astype(F32)
        by_l = jnp.concatenate([first, by_l[half:]], axis=0).astype(BF16)
        by_x = jnp.concatenate([by_x[:half], second], axis=0).astype(BF16)
        return own + swap(by_l, self.l).astype(F32) + swap(by_x, self.x).astype(F32)


def product_split(left, pieces):
    width = left.shape[1] // len(pieces)
    return sum(product(left[:, i * width : (i + 1) * width], one) for i, one in enumerate(pieces))


def product_nt_split(left, pieces):
    return jnp.concatenate([product_nt(left, one) for one in pieces], axis=1)


def reorder(values, matrix):
    rows = values.shape[0]
    high = lax.reduce_precision(values, 8, 7)
    parts = jnp.concatenate([high.astype(BF16), (values - high).astype(BF16)], axis=0)
    parts = product_nt(parts, matrix)
    return parts[:rows] + parts[rows:]


def passed_along(value, axes, count, steps):
    initial, last = (max(0, -steps), min(count, count - steps))
    return lax.ppermute(value, axes, [(source, source + steps) for source in range(initial, last)])


def body(
    plan,
    tokens,
    per_layer,
    positions,
    span_start,
    cotangent,
    query_weight,
    key_weight,
    value_weight,
    output_weight,
    laurel_left,
    laurel_right,
    gate_weight,
    up_weight,
    down_weight,
    side_gate,
    side_output,
    norm_input,
    norm_attn,
    norm_laurel,
    norm_before,
    norm_after,
    norm_layer,
    norm_query,
    norm_key,
):
    batch, block, width = tokens.shape
    rows = batch * block
    head_size = norm_query.shape[0]
    heads = query_weight.shape[1] // head_size
    kv_heads = key_weight.shape[1] // head_size
    group = heads // kv_heads
    seq_count = 2 ** len(plan.seq)
    local_rows = gate_weight.shape[0]
    team_size = 2 ** len(plan.team)
    hidden_own = gate_weight.shape[1] // team_size

    kvl_widths = [key_weight.shape[1], value_weight.shape[1], laurel_left.shape[1]]
    rest_widths = [laurel_right.shape[1], side_gate.shape[1], side_output.shape[1]]
    feed_local = jnp.concatenate(
        [
            one.reshape(local_rows, team_size, hidden_own).transpose(1, 0, 2)
            for one in (gate_weight, up_weight, down_weight)
        ],
        axis=1,
    )
    feed_team = lax.all_to_all(feed_local, plan.team, split_axis=0, concat_axis=0, tiled=True)
    feed_team = feed_team.reshape(team_size, 3, local_rows, hidden_own).transpose(1, 0, 2, 3)
    blocks = (
        query_weight,
        jnp.concatenate([key_weight, value_weight, laurel_left], axis=1),
        output_weight,
        jnp.concatenate([laurel_right, side_gate, side_output], axis=1),
    )
    first_axes = plan.far_seq + (plan.l,)
    steps_x, steps_y = plan.order_x[len(first_axes) :], plan.order_y[len(first_axes) :]
    query_block, kvl_block = [plan.grow(block, first_axes) for block in blocks[:2]]
    output_block, rest_block = [plan.grow(block, plan.far_seq) for block in blocks[2:]]
    kvl_block, query_block, output_block, rest_block, feed_team = lax.optimization_barrier(
        (kvl_block, query_block, output_block, rest_block, feed_team)
    )
    feed_full = lax.all_gather(feed_team.reshape(-1, hidden_own), plan.far, axis=0, tiled=True)
    feed_full = feed_full.reshape(-1, 3, team_size * local_rows, hidden_own)
    kvl_full = plan.gather_pieces(kvl_block, steps_y)
    query_full = plan.gather_pieces(query_block, steps_x)
    output_block, kvl_full = together(output_block, kvl_full)
    output_full = plan.gather_pieces(plan.grow(output_block, (plan.l,)), steps_y)
    rest_block, query_full = together(rest_block, query_full)
    rest_full = plan.gather(rest_block, plan.far_seq, (plan.l,) + steps_x + (plan.c,))
    right_full, side_gate_full, side_output_full = split_columns(rest_full, rest_widths)

    places = jnp.arange(width, dtype=jnp.int32)
    far_team = plan.to_far_team(places[None])[0]
    to_far_team = (places[:, None] == far_team[None, :]).astype(BF16)
    spread_x = (places[:, None] == plan.spread_order(width, plan.order_x)[None, :]).astype(BF16)
    spread_y = (places[:, None] == plan.spread_order(width, plan.order_y)[None, :]).astype(BF16)
    gains = jnp.stack([norm_input, norm_attn, norm_laurel, norm_before, norm_after, norm_layer])
    norm_input, norm_attn, norm_laurel, norm_before, norm_after, norm_layer = plan.to_far_team(gains)
    inputs = product(tokens.reshape(rows, width), to_far_team)
    upstream = product(cotangent.reshape(rows, width), to_far_team)
    side_in = per_layer.astype(F32).reshape(rows, -1)
    normed, pre_pull = jax.vjp(rms, inputs, norm_input)
    normed_low = normed.astype(BF16)
    normed_x = product(normed_low, spread_x).astype(BF16)
    normed_y = product(normed_low, spread_y).astype(BF16)
    queries = product_split(normed_x, query_full).reshape(batch, block, heads, head_size)
    keys, values, latent = split_columns(product_split(normed_y, kvl_full), kvl_widths)
    keys = keys.reshape(batch, block, kv_heads, head_size)
    values = values.reshape(batch, block, kv_heads, head_size)
    latent_low = latent.astype(BF16)

    def head_prep(query_in, key_in, value_in, gain_query, gain_key):
        return (
            rotate(rms(query_in, gain_query), positions),
            rotate(rms(key_in, gain_key), positions),
            rms(value_in, 1.0),
        )

    (rot_query, rot_key, rot_value), prep_pull = jax.vjp(
        head_prep, queries, keys, values, norm_query, norm_key
    )
    query_low = rot_query.astype(BF16)
    pair_low = jnp.stack([rot_key.astype(BF16), rot_value.astype(BF16)])
    left_count = WINDOW // block
    right_count = (SPAN + block - 2) // block
    offsets = list(range(left_count, 0, -1)) + [0] + list(range(-1, -right_count - 1, -1))
    gathered = []
    for offset in offsets:
        if offset == 0:
            gathered.append(pair_low)
        else:
            gathered.append(passed_along(pair_low, plan.seq, seq_count, offset))
    pairs_all = jnp.concatenate(gathered, axis=2)
    keys_all = pairs_all[0]
    values_all = pairs_all[1]
    key_count = keys_all.shape[1]
    seq_index = lax.axis_index(plan.seq)
    total_length = block * seq_count
    query_places = seq_index * block + jnp.arange(block, dtype=jnp.int32)
    key_places = (seq_index - left_count) * block + jnp.arange(key_count, dtype=jnp.int32)
    in_query = (query_places[None, :, None] >= span_start[:, None, :]) & (
        query_places[None, :, None] < span_start[:, None, :] + SPAN
    )
    in_key = (key_places[None, :, None] >= span_start[:, None, :]) & (
        key_places[None, :, None] < span_start[:, None, :] + SPAN
    )
    same = jnp.any(in_query[:, :, None, :] & in_key[:, None, :, :], axis=-1)
    near = (key_places[None, :] <= query_places[:, None]) & (
        query_places[:, None] - key_places[None, :] < WINDOW
    )
    valid = (key_places >= 0) & (key_places < total_length)
    allowed = (valid[None, None, :] & (near[None] | same))[:, None, None]
    query_group = query_low.reshape(batch, block, kv_heads, group, head_size)
    scores = jnp.einsum("btkgd,bskd->bkgts", query_group, keys_all, preferred_element_type=F32)
    masked = jnp.where(allowed, scores, -1e30)
    top = jnp.max(masked, axis=-1, keepdims=True)
    expo = jnp.exp(masked - top)
    total = jnp.sum(expo, axis=-1, keepdims=True)
    probs = expo / total
    probs_low = probs.astype(BF16)
    attended = jnp.einsum("bkgts,bskd->btkgd", probs_low, values_all, preferred_element_type=F32)
    attended_low = attended.reshape(rows, heads * head_size).astype(BF16)
    attn_proj = reorder(product_nt_split(attended_low, output_full), spread_y)
    laurel = product_nt(latent_low, right_full)
    (resid_one, feed_in), mid_pull = jax.vjp(
        middle, inputs, normed, attn_proj, laurel, norm_attn, norm_laurel, norm_before
    )

    feed_low = feed_in.astype(BF16)
    feed_full, feed_low = lax.optimization_barrier((feed_full, feed_low))
    gate_full, up_full, down_full = [feed_full[:, at].reshape(width, hidden_own) for at in range(3)]
    pulls = []
    hidden_chunks = []

    def forward_chunk(chunk):
        hidden, pull = jax.vjp(gate_act, product(chunk, gate_full), product(chunk, up_full))
        hidden_low = hidden.astype(BF16)
        pulls.append(pull)
        hidden_chunks.append(hidden_low)
        return product_nt(hidden_low, down_full).astype(BF16)

    feed_chunks, feed_parts = plan.team_map(feed_low, forward_chunk)
    feed_out = plan.team_scatter(feed_parts)

    resid_two, after_pull = jax.vjp(after_feed, resid_one, feed_out, norm_after)
    resid_low = resid_two.astype(BF16)
    side_pre = product(resid_low, side_gate_full)
    side_val, side_pull = jax.vjp(side_act, side_pre, side_in)
    side_low = side_val.astype(BF16)
    side_out = product_nt(side_low, side_output_full)
    result, final_pull = jax.vjp(finish, resid_two, side_out, norm_layer)
    output = product_nt(result.astype(BF16), to_far_team).astype(BF16).reshape(batch, block, width)

    d_resid_two, d_side_out, grad_norm_layer = final_pull(upstream)
    d_side_out_low = d_side_out.astype(BF16)
    d_side = product(d_side_out_low, side_output_full)
    d_side_pre, d_side_in = side_pull(d_side)
    d_side_pre_low = d_side_pre.astype(BF16)
    d_resid_two = d_resid_two + product_nt(d_side_pre_low, side_gate_full)
    d_resid_one, d_feed_out, grad_norm_after = after_pull(d_resid_two)

    d_gate_chunks = []
    d_up_chunks = []

    def backward_chunk(chunk):
        d_gate, d_up = pulls[len(d_gate_chunks)](product(chunk, down_full))
        d_gate_chunks.append(d_gate.astype(BF16))
        d_up_chunks.append(d_up.astype(BF16))
        part = product_nt(d_gate_chunks[-1], gate_full) + product_nt(d_up_chunks[-1], up_full)
        return part.astype(BF16)

    d_out_chunks, d_feed_parts = plan.team_map(d_feed_out.astype(BF16), backward_chunk)
    d_gate_chunks, d_up_chunks, feed_chunks, d_out_chunks, hidden_chunks, d_feed_parts = together(
        d_gate_chunks, d_up_chunks, feed_chunks, d_out_chunks, hidden_chunks, d_feed_parts
    )
    d_feed_in = plan.team_scatter(d_feed_parts)

    feed_all = jnp.concatenate(feed_chunks, axis=0)
    d_out_all = jnp.concatenate(d_out_chunks, axis=0)
    feed_terms = jnp.stack(
        [
            product_tn(left, jnp.concatenate(right, axis=0)).astype(BF16).reshape(-1, team_size * local_rows, hidden_own)
            for left, right in (
                (feed_all, d_gate_chunks),
                (feed_all, d_up_chunks),
                (d_out_all, hidden_chunks),
            )
        ],
        axis=1,
    )
    d_feed_in, feed_terms = together(d_feed_in, feed_terms)
    feed_sum = lax.psum_scatter(
        feed_terms.reshape(-1, hidden_own), plan.far, scatter_dimension=0, tiled=True
    )
    feed_sum = feed_sum.reshape(3, team_size, local_rows, hidden_own).transpose(1, 0, 2, 3)
    feed_grads = lax.all_to_all(
        feed_sum.reshape(team_size, 3 * local_rows, hidden_own),
        plan.team,
        split_axis=0,
        concat_axis=0,
        tiled=True,
    )
    grad_gate, grad_up, grad_down = [
        jnp.concatenate(
            [feed_grads[at, index * local_rows : (index + 1) * local_rows] for at in range(team_size)],
            axis=1,
        ).astype(F32)
        for index in range(3)
    ]

    (
        d_inputs,
        d_normed,
        d_attn_proj,
        d_laurel,
        grad_norm_attn,
        grad_norm_laurel,
        grad_norm_before,
    ) = mid_pull((d_resid_one, d_feed_in))
    d_attn_low = d_attn_proj.astype(BF16)
    d_laurel_low = d_laurel.astype(BF16)
    d_attn_y = product(d_attn_low, spread_y).astype(BF16)
    d_attended_low = product_split(d_attn_y, output_full).astype(BF16)
    d_latent_low = product(d_laurel_low, right_full).astype(BF16)
    spread = jnp.concatenate([d_laurel_low, resid_low, d_side_out_low], axis=0)
    spread = product(spread, spread_x).astype(BF16)
    output_sum = plan.spread_begin([(d_attn_y, attended_low)])
    d_attended_low, output_sum = together(d_attended_low, output_sum)
    grad_output = plan.spread_end(output_sum, plan.order_y)

    d_att = d_attended_low.reshape(batch, block, kv_heads, group, head_size)
    d_values_all = jnp.einsum("bkgts,btkgd->bskd", probs_low, d_att, preferred_element_type=F32)
    d_probs = jnp.einsum("btkgd,bskd->bkgts", d_att, values_all, preferred_element_type=F32)
    d_scores = probs * (d_probs - jnp.sum(probs * d_probs, axis=-1, keepdims=True))
    d_scores_low = d_scores.astype(BF16)
    d_query_rot = jnp.einsum("bkgts,bskd->btkgd", d_scores_low, keys_all, preferred_element_type=F32)
    d_keys_all = jnp.einsum(
        "bkgts,btkgd->bskd", d_scores_low, query_group, preferred_element_type=F32
    )
    d_pairs = jnp.stack([d_keys_all, d_values_all])
    d_pair_total = d_pairs[:, :, left_count * block : (left_count + 1) * block]
    for position, offset in enumerate(offsets):
        if offset != 0:
            piece = d_pairs[:, :, position * block : (position + 1) * block].astype(BF16)
            d_pair_total = d_pair_total + passed_along(piece, plan.seq, seq_count, -offset).astype(F32)
    d_queries, d_keys, d_values, grad_norm_query, grad_norm_key = prep_pull(
        (d_query_rot.reshape(batch, block, heads, head_size), d_pair_total[0], d_pair_total[1])
    )
    d_queries_low = d_queries.reshape(rows, -1).astype(BF16)
    query_sum = plan.spread_begin([(normed_x, d_queries_low)])
    d_keys, d_values, query_sum = together(d_keys, d_values, query_sum)
    d_kvl_low = jnp.concatenate(
        [
            d_keys.reshape(rows, -1).astype(BF16),
            d_values.reshape(rows, -1).astype(BF16),
            d_latent_low,
        ],
        axis=1,
    )
    spread, d_kvl_low = together(spread, d_kvl_low)
    rest_sum = plan.spread_begin(
        [
            (spread[:rows], latent_low),
            (spread[rows : 2 * rows], d_side_pre_low),
            (spread[2 * rows :], side_low),
        ]
    )
    kvl_sum = plan.spread_begin([(normed_y, d_kvl_low)])
    grad_right, grad_side_gate, grad_side_output = split_columns(
        plan.spread_end(rest_sum, plan.order_x), rest_widths
    )
    d_normed = d_normed + reorder(product_nt_split(d_queries_low, query_full), spread_x)
    d_normed = d_normed + reorder(product_nt_split(d_kvl_low, kvl_full), spread_y)
    d_inputs_norm, grad_norm_input = pre_pull(d_normed)
    grad_tokens = reorder(d_inputs + d_inputs_norm, to_far_team).reshape(batch, block, width)
    grad_side = d_side_in.reshape(batch, block, -1)
    norm_grads = jnp.stack(
        [
            grad_norm_input,
            grad_norm_attn,
            grad_norm_laurel,
            grad_norm_before,
            grad_norm_after,
            grad_norm_layer,
        ]
    )
    gain_grads = jnp.concatenate(
        [plan.from_far_team(norm_grads).reshape(-1), grad_norm_query, grad_norm_key]
    )
    gain_grads, kvl_sum = together(gain_grads, kvl_sum)
    grad_query = plan.spread_end(query_sum, plan.order_x)
    grad_key, grad_value, grad_left = split_columns(
        plan.spread_end(kvl_sum, plan.order_y), kvl_widths
    )
    gain_grads = plan.total(gain_grads)
    gain_parts = split_columns(gain_grads, [width] * 6 + [head_size] * 2)
    return (
        output,
        grad_tokens,
        grad_side,
        grad_query,
        grad_key,
        grad_value,
        grad_output,
        grad_left,
        grad_right,
        grad_gate,
        grad_up,
        grad_down,
        grad_side_gate,
        grad_side_output,
    ) + tuple(gain_parts)


def solution(mesh):
    seq_bits = int(math.log2(mesh.shape["seq"]))
    dp_bits = int(math.log2(mesh.shape["dp"]))
    plan = Plan(seq_bits, dp_bits)
    binary = Mesh(mesh.devices.reshape((2,) * (seq_bits + dp_bits)), plan.every)
    token_spec = P(plan.dp, plan.seq, None)
    weight_spec = P(plan.every, None)

    def step(*arrays):
        return body(plan, *arrays)

    return jax.shard_map(
        step,
        mesh=binary,
        in_specs=(token_spec, token_spec, P(plan.dp, plan.seq), P(plan.dp, None), token_spec)
        + (weight_spec,) * 11
        + (P(),) * 8,
        out_specs=(token_spec,) * 3 + (weight_spec,) * 11 + (P(),) * 8,
        check_vma=False,
    )
```

```python
import math

import jax
import jax.numpy as jnp
from jax import lax
from jax.sharding import Mesh
from jax.sharding import PartitionSpec as P

WINDOW = 512
SPAN = 256
EPS = 1e-06
HALF_ROOT = 1.0 / math.sqrt(2.0)
F32 = jnp.float32
BF16 = jnp.bfloat16


def rms(values, gain):
    return values * lax.rsqrt(jnp.mean(values * values, axis=-1, keepdims=True) + EPS) * gain


def gelu_tanh(values):
    return jax.nn.gelu(values, approximate=True)


def product(left, right):
    return jnp.dot(left, right, preferred_element_type=F32)


def product_nt(left, right):
    return lax.dot_general(left, right, (((1,), (1,)), ((), ())), preferred_element_type=F32)


def product_tn(left, right):
    return lax.dot_general(left, right, (((0,), (0,)), ((), ())), preferred_element_type=F32)


def rotate(values, places):
    size = values.shape[-1]
    half = size // 2
    freq = 10000.0 ** (-(2.0 * jnp.arange(half, dtype=F32)) / size)
    angle = places.astype(F32)[..., None] * freq
    cosine = jnp.cos(angle)[..., None, :]
    sine = jnp.sin(angle)[..., None, :]
    first = values[..., :half]
    second = values[..., half:]
    return jnp.concatenate(
        [first * cosine - second * sine, second * cosine + first * sine], axis=-1
    )


def middle(inputs, normed, attn_proj, laurel, gain_attn, gain_laurel, gain_before):
    resid = (inputs + rms(attn_proj, gain_attn) + normed + rms(laurel, gain_laurel)) * HALF_ROOT
    return (resid, rms(resid, gain_before))


def gate_act(gate_val, up_val):
    return gelu_tanh(gate_val) * up_val


def after_feed(resid_one, feed_out, gain_after):
    return resid_one + rms(feed_out, gain_after)


def side_act(side_pre, side_in):
    return gelu_tanh(side_pre) * side_in


def finish(resid_two, side_out, gain_layer):
    return resid_two + rms(side_out, gain_layer)


def swap(value, axis):
    return lax.ppermute(value, axis, [(0, 1), (1, 0)])


def together(*values):
    return lax.optimization_barrier(values)


def split_columns(whole, widths):
    pieces = []
    offset = 0
    for width_one in widths:
        pieces.append(whole[..., offset : offset + width_one])
        offset = offset + width_one
    return pieces


class Plan:
    def __init__(self, seq_bits, dp_bits):
        self.seq = tuple("s%d" % i for i in range(seq_bits))
        self.dp = tuple("d%d" % i for i in range(dp_bits))
        self.every = self.seq + self.dp
        self.l, self.x = self.seq[-2:]
        self.c = self.dp[-1]
        self.team = (self.l, self.x, self.c)
        self.far_seq = self.seq[:-2]
        self.far_dp = self.dp[:-1]
        self.far = self.far_seq + self.far_dp
        self.canon = self.far + self.team
        self.order = self.far_seq + (self.l,) + self.far_dp + (self.x,)

    def flipped(self, value, axes, dims):
        for axis, dim in zip(axes, dims):
            value = jnp.where(lax.axis_index(axis) == 1, jnp.flip(value, dim), value)
        return value

    def to_far_team(self, value):
        rows, width = value.shape
        parts = value.reshape((rows,) + (2,) * len(self.every) + (-1,))
        parts = self.flipped(parts, self.far, [1 + self.every.index(axis) for axis in self.far])
        order = [0] + [1 + self.every.index(axis) for axis in self.canon] + [1 + len(self.every)]
        return parts.transpose(order).reshape(rows, width)

    def from_far_team(self, value):
        rows, width = value.shape
        parts = value.reshape((rows,) + (2,) * len(self.every) + (-1,))
        parts = self.flipped(parts, self.far, [1 + self.canon.index(axis) for axis in self.far])
        order = [0] + [1 + self.canon.index(axis) for axis in self.every] + [1 + len(self.every)]
        return parts.transpose(order).reshape(rows, width)

    def spread_order(self, width):
        own = jnp.arange(width, dtype=jnp.int32).reshape((2,) * len(self.canon) + (-1,))
        own = self.flipped(own, self.team, [self.canon.index(axis) for axis in self.team])
        axes = (self.c,) + tuple(reversed(self.order))
        return own.transpose([self.canon.index(axis) for axis in axes] + [len(self.canon)]).reshape(-1)

    def pieces(self, blocks, axes):
        for axis in axes:
            blocks = [one for block in blocks for one in (block, swap(block, axis))]
        return blocks

    def grow(self, block, axes):
        for axis in axes:
            block = jnp.concatenate([block, swap(block, axis)], axis=0)
        return block

    def gather_pieces(self, block):
        other = swap(block, self.order[-1])
        return [block, other, swap(block, self.c), swap(other, self.c)]

    def far_team_rows(self, pieces):
        axes = (self.c,) + tuple(reversed(self.order))
        whole = jnp.concatenate(pieces, axis=0)
        whole = whole.reshape((2,) * len(axes) + (-1, whole.shape[-1]))
        whole = whole.transpose([axes.index(axis) for axis in self.canon] + [len(axes), len(axes) + 1])
        whole = self.flipped(whole, self.team, [self.canon.index(axis) for axis in self.team])
        return whole.reshape((-1, whole.shape[-1]))

    def fold(self, pieces, axes):
        for axis in reversed(axes):
            pieces = [
                (kept.astype(F32) + swap(away, axis).astype(F32)).astype(BF16)
                for kept, away in zip(pieces[::2], pieces[1::2])
            ]
        return pieces

    def spread_begin(self, pairs):
        half = pairs[0][0].shape[1] // 2
        away = jnp.concatenate([product_tn(one[:, half:], two).astype(BF16) for one, two in pairs], axis=1)
        kept = jnp.concatenate([product_tn(one[:, :half], two).astype(BF16) for one, two in pairs], axis=1)
        return (kept.astype(F32) + swap(away, self.c).astype(F32)).astype(BF16)

    def spread_step(self, total, axes):
        for axis in axes:
            half = total.shape[0] // 2
            total = total[:half].astype(F32) + swap(total[half:], axis).astype(F32)
            if axis != self.order[0]:
                total = total.astype(BF16)
        return total

    def near_gather(self, key, value):
        pair = jnp.stack([key, value])[:, None]
        for axis in reversed(self.far_seq):
            pair = jnp.concatenate([pair, swap(pair, axis)], axis=1)
        key, value = pair[0][None], pair[1][None]
        key = jnp.concatenate([key, swap(key, self.x)], axis=0)
        key = jnp.stack([key, swap(key, self.l)], axis=0)
        value = jnp.concatenate([value, swap(value, self.l)], axis=0)
        value = jnp.stack([value, swap(value, self.x)], axis=1)
        return [one.reshape((-1,) + one.shape[3:]) for one in (key, value)]

    def near_sum(self, key, value):
        def step(total, dim, axis):
            total = total.astype(BF16)
            away = swap(lax.index_in_dim(total, 1, dim, False), axis).astype(F32)
            return lax.index_in_dim(total, 0, dim, False).astype(F32) + away

        shape = (2, 2) + (2,) * len(self.far_seq)
        key, value = [one.reshape(shape + one.shape[1:]) for one in (key, value)]
        key = step(step(key, 0, self.l), 0, self.x)
        value = step(step(value, 1, self.x), 0, self.l)
        pair = jnp.stack([key, value])
        for axis in self.far_seq:
            pair = step(pair, 1, axis)
        return pair

    def near_places(self):
        place = jnp.zeros((1,), jnp.int32)
        for axis in (self.l, self.x) + self.far_seq:
            bit = lax.axis_index(axis)
            weight = 2 ** (len(self.seq) - 1 - self.seq.index(axis))
            place = (place[:, None] + weight * jnp.stack([bit, 1 - bit])[None, :]).reshape(-1)
        return place

    def own_rows(self, sums, local_rows):
        size = 2 ** len(self.team)
        sums = jnp.concatenate([one.reshape(size, local_rows, -1) for one in sums], axis=1)
        moved = lax.all_to_all(sums, self.team, split_axis=0, concat_axis=0, tiled=True)
        return [
            jnp.concatenate([moved[at, first : first + local_rows] for at in range(size)], axis=1).astype(F32)
            for first in range(0, moved.shape[1], local_rows)
        ]

    def total(self, value):
        for axis in reversed(self.every):
            value = value + swap(value, axis)
        return value

    def team_map(self, own, function):
        def chunk_of(piece):
            return jnp.concatenate([piece, swap(piece, self.c)], axis=0)

        by_x, by_l = swap(own, self.x), swap(own, self.l)
        chunks = [chunk_of(own)]
        results = [function(chunks[0])]
        by_x, by_l, results = together(by_x, by_l, results)
        half = own.shape[0] // 2
        both = jnp.concatenate([swap(by_x[:half], self.l), swap(by_l[half:], self.x)], axis=0)
        for piece in (by_x, by_l, both):
            chunks.append(chunk_of(piece))
            results.append(function(chunks[-1]))
        return chunks, results

    def team_scatter(self, chunks):
        sums = []
        for chunk in chunks:
            rows = chunk.shape[0] // 2
            other = swap(chunk[rows:].astype(BF16), self.c)
            sums.append(chunk[:rows].astype(F32) + other.astype(F32))
        own, by_x, by_l, both = sums
        half = own.shape[0] // 2
        both = both.astype(BF16)
        first = by_l[:half] + swap(both[:half], self.x).astype(F32)
        second = by_x[half:] + swap(both[half:], self.l).astype(F32)
        by_l = jnp.concatenate([first, by_l[half:]], axis=0).astype(BF16)
        by_x = jnp.concatenate([by_x[:half], second], axis=0).astype(BF16)
        return own + swap(by_l, self.l).astype(F32) + swap(by_x, self.x).astype(F32)


def product_split(left, pieces):
    width = left.shape[1] // len(pieces)
    return sum(product(left[:, i * width : (i + 1) * width], one) for i, one in enumerate(pieces))


def product_nt_split(left, pieces):
    return jnp.concatenate([product_nt(left, one) for one in pieces], axis=1)


def reorder(values, matrix):
    rows = values.shape[0]
    high = lax.reduce_precision(values, 8, 7)
    parts = jnp.concatenate([high.astype(BF16), (values - high).astype(BF16)], axis=0)
    parts = product_nt(parts, matrix)
    return parts[:rows] + parts[rows:]


def passed_along(value, axes, count, steps):
    initial, last = (max(0, -steps), min(count, count - steps))
    return lax.ppermute(value, axes, [(source, source + steps) for source in range(initial, last)])


def body(
    plan,
    tokens,
    per_layer,
    positions,
    span_start,
    cotangent,
    query_weight,
    key_weight,
    value_weight,
    output_weight,
    laurel_left,
    laurel_right,
    gate_weight,
    up_weight,
    down_weight,
    side_gate,
    side_output,
    norm_input,
    norm_attn,
    norm_laurel,
    norm_before,
    norm_after,
    norm_layer,
    norm_query,
    norm_key,
):
    batch, block, width = tokens.shape
    rows = batch * block
    head_size = norm_query.shape[0]
    heads = query_weight.shape[1] // head_size
    kv_heads = key_weight.shape[1] // head_size
    group = heads // kv_heads
    seq_count = 2 ** len(plan.seq)
    local_rows = gate_weight.shape[0]
    team_size = 2 ** len(plan.team)
    hidden_own = gate_weight.shape[1] // team_size

    kvl_widths = [key_weight.shape[1], value_weight.shape[1], laurel_left.shape[1]]
    rest_widths = [laurel_right.shape[1], side_gate.shape[1], side_output.shape[1]]
    feed_local = jnp.concatenate(
        [
            one.reshape(local_rows, team_size, hidden_own).transpose(1, 0, 2)
            for one in (gate_weight, up_weight, down_weight)
        ],
        axis=1,
    )
    feed_team = lax.all_to_all(feed_local, plan.team, split_axis=0, concat_axis=0, tiled=True)
    gate_own, up_own, down_own = [
        feed_team[:, index * local_rows : (index + 1) * local_rows].reshape(-1, hidden_own)
        for index in range(3)
    ]
    block_widths = [sum(kvl_widths), query_weight.shape[1], output_weight.shape[1] + sum(rest_widths)]
    attn_block = jnp.concatenate(
        [key_weight, value_weight, laurel_left, query_weight, output_weight]
        + [laurel_right, side_gate, side_output],
        axis=1,
    )
    attn_block = plan.grow(attn_block, plan.far_seq)
    attn_block, gate_own, up_own, down_own = together(attn_block, gate_own, up_own, down_own)
    attn_block = plan.grow(attn_block, (plan.l,))
    gate_far = plan.pieces([gate_own], plan.far_seq)
    gate_first = plan.pieces(gate_far[:1], plan.far_dp)
    up_first = plan.pieces([up_own], plan.far_dp)
    attn_block, gate_far, gate_first, up_first = together(attn_block, gate_far, gate_first, up_first)
    kvl_block, query_block, rest_block = split_columns(attn_block, block_widths)
    kvl_block = plan.grow(kvl_block, plan.far_dp)
    query_block = plan.grow(query_block, plan.far_dp)
    up_far = plan.pieces([up_own], plan.far_seq)
    kvl_full = plan.gather_pieces(kvl_block)
    kvl_full, query_block, up_far = together(kvl_full, query_block, up_far)
    query_full = plan.gather_pieces(query_block)
    down_far = plan.pieces([down_own], plan.far_seq)
    rest_block = plan.grow(rest_block, plan.far_dp)

    places = jnp.arange(width, dtype=jnp.int32)
    far_team = plan.to_far_team(places[None])[0]
    to_far_team = (places[:, None] == far_team[None, :]).astype(BF16)
    to_spread = (places[:, None] == plan.spread_order(width)[None, :]).astype(BF16)
    gains = jnp.stack([norm_input, norm_attn, norm_laurel, norm_before, norm_after, norm_layer])
    norm_input, norm_attn, norm_laurel, norm_before, norm_after, norm_layer = plan.to_far_team(gains)
    inputs = product(tokens.reshape(rows, width), to_far_team)
    upstream = product(cotangent.reshape(rows, width), to_far_team)
    side_in = per_layer.astype(F32).reshape(rows, -1)
    normed, pre_pull = jax.vjp(rms, inputs, norm_input)
    normed_low = normed.astype(BF16)
    normed_spread = product(normed_low, to_spread).astype(BF16)
    keys, values, latent = split_columns(product_split(normed_spread, kvl_full), kvl_widths)
    queries = product_split(normed_spread, query_full).reshape(batch, block, heads, head_size)
    keys = keys.reshape(batch, block, kv_heads, head_size)
    values = values.reshape(batch, block, kv_heads, head_size)
    latent_low = latent.astype(BF16)

    def head_prep(query_in, key_in, value_in, gain_query, gain_key):
        return (
            rotate(rms(query_in, gain_query), positions),
            rotate(rms(key_in, gain_key), positions),
            rms(value_in, 1.0),
        )

    (rot_query, rot_key, rot_value), prep_pull = jax.vjp(
        head_prep, queries, keys, values, norm_query, norm_key
    )
    query_low = rot_query.astype(BF16)
    key_low = rot_key.astype(BF16)
    value_low = rot_value.astype(BF16)
    left_count = WINDOW // block
    right_count = (SPAN + block - 2) // block
    offsets = list(range(left_count, 0, -1)) + [0] + list(range(-1, -right_count - 1, -1))
    whole_sequence = seq_count <= len(offsets) + 1
    seq_index = lax.axis_index(plan.seq)
    total_length = block * seq_count
    if whole_sequence:
        keys_all, values_all = [
            one.swapaxes(0, 1).reshape(batch, total_length, kv_heads, head_size)
            for one in plan.near_gather(key_low, value_low)
        ]
        key_blocks = plan.near_places()
    else:
        pair_low = jnp.stack([key_low, value_low])
        gathered = [
            passed_along(pair_low, plan.seq, seq_count, offset) if offset else pair_low
            for offset in offsets
        ]
        keys_all, values_all = jnp.concatenate(gathered, axis=2)
        key_blocks = seq_index - jnp.array(offsets, dtype=jnp.int32)
    key_count = keys_all.shape[1]
    keys_all, values_all, query_full, down_far, rest_block = together(
        keys_all, values_all, query_full, down_far, rest_block
    )
    rest_full = plan.gather_pieces(rest_block)
    gate_last = plan.pieces(gate_far[1:], plan.far_dp)
    down_first = plan.pieces(down_far[:1], plan.far_dp)
    query_places = seq_index * block + jnp.arange(block, dtype=jnp.int32)
    key_places = (key_blocks[:, None] * block + jnp.arange(block, dtype=jnp.int32)).reshape(-1)
    in_query = (query_places[None, :, None] >= span_start[:, None, :]) & (
        query_places[None, :, None] < span_start[:, None, :] + SPAN
    )
    in_key = (key_places[None, :, None] >= span_start[:, None, :]) & (
        key_places[None, :, None] < span_start[:, None, :] + SPAN
    )
    same = jnp.any(in_query[:, :, None, :] & in_key[:, None, :, :], axis=-1)
    near = (key_places[None, :] <= query_places[:, None]) & (
        query_places[:, None] - key_places[None, :] < WINDOW
    )
    valid = (key_places >= 0) & (key_places < total_length)
    allowed = (valid[None, None, :] & (near[None] | same))[:, None, None]
    query_group = query_low.reshape(batch, block, kv_heads, group, head_size)
    scores = jnp.einsum("btkgd,bskd->bkgts", query_group, keys_all, preferred_element_type=F32)
    masked = jnp.where(allowed, scores, -1e30)
    top = jnp.max(masked, axis=-1, keepdims=True)
    expo = jnp.exp(masked - top)
    total = jnp.sum(expo, axis=-1, keepdims=True)
    probs = expo / total
    probs_low = probs.astype(BF16)
    attended = jnp.einsum("bkgts,bskd->btkgd", probs_low, values_all, preferred_element_type=F32)
    attended_low = attended.reshape(rows, heads * head_size).astype(BF16)
    attended_low, rest_full, gate_last, down_first = together(
        attended_low, rest_full, gate_last, down_first
    )
    up_last = plan.pieces(up_far[1:], plan.far_dp)
    down_last = plan.pieces(down_far[1:], plan.far_dp)
    gate_full, up_full, down_full = [
        jnp.concatenate(first + last, axis=0)
        for first, last in ((gate_first, gate_last), (up_first, up_last), (down_first, down_last))
    ]
    output_full = [one[:, : output_weight.shape[1]] for one in rest_full]
    rest_full = plan.far_team_rows([one[:, output_weight.shape[1] :] for one in rest_full])
    right_full, side_gate_full, side_output_full = split_columns(rest_full, rest_widths)
    attn_proj = reorder(product_nt_split(attended_low, output_full), to_spread)
    laurel = product_nt(latent_low, right_full)
    (resid_one, feed_in), mid_pull = jax.vjp(
        middle, inputs, normed, attn_proj, laurel, norm_attn, norm_laurel, norm_before
    )

    feed_low = feed_in.astype(BF16)
    pulls = []
    hidden_chunks = []

    def forward_chunk(chunk):
        hidden, pull = jax.vjp(gate_act, product(chunk, gate_full), product(chunk, up_full))
        hidden_low = hidden.astype(BF16)
        pulls.append(pull)
        hidden_chunks.append(hidden_low)
        return product_nt(hidden_low, down_full).astype(BF16)

    feed_chunks, feed_parts = plan.team_map(feed_low, forward_chunk)
    feed_out = plan.team_scatter(feed_parts)

    resid_two, after_pull = jax.vjp(after_feed, resid_one, feed_out, norm_after)
    resid_low = resid_two.astype(BF16)
    side_pre = product(resid_low, side_gate_full)
    side_val, side_pull = jax.vjp(side_act, side_pre, side_in)
    side_low = side_val.astype(BF16)
    side_out = product_nt(side_low, side_output_full)
    result, final_pull = jax.vjp(finish, resid_two, side_out, norm_layer)
    output = product_nt(result.astype(BF16), to_far_team).astype(BF16).reshape(batch, block, width)

    d_resid_two, d_side_out, grad_norm_layer = final_pull(upstream)
    d_side_out_low = d_side_out.astype(BF16)
    d_side = product(d_side_out_low, side_output_full)
    d_side_pre, d_side_in = side_pull(d_side)
    d_side_pre_low = d_side_pre.astype(BF16)
    d_resid_two = d_resid_two + product_nt(d_side_pre_low, side_gate_full)
    d_resid_one, d_feed_out, grad_norm_after = after_pull(d_resid_two)

    d_gate_chunks = []
    d_up_chunks = []

    def backward_chunk(chunk):
        d_gate, d_up = pulls[len(d_gate_chunks)](product(chunk, down_full))
        d_gate_chunks.append(d_gate.astype(BF16))
        d_up_chunks.append(d_up.astype(BF16))
        part = product_nt(d_gate_chunks[-1], gate_full) + product_nt(d_up_chunks[-1], up_full)
        return part.astype(BF16)

    d_out_chunks, d_feed_parts = plan.team_map(d_feed_out.astype(BF16), backward_chunk)
    d_gate_chunks, d_up_chunks, feed_chunks, d_out_chunks, hidden_chunks, d_feed_parts = together(
        d_gate_chunks, d_up_chunks, feed_chunks, d_out_chunks, hidden_chunks, d_feed_parts
    )
    d_feed_in = plan.team_scatter(d_feed_parts)

    feed_all = jnp.concatenate(feed_chunks, axis=0)
    d_out_all = jnp.concatenate(d_out_chunks, axis=0)
    far_count = 2 ** len(plan.far)

    def far_terms(left, right):
        right = jnp.concatenate(right, axis=0)
        part = width // far_count
        return [
            product_tn(left[:, at * part : (at + 1) * part], right).astype(BF16)
            for at in range(far_count)
        ]

    gate_terms = far_terms(feed_all, d_gate_chunks)
    up_terms = far_terms(feed_all, d_up_chunks)
    down_terms = far_terms(d_out_all, hidden_chunks)
    gate_terms = plan.fold(gate_terms, plan.far_dp)
    d_feed_in, gate_terms, up_terms, down_terms = together(d_feed_in, gate_terms, up_terms, down_terms)

    (
        d_inputs,
        d_normed,
        d_attn_proj,
        d_laurel,
        grad_norm_attn,
        grad_norm_laurel,
        grad_norm_before,
    ) = mid_pull((d_resid_one, d_feed_in))
    d_attn_low = d_attn_proj.astype(BF16)
    d_laurel_low = d_laurel.astype(BF16)
    d_attn_spread = product(d_attn_low, to_spread).astype(BF16)
    d_attended_low = product_split(d_attn_spread, output_full).astype(BF16)
    d_latent_low = product(d_laurel_low, right_full).astype(BF16)
    spread = jnp.concatenate([d_laurel_low, resid_low, d_side_out_low], axis=0)
    spread = product(spread, to_spread).astype(BF16)
    output_sum = plan.spread_begin(
        [
            (d_attn_spread, attended_low),
            (spread[:rows], latent_low),
            (spread[rows : 2 * rows], d_side_pre_low),
            (spread[2 * rows :], side_low),
        ]
    )
    d_attended_low, output_sum, gate_terms, up_terms = together(
        d_attended_low, output_sum, gate_terms, up_terms
    )
    steps = tuple(reversed(plan.order))
    output_sum = plan.spread_step(output_sum, steps[:1])
    gate_terms = plan.fold(gate_terms, plan.far_seq)
    up_terms = plan.fold(up_terms, plan.far_dp)

    d_att = d_attended_low.reshape(batch, block, kv_heads, group, head_size)
    d_values_all = jnp.einsum("bkgts,btkgd->bskd", probs_low, d_att, preferred_element_type=F32)
    d_probs = jnp.einsum("btkgd,bskd->bkgts", d_att, values_all, preferred_element_type=F32)
    d_scores = probs * (d_probs - jnp.sum(probs * d_probs, axis=-1, keepdims=True))
    d_scores_low = d_scores.astype(BF16)
    d_query_rot = jnp.einsum("bkgts,bskd->btkgd", d_scores_low, keys_all, preferred_element_type=F32)
    d_keys_all = jnp.einsum(
        "bkgts,btkgd->bskd", d_scores_low, query_group, preferred_element_type=F32
    )
    d_keys_all, d_values_all, d_query_rot, gate_terms, up_terms, down_terms = together(
        d_keys_all, d_values_all, d_query_rot, gate_terms, up_terms, down_terms
    )
    up_terms = plan.fold(up_terms, plan.far_seq)
    down_terms = plan.fold(down_terms, plan.far_dp)
    if whole_sequence:
        d_pair_total = plan.near_sum(
            *[
                one.reshape(batch, seq_count, block, kv_heads, head_size).swapaxes(0, 1)
                for one in (d_keys_all, d_values_all)
            ]
        )
    else:
        d_pairs = jnp.stack([d_keys_all, d_values_all])
        d_pair_total = d_pairs[:, :, left_count * block : (left_count + 1) * block]
        for position, offset in enumerate(offsets):
            if offset != 0:
                piece = d_pairs[:, :, position * block : (position + 1) * block].astype(BF16)
                moved = passed_along(piece, plan.seq, seq_count, -offset)
                d_pair_total = d_pair_total + moved.astype(F32)
    d_queries, d_keys, d_values, grad_norm_query, grad_norm_key = prep_pull(
        (d_query_rot.reshape(batch, block, heads, head_size), d_pair_total[0], d_pair_total[1])
    )
    d_queries_low = d_queries.reshape(rows, -1).astype(BF16)
    query_sum = plan.spread_begin([(normed_spread, d_queries_low)])
    d_keys, d_values, output_sum, query_sum, up_terms, down_terms = together(
        d_keys, d_values, output_sum, query_sum, up_terms, down_terms
    )
    query_sum = plan.spread_step(query_sum, steps[:1])
    down_terms = plan.fold(down_terms, plan.far_seq)
    grad_gate, grad_up = plan.own_rows(gate_terms + up_terms, local_rows)
    (grad_down,) = plan.own_rows(down_terms, local_rows)
    d_kvl_low = jnp.concatenate(
        [
            d_keys.reshape(rows, -1).astype(BF16),
            d_values.reshape(rows, -1).astype(BF16),
            d_latent_low,
        ],
        axis=1,
    )
    kvl_sum = plan.spread_begin([(normed_spread, d_kvl_low)])
    d_spread = product_nt_split(d_queries_low, query_full) + product_nt_split(d_kvl_low, kvl_full)
    d_normed = d_normed + reorder(d_spread, to_spread)
    d_inputs_norm, grad_norm_input = pre_pull(d_normed)
    grad_tokens = reorder(d_inputs + d_inputs_norm, to_far_team).reshape(batch, block, width)
    grad_side = d_side_in.reshape(batch, block, -1)
    norm_grads = jnp.stack(
        [
            grad_norm_input,
            grad_norm_attn,
            grad_norm_laurel,
            grad_norm_before,
            grad_norm_after,
            grad_norm_layer,
        ]
    )
    gain_grads = jnp.concatenate(
        [plan.from_far_team(norm_grads).reshape(-1), grad_norm_query, grad_norm_key]
    )
    gain_grads, kvl_sum, grad_gate, grad_up = together(gain_grads, kvl_sum, grad_gate, grad_up)
    grad_query = plan.spread_step(query_sum, steps[1:])
    grad_output, grad_right, grad_side_gate, grad_side_output = split_columns(
        plan.spread_step(output_sum, steps[1:]), [output_weight.shape[1]] + rest_widths
    )
    grad_key, grad_value, grad_left = split_columns(plan.spread_step(kvl_sum, steps), kvl_widths)
    gain_grads = plan.total(gain_grads)
    gain_parts = split_columns(gain_grads, [width] * 6 + [head_size] * 2)
    return (
        output,
        grad_tokens,
        grad_side,
        grad_query,
        grad_key,
        grad_value,
        grad_output,
        grad_left,
        grad_right,
        grad_gate,
        grad_up,
        grad_down,
        grad_side_gate,
        grad_side_output,
    ) + tuple(gain_parts)


def solution(mesh):
    seq_bits = int(math.log2(mesh.shape["seq"]))
    dp_bits = int(math.log2(mesh.shape["dp"]))
    plan = Plan(seq_bits, dp_bits)
    binary = Mesh(mesh.devices.reshape((2,) * (seq_bits + dp_bits)), plan.every)
    token_spec = P(plan.dp, plan.seq, None)
    weight_spec = P(plan.every, None)

    def step(*arrays):
        return body(plan, *arrays)

    return jax.shard_map(
        step,
        mesh=binary,
        in_specs=(token_spec, token_spec, P(plan.dp, plan.seq), P(plan.dp, None), token_spec)
        + (weight_spec,) * 11
        + (P(),) * 8,
        out_specs=(token_spec,) * 3 + (weight_spec,) * 11 + (P(),) * 8,
        check_vma=False,
    )
```

```python
import math

import jax
import jax.numpy as jnp
from jax import lax
from jax.sharding import Mesh
from jax.sharding import PartitionSpec as P

WINDOW = 512
SPAN = 256
EPS = 1e-06
HALF_ROOT = 1.0 / math.sqrt(2.0)
F32 = jnp.float32
BF16 = jnp.bfloat16


def rms(values, gain):
    return values * lax.rsqrt(jnp.mean(values * values, axis=-1, keepdims=True) + EPS) * gain


def gelu_tanh(values):
    return jax.nn.gelu(values, approximate=True)


def product(left, right):
    return jnp.dot(left, right, preferred_element_type=F32)


def product_nt(left, right):
    return lax.dot_general(left, right, (((1,), (1,)), ((), ())), preferred_element_type=F32)


def product_tn(left, right):
    return lax.dot_general(left, right, (((0,), (0,)), ((), ())), preferred_element_type=F32)


def rotate(values, places):
    size = values.shape[-1]
    half = size // 2
    freq = 10000.0 ** (-(2.0 * jnp.arange(half, dtype=F32)) / size)
    angle = places.astype(F32)[..., None] * freq
    cosine = jnp.cos(angle)[..., None, :]
    sine = jnp.sin(angle)[..., None, :]
    first = values[..., :half]
    second = values[..., half:]
    return jnp.concatenate(
        [first * cosine - second * sine, second * cosine + first * sine], axis=-1
    )


def middle(inputs, normed, attn_proj, laurel, gain_attn, gain_laurel, gain_before):
    resid = (inputs + rms(attn_proj, gain_attn) + normed + rms(laurel, gain_laurel)) * HALF_ROOT
    return (resid, rms(resid, gain_before))


def gate_act(gate_val, up_val):
    return gelu_tanh(gate_val) * up_val


def after_feed(resid_one, feed_out, gain_after):
    return resid_one + rms(feed_out, gain_after)


def side_act(side_pre, side_in):
    return gelu_tanh(side_pre) * side_in


def finish(resid_two, side_out, gain_layer):
    return resid_two + rms(side_out, gain_layer)


def swap(value, axis):
    return lax.ppermute(value, axis, [(0, 1), (1, 0)])


def together(*values):
    return lax.optimization_barrier(values)


def split_columns(whole, widths):
    pieces = []
    offset = 0
    for width_one in widths:
        pieces.append(whole[..., offset : offset + width_one])
        offset = offset + width_one
    return pieces


class Plan:
    def __init__(self, seq_bits, dp_bits):
        self.seq = tuple("s%d" % i for i in range(seq_bits))
        self.dp = tuple("d%d" % i for i in range(dp_bits))
        self.every = self.seq + self.dp
        self.l, self.x = self.seq[-2:]
        self.c = self.dp[-1]
        self.team = (self.l, self.x, self.c)
        self.far_seq = self.seq[:-2]
        self.far_dp = self.dp[:-1]
        self.far = self.far_seq + self.far_dp
        self.canon = self.far + self.team
        self.order = self.far_seq + (self.l,) + self.far_dp + (self.x,)

    def flipped(self, value, axes, dims):
        for axis, dim in zip(axes, dims):
            value = jnp.where(lax.axis_index(axis) == 1, jnp.flip(value, dim), value)
        return value

    def to_far_team(self, value):
        rows, width = value.shape
        parts = value.reshape((rows,) + (2,) * len(self.every) + (-1,))
        parts = self.flipped(parts, self.far, [1 + self.every.index(axis) for axis in self.far])
        order = [0] + [1 + self.every.index(axis) for axis in self.canon] + [1 + len(self.every)]
        return parts.transpose(order).reshape(rows, width)

    def from_far_team(self, value):
        rows, width = value.shape
        parts = value.reshape((rows,) + (2,) * len(self.every) + (-1,))
        parts = self.flipped(parts, self.far, [1 + self.canon.index(axis) for axis in self.far])
        order = [0] + [1 + self.canon.index(axis) for axis in self.every] + [1 + len(self.every)]
        return parts.transpose(order).reshape(rows, width)

    def spread_order(self, width):
        own = jnp.arange(width, dtype=jnp.int32).reshape((2,) * len(self.canon) + (-1,))
        own = self.flipped(own, self.team, [self.canon.index(axis) for axis in self.team])
        axes = (self.c,) + tuple(reversed(self.order))
        return own.transpose([self.canon.index(axis) for axis in axes] + [len(self.canon)]).reshape(-1)

    def pieces(self, blocks, axes):
        for axis in axes:
            blocks = [one for block in blocks for one in (block, swap(block, axis))]
        return blocks

    def grow(self, block, axes):
        for axis in axes:
            block = jnp.concatenate([block, swap(block, axis)], axis=0)
        return block

    def gather_pieces(self, block):
        other = swap(block, self.order[-1])
        return [block, other, swap(block, self.c), swap(other, self.c)]

    def far_team_rows(self, pieces):
        axes = (self.c,) + tuple(reversed(self.order))
        whole = jnp.concatenate(pieces, axis=0)
        whole = whole.reshape((2,) * len(axes) + (-1, whole.shape[-1]))
        whole = whole.transpose([axes.index(axis) for axis in self.canon] + [len(axes), len(axes) + 1])
        whole = self.flipped(whole, self.team, [self.canon.index(axis) for axis in self.team])
        return whole.reshape((-1, whole.shape[-1]))

    def fold(self, pieces, axes):
        for axis in reversed(axes):
            pieces = [
                (kept.astype(F32) + swap(away, axis).astype(F32)).astype(BF16)
                for kept, away in zip(pieces[::2], pieces[1::2])
            ]
        return pieces

    def spread_begin(self, pairs):
        half = pairs[0][0].shape[1] // 2
        away = jnp.concatenate([product_tn(one[:, half:], two).astype(BF16) for one, two in pairs], axis=1)
        kept = jnp.concatenate([product_tn(one[:, :half], two).astype(BF16) for one, two in pairs], axis=1)
        return (kept.astype(F32) + swap(away, self.c).astype(F32)).astype(BF16)

    def spread_step(self, total, axes):
        for axis in axes:
            half = total.shape[0] // 2
            total = total[:half].astype(F32) + swap(total[half:], axis).astype(F32)
            if axis != self.order[0]:
                total = total.astype(BF16)
        return total

    def near_far(self, key, value):
        pair = jnp.stack([key, value])[:, None]
        for axis in reversed(self.far_seq):
            pair = jnp.concatenate([pair, swap(pair, axis)], axis=1)
        return pair

    def near_gather(self, pair):
        key, value = pair[0][None], pair[1][None]
        key = jnp.concatenate([key, swap(key, self.x)], axis=0)
        key = jnp.stack([key, swap(key, self.l)], axis=0)
        value = jnp.concatenate([value, swap(value, self.l)], axis=0)
        value = jnp.stack([value, swap(value, self.x)], axis=1)
        return [one.reshape((-1,) + one.shape[3:]) for one in (key, value)]

    def near_sum(self, key, value):
        def step(total, dim, axis):
            total = total.astype(BF16)
            away = swap(lax.index_in_dim(total, 1, dim, False), axis).astype(F32)
            return lax.index_in_dim(total, 0, dim, False).astype(F32) + away

        shape = (2, 2) + (2,) * len(self.far_seq)
        key, value = [one.reshape(shape + one.shape[1:]) for one in (key, value)]
        key = step(step(key, 0, self.l), 0, self.x)
        value = step(step(value, 1, self.x), 0, self.l)
        pair = jnp.stack([key, value])
        for axis in self.far_seq:
            pair = step(pair, 1, axis)
        return pair

    def near_places(self):
        place = jnp.zeros((1,), jnp.int32)
        for axis in (self.l, self.x) + self.far_seq:
            bit = lax.axis_index(axis)
            weight = 2 ** (len(self.seq) - 1 - self.seq.index(axis))
            place = (place[:, None] + weight * jnp.stack([bit, 1 - bit])[None, :]).reshape(-1)
        return place

    def own_rows(self, sums, local_rows):
        size = 2 ** len(self.team)
        sums = jnp.concatenate([one.reshape(size, local_rows, -1) for one in sums], axis=1)
        moved = lax.all_to_all(sums, self.team, split_axis=0, concat_axis=0, tiled=True)
        return [
            jnp.concatenate([moved[at, first : first + local_rows] for at in range(size)], axis=1).astype(F32)
            for first in range(0, moved.shape[1], local_rows)
        ]

    def total(self, value):
        for axis in reversed(self.every):
            value = value + swap(value, axis)
        return value

    def team_map(self, own, function):
        def chunk_of(piece):
            return jnp.concatenate([piece, swap(piece, self.c)], axis=0)

        by_x, by_l = swap(own, self.x), swap(own, self.l)
        chunks = [chunk_of(own)]
        results = [function(chunks[0])]
        by_x, by_l, results = together(by_x, by_l, results)
        half = own.shape[0] // 2
        both = jnp.concatenate([swap(by_x[:half], self.l), swap(by_l[half:], self.x)], axis=0)
        for piece in (by_x, by_l, both):
            chunks.append(chunk_of(piece))
            results.append(function(chunks[-1]))
        return chunks, results

    def core_sums(self, chunks):
        sums = []
        for chunk in chunks:
            rows = chunk.shape[0] // 2
            other = swap(chunk[rows:].astype(BF16), self.c)
            sums.append(chunk[:rows].astype(F32) + other.astype(F32))
        return sums

    def team_near(self, sums):
        own, by_x, by_l, both = sums
        half = own.shape[0] // 2
        both = both.astype(BF16)
        first = by_l[:half] + swap(both[:half], self.x).astype(F32)
        second = by_x[half:] + swap(both[half:], self.l).astype(F32)
        by_l = jnp.concatenate([first, by_l[half:]], axis=0).astype(BF16)
        by_x = jnp.concatenate([by_x[:half], second], axis=0).astype(BF16)
        return own, by_l, by_x

    def team_far(self, sums):
        own, by_l, by_x = sums
        return own + swap(by_l, self.l).astype(F32) + swap(by_x, self.x).astype(F32)


def product_split(left, pieces):
    width = left.shape[1] // len(pieces)
    return sum(product(left[:, i * width : (i + 1) * width], one) for i, one in enumerate(pieces))


def product_nt_split(left, pieces):
    return jnp.concatenate([product_nt(left, one) for one in pieces], axis=1)


def reorder(values, matrix):
    rows = values.shape[0]
    high = lax.reduce_precision(values, 8, 7)
    parts = jnp.concatenate([high.astype(BF16), (values - high).astype(BF16)], axis=0)
    parts = product_nt(parts, matrix)
    return parts[:rows] + parts[rows:]


def passed_along(value, axes, count, steps):
    initial, last = (max(0, -steps), min(count, count - steps))
    return lax.ppermute(value, axes, [(source, source + steps) for source in range(initial, last)])


def body(
    plan,
    tokens,
    per_layer,
    positions,
    span_start,
    cotangent,
    query_weight,
    key_weight,
    value_weight,
    output_weight,
    laurel_left,
    laurel_right,
    gate_weight,
    up_weight,
    down_weight,
    side_gate,
    side_output,
    norm_input,
    norm_attn,
    norm_laurel,
    norm_before,
    norm_after,
    norm_layer,
    norm_query,
    norm_key,
):
    batch, block, width = tokens.shape
    rows = batch * block
    head_size = norm_query.shape[0]
    heads = query_weight.shape[1] // head_size
    kv_heads = key_weight.shape[1] // head_size
    group = heads // kv_heads
    seq_count = 2 ** len(plan.seq)
    local_rows = gate_weight.shape[0]
    team_size = 2 ** len(plan.team)
    hidden_own = gate_weight.shape[1] // team_size

    kvl_widths = [
        key_weight.shape[1],
        value_weight.shape[1],
        laurel_left.shape[1],
        laurel_right.shape[1],
    ]
    rest_widths = [output_weight.shape[1], side_gate.shape[1], side_output.shape[1]]
    feed_local = jnp.concatenate(
        [
            one.reshape(local_rows, team_size, hidden_own).transpose(1, 0, 2)
            for one in (gate_weight, up_weight, down_weight)
        ],
        axis=1,
    )
    feed_team = lax.all_to_all(feed_local, plan.team, split_axis=0, concat_axis=0, tiled=True)
    gate_own, up_own, down_own = [
        feed_team[:, index * local_rows : (index + 1) * local_rows].reshape(-1, hidden_own)
        for index in range(3)
    ]
    block_widths = [sum(kvl_widths), query_weight.shape[1], sum(rest_widths)]
    attn_block = jnp.concatenate(
        [key_weight, value_weight, laurel_left, laurel_right, query_weight]
        + [output_weight, side_gate, side_output],
        axis=1,
    )
    attn_block = plan.grow(attn_block, plan.far_seq)
    attn_block, gate_own, up_own, down_own = together(attn_block, gate_own, up_own, down_own)
    attn_block = plan.grow(attn_block, (plan.l,))
    gate_first = plan.pieces([gate_own], plan.far_dp)
    up_first = plan.pieces([up_own], plan.far_dp)
    attn_block, gate_own, gate_first, up_first = together(attn_block, gate_own, gate_first, up_first)
    kvl_block, query_block, rest_block = split_columns(attn_block, block_widths)
    kvl_block = plan.grow(kvl_block, plan.far_dp)
    query_block = plan.grow(query_block, plan.far_dp)
    gate_far = plan.pieces([gate_own], plan.far_seq)
    kvl_full = plan.gather_pieces(kvl_block)
    kvl_full, query_block, gate_far, up_own, rest_block = together(
        kvl_full, query_block, gate_far, up_own, rest_block
    )
    up_far = plan.pieces([up_own], plan.far_seq)
    gate_last = plan.pieces(gate_far[1:], plan.far_dp)
    query_full = plan.gather_pieces(query_block)
    rest_block = plan.grow(rest_block, plan.far_dp)
    right_full = plan.far_team_rows([one[:, -kvl_widths[3] :] for one in kvl_full])
    kvl_full = [one[:, : -kvl_widths[3]] for one in kvl_full]

    places = jnp.arange(width, dtype=jnp.int32)
    far_team = plan.to_far_team(places[None])[0]
    to_far_team = (places[:, None] == far_team[None, :]).astype(BF16)
    to_spread = (places[:, None] == plan.spread_order(width)[None, :]).astype(BF16)
    gains = jnp.stack([norm_input, norm_attn, norm_laurel, norm_before, norm_after, norm_layer])
    norm_input, norm_attn, norm_laurel, norm_before, norm_after, norm_layer = plan.to_far_team(gains)
    inputs = product(tokens.reshape(rows, width), to_far_team)
    upstream = product(cotangent.reshape(rows, width), to_far_team)
    side_in = per_layer.astype(F32).reshape(rows, -1)
    normed, pre_pull = jax.vjp(rms, inputs, norm_input)
    normed_low = normed.astype(BF16)
    normed_spread = product(normed_low, to_spread).astype(BF16)
    keys, values, latent = split_columns(
        product_split(normed_spread, kvl_full), kvl_widths[:3]
    )
    queries = product_split(normed_spread, query_full).reshape(batch, block, heads, head_size)
    keys = keys.reshape(batch, block, kv_heads, head_size)
    values = values.reshape(batch, block, kv_heads, head_size)
    latent_low = latent.astype(BF16)

    def head_prep(query_in, key_in, value_in, gain_query, gain_key):
        return (
            rotate(rms(query_in, gain_query), positions),
            rotate(rms(key_in, gain_key), positions),
            rms(value_in, 1.0),
        )

    (rot_query, rot_key, rot_value), prep_pull = jax.vjp(
        head_prep, queries, keys, values, norm_query, norm_key
    )
    query_low = rot_query.astype(BF16)
    key_low = rot_key.astype(BF16)
    value_low = rot_value.astype(BF16)
    left_count = WINDOW // block
    right_count = (SPAN + block - 2) // block
    offsets = list(range(left_count, 0, -1)) + [0] + list(range(-1, -right_count - 1, -1))
    whole_sequence = seq_count <= len(offsets) + 1
    seq_index = lax.axis_index(plan.seq)
    total_length = block * seq_count
    if whole_sequence:
        pair_low = plan.near_far(key_low, value_low)
        pair_low, up_far, down_own = together(pair_low, up_far, down_own)
        keys_all, values_all = [
            one.swapaxes(0, 1).reshape(batch, total_length, kv_heads, head_size)
            for one in plan.near_gather(pair_low)
        ]
        key_blocks = plan.near_places()
    else:
        pair_low = jnp.stack([key_low, value_low])
        gathered = [
            passed_along(pair_low, plan.seq, seq_count, offset) if offset else pair_low
            for offset in offsets
        ]
        keys_all, values_all = jnp.concatenate(gathered, axis=2)
        key_blocks = seq_index - jnp.array(offsets, dtype=jnp.int32)
    key_count = keys_all.shape[1]
    down_far = plan.pieces([down_own], plan.far_seq)
    keys_all, values_all, rest_block = together(keys_all, values_all, rest_block)
    rest_full = plan.gather_pieces(rest_block)
    up_last = plan.pieces(up_far[1:], plan.far_dp)
    down_first = plan.pieces(down_far[:1], plan.far_dp)
    query_places = seq_index * block + jnp.arange(block, dtype=jnp.int32)
    key_places = (key_blocks[:, None] * block + jnp.arange(block, dtype=jnp.int32)).reshape(-1)
    in_query = (query_places[None, :, None] >= span_start[:, None, :]) & (
        query_places[None, :, None] < span_start[:, None, :] + SPAN
    )
    in_key = (key_places[None, :, None] >= span_start[:, None, :]) & (
        key_places[None, :, None] < span_start[:, None, :] + SPAN
    )
    same = jnp.any(in_query[:, :, None, :] & in_key[:, None, :, :], axis=-1)
    near = (key_places[None, :] <= query_places[:, None]) & (
        query_places[:, None] - key_places[None, :] < WINDOW
    )
    valid = (key_places >= 0) & (key_places < total_length)
    allowed = (valid[None, None, :] & (near[None] | same))[:, None, None]
    query_group = query_low.reshape(batch, block, kv_heads, group, head_size)
    scores = jnp.einsum("btkgd,bskd->bkgts", query_group, keys_all, preferred_element_type=F32)
    masked = jnp.where(allowed, scores, -1e30)
    top = jnp.max(masked, axis=-1, keepdims=True)
    expo = jnp.exp(masked - top)
    total = jnp.sum(expo, axis=-1, keepdims=True)
    probs = expo / total
    probs_low = probs.astype(BF16)
    attended = jnp.einsum("bkgts,bskd->btkgd", probs_low, values_all, preferred_element_type=F32)
    attended_low = attended.reshape(rows, heads * head_size).astype(BF16)
    attended_low, gate_last, up_last, down_first = together(
        attended_low, gate_last, up_last, down_first
    )
    down_last = plan.pieces(down_far[1:], plan.far_dp)
    gate_full, up_full, down_full = [
        jnp.concatenate(first + last, axis=0)
        for first, last in ((gate_first, gate_last), (up_first, up_last), (down_first, down_last))
    ]
    output_full = [one[:, : rest_widths[0]] for one in rest_full]
    side_full = plan.far_team_rows([one[:, rest_widths[0] :] for one in rest_full])
    side_gate_full, side_output_full = split_columns(side_full, rest_widths[1:])
    attn_proj = reorder(product_nt_split(attended_low, output_full), to_spread)
    laurel = product_nt(latent_low, right_full)
    (resid_one, feed_in), mid_pull = jax.vjp(
        middle, inputs, normed, attn_proj, laurel, norm_attn, norm_laurel, norm_before
    )

    feed_low = feed_in.astype(BF16)
    pulls = []
    hidden_chunks = []

    def forward_chunk(chunk):
        hidden, pull = jax.vjp(gate_act, product(chunk, gate_full), product(chunk, up_full))
        hidden_low = hidden.astype(BF16)
        pulls.append(pull)
        hidden_chunks.append(hidden_low)
        return product_nt(hidden_low, down_full).astype(BF16)

    feed_chunks, feed_parts = plan.team_map(feed_low, forward_chunk)
    feed_out = plan.team_far(plan.team_near(plan.core_sums(feed_parts)))

    resid_two, after_pull = jax.vjp(after_feed, resid_one, feed_out, norm_after)
    resid_low = resid_two.astype(BF16)
    side_pre = product(resid_low, side_gate_full)
    side_val, side_pull = jax.vjp(side_act, side_pre, side_in)
    side_low = side_val.astype(BF16)
    side_out = product_nt(side_low, side_output_full)
    result, final_pull = jax.vjp(finish, resid_two, side_out, norm_layer)
    output = product_nt(result.astype(BF16), to_far_team).astype(BF16).reshape(batch, block, width)

    d_resid_two, d_side_out, grad_norm_layer = final_pull(upstream)
    d_side_out_low = d_side_out.astype(BF16)
    d_side = product(d_side_out_low, side_output_full)
    d_side_pre, d_side_in = side_pull(d_side)
    d_side_pre_low = d_side_pre.astype(BF16)
    d_resid_two = d_resid_two + product_nt(d_side_pre_low, side_gate_full)
    d_resid_one, d_feed_out, grad_norm_after = after_pull(d_resid_two)

    d_out_low = d_feed_out.astype(BF16)
    side_spread = product(jnp.concatenate([resid_low, d_side_out_low], axis=0), to_spread).astype(BF16)
    side_sum = plan.spread_begin(
        [(side_spread[:rows], d_side_pre_low), (side_spread[rows:], side_low)]
    )
    d_gate_chunks = []
    d_up_chunks = []

    def backward_chunk(chunk):
        d_gate, d_up = pulls[len(d_gate_chunks)](product(chunk, down_full))
        d_gate_chunks.append(d_gate.astype(BF16))
        d_up_chunks.append(d_up.astype(BF16))
        part = product_nt(d_gate_chunks[-1], gate_full) + product_nt(d_up_chunks[-1], up_full)
        return part.astype(BF16)

    d_out_chunks, d_feed_parts = plan.team_map(d_out_low, backward_chunk)
    d_feed_sums = plan.core_sums(d_feed_parts)
    d_gate_chunks, d_up_chunks, feed_chunks, d_out_chunks, hidden_chunks, d_feed_sums = together(
        d_gate_chunks, d_up_chunks, feed_chunks, d_out_chunks, hidden_chunks, d_feed_sums
    )
    far_count = 2 ** len(plan.far)

    def far_terms(left, right):
        right = jnp.concatenate(right, axis=0)
        part = width // far_count
        return [
            product_tn(left[:, at * part : (at + 1) * part], right).astype(BF16)
            for at in range(far_count)
        ]

    feed_all = jnp.concatenate(feed_chunks, axis=0)
    gate_terms = far_terms(feed_all, d_gate_chunks)
    d_feed_sums = plan.team_near(d_feed_sums)
    d_feed_sums, d_up_chunks, feed_all, gate_terms = together(
        d_feed_sums, d_up_chunks, feed_all, gate_terms
    )
    up_terms = far_terms(feed_all, d_up_chunks)
    gate_terms = plan.fold(gate_terms, plan.far_dp)
    d_feed_in = plan.team_far(d_feed_sums)
    d_feed_in, up_terms, hidden_chunks, side_sum = together(
        d_feed_in, up_terms, hidden_chunks, side_sum
    )
    steps = tuple(reversed(plan.order))
    side_sum = plan.spread_step(side_sum, steps[:1])
    down_terms = far_terms(jnp.concatenate(d_out_chunks, axis=0), hidden_chunks)

    (
        d_inputs,
        d_normed,
        d_attn_proj,
        d_laurel,
        grad_norm_attn,
        grad_norm_laurel,
        grad_norm_before,
    ) = mid_pull((d_resid_one, d_feed_in))
    d_attn_low = d_attn_proj.astype(BF16)
    d_laurel_low = d_laurel.astype(BF16)
    d_attn_spread = product(d_attn_low, to_spread).astype(BF16)
    d_attended_low = product_split(d_attn_spread, output_full).astype(BF16)
    d_latent_low = product(d_laurel_low, right_full).astype(BF16)
    output_sum = plan.spread_begin([(d_attn_spread, attended_low)])
    d_attended_low, output_sum, gate_terms, up_terms, down_terms = together(
        d_attended_low, output_sum, gate_terms, up_terms, down_terms
    )
    output_sum = plan.spread_step(output_sum, steps[:1])
    gate_terms = plan.fold(gate_terms, plan.far_seq)
    up_terms = plan.fold(up_terms, plan.far_dp)

    d_att = d_attended_low.reshape(batch, block, kv_heads, group, head_size)
    d_values_all = jnp.einsum("bkgts,btkgd->bskd", probs_low, d_att, preferred_element_type=F32)
    d_probs = jnp.einsum("btkgd,bskd->bkgts", d_att, values_all, preferred_element_type=F32)
    d_scores = probs * (d_probs - jnp.sum(probs * d_probs, axis=-1, keepdims=True))
    d_scores_low = d_scores.astype(BF16)
    d_query_rot = jnp.einsum("bkgts,bskd->btkgd", d_scores_low, keys_all, preferred_element_type=F32)
    d_keys_all = jnp.einsum(
        "bkgts,btkgd->bskd", d_scores_low, query_group, preferred_element_type=F32
    )
    d_keys_all, d_values_all, d_query_rot, gate_terms, up_terms, down_terms, output_sum, side_sum = together(
        d_keys_all, d_values_all, d_query_rot, gate_terms, up_terms, down_terms, output_sum, side_sum
    )
    output_sum = jnp.concatenate([output_sum, side_sum], axis=1)
    up_terms = plan.fold(up_terms, plan.far_seq)
    down_terms = plan.fold(down_terms, plan.far_dp)
    if whole_sequence:
        d_pair_total = plan.near_sum(
            *[
                one.reshape(batch, seq_count, block, kv_heads, head_size).swapaxes(0, 1)
                for one in (d_keys_all, d_values_all)
            ]
        )
    else:
        d_pairs = jnp.stack([d_keys_all, d_values_all])
        d_pair_total = d_pairs[:, :, left_count * block : (left_count + 1) * block]
        for position, offset in enumerate(offsets):
            if offset != 0:
                piece = d_pairs[:, :, position * block : (position + 1) * block].astype(BF16)
                moved = passed_along(piece, plan.seq, seq_count, -offset)
                d_pair_total = d_pair_total + moved.astype(F32)
    d_queries, d_keys, d_values, grad_norm_query, grad_norm_key = prep_pull(
        (d_query_rot.reshape(batch, block, heads, head_size), d_pair_total[0], d_pair_total[1])
    )
    d_queries_low = d_queries.reshape(rows, -1).astype(BF16)
    query_sum = plan.spread_begin([(normed_spread, d_queries_low)])
    d_keys, d_values, query_sum, output_sum, up_terms, down_terms = together(
        d_keys, d_values, query_sum, output_sum, up_terms, down_terms
    )
    query_sum = plan.spread_step(query_sum, steps[:1])
    down_terms = plan.fold(down_terms, plan.far_seq)
    grad_gate, grad_up, grad_down = plan.own_rows(gate_terms + up_terms + down_terms, local_rows)
    d_kvl_low = jnp.concatenate(
        [
            d_keys.reshape(rows, -1).astype(BF16),
            d_values.reshape(rows, -1).astype(BF16),
            d_latent_low,
        ],
        axis=1,
    )
    laurel_spread = product(d_laurel_low, to_spread).astype(BF16)
    kvl_sum = plan.spread_begin([(normed_spread, d_kvl_low), (laurel_spread, latent_low)])
    d_spread = product_nt_split(d_queries_low, query_full) + product_nt_split(d_kvl_low, kvl_full)
    d_normed = d_normed + reorder(d_spread, to_spread)
    d_inputs_norm, grad_norm_input = pre_pull(d_normed)
    grad_tokens = reorder(d_inputs + d_inputs_norm, to_far_team).reshape(batch, block, width)
    grad_side = d_side_in.reshape(batch, block, -1)
    norm_grads = jnp.stack(
        [
            grad_norm_input,
            grad_norm_attn,
            grad_norm_laurel,
            grad_norm_before,
            grad_norm_after,
            grad_norm_layer,
        ]
    )
    gain_grads = jnp.concatenate(
        [plan.from_far_team(norm_grads).reshape(-1), grad_norm_query, grad_norm_key]
    )
    gain_grads, kvl_sum = together(gain_grads, kvl_sum)
    grad_query = plan.spread_step(query_sum, steps[1:])
    grad_output, grad_side_gate, grad_side_output = split_columns(
        plan.spread_step(output_sum, steps[1:]), rest_widths
    )
    grad_key, grad_value, grad_left, grad_right = split_columns(
        plan.spread_step(kvl_sum, steps), kvl_widths
    )
    gain_grads = plan.total(gain_grads)
    gain_parts = split_columns(gain_grads, [width] * 6 + [head_size] * 2)
    return (
        output,
        grad_tokens,
        grad_side,
        grad_query,
        grad_key,
        grad_value,
        grad_output,
        grad_left,
        grad_right,
        grad_gate,
        grad_up,
        grad_down,
        grad_side_gate,
        grad_side_output,
    ) + tuple(gain_parts)


def solution(mesh):
    seq_bits = int(math.log2(mesh.shape["seq"]))
    dp_bits = int(math.log2(mesh.shape["dp"]))
    plan = Plan(seq_bits, dp_bits)
    binary = Mesh(mesh.devices.reshape((2,) * (seq_bits + dp_bits)), plan.every)
    token_spec = P(plan.dp, plan.seq, None)
    weight_spec = P(plan.every, None)

    def step(*arrays):
        return body(plan, *arrays)

    return jax.shard_map(
        step,
        mesh=binary,
        in_specs=(token_spec, token_spec, P(plan.dp, plan.seq), P(plan.dp, None), token_spec)
        + (weight_spec,) * 11
        + (P(),) * 8,
        out_specs=(token_spec,) * 3 + (weight_spec,) * 11 + (P(),) * 8,
        check_vma=False,
    )
```

```python
import math

import jax
import jax.numpy as jnp
from jax import lax
from jax.sharding import Mesh
from jax.sharding import PartitionSpec as P

WINDOW = 512
SPAN = 256
EPS = 1e-06
HALF_ROOT = 1.0 / math.sqrt(2.0)
F32 = jnp.float32
BF16 = jnp.bfloat16


def rms(values, gain):
    return values * lax.rsqrt(jnp.mean(values * values, axis=-1, keepdims=True) + EPS) * gain


def gelu_tanh(values):
    return jax.nn.gelu(values, approximate=True)


def product(left, right):
    return jnp.dot(left, right, preferred_element_type=F32)


def product_nt(left, right):
    return lax.dot_general(left, right, (((1,), (1,)), ((), ())), preferred_element_type=F32)


def product_tn(left, right):
    return lax.dot_general(left, right, (((0,), (0,)), ((), ())), preferred_element_type=F32)


def rotate(values, places):
    size = values.shape[-1]
    half = size // 2
    freq = 10000.0 ** (-(2.0 * jnp.arange(half, dtype=F32)) / size)
    angle = places.astype(F32)[..., None] * freq
    cosine = jnp.cos(angle)[..., None, :]
    sine = jnp.sin(angle)[..., None, :]
    first = values[..., :half]
    second = values[..., half:]
    return jnp.concatenate(
        [first * cosine - second * sine, second * cosine + first * sine], axis=-1
    )


def middle(inputs, normed, attn_proj, laurel, gain_attn, gain_laurel, gain_before):
    resid = (inputs + rms(attn_proj, gain_attn) + normed + rms(laurel, gain_laurel)) * HALF_ROOT
    return (resid, rms(resid, gain_before))


def gate_act(gate_val, up_val):
    return gelu_tanh(gate_val) * up_val


def after_feed(resid_one, feed_out, gain_after):
    return resid_one + rms(feed_out, gain_after)


def side_act(side_pre, side_in):
    return gelu_tanh(side_pre) * side_in


def finish(resid_two, side_out, gain_layer):
    return resid_two + rms(side_out, gain_layer)


def swap(value, axis):
    return lax.ppermute(value, axis, [(0, 1), (1, 0)])


def together(*values):
    return lax.optimization_barrier(values)


def split_columns(whole, widths):
    pieces = []
    offset = 0
    for width_one in widths:
        pieces.append(whole[..., offset : offset + width_one])
        offset = offset + width_one
    return pieces


class Plan:
    def __init__(self, seq_bits, dp_bits):
        self.seq = tuple("s%d" % i for i in range(seq_bits))
        self.dp = tuple("d%d" % i for i in range(dp_bits))
        self.every = self.seq + self.dp
        self.l, self.x = self.seq[-2:]
        self.c = self.dp[-1]
        self.team = (self.l, self.x, self.c)
        self.far_seq = self.seq[:-2]
        self.far_dp = self.dp[:-1]
        self.far = self.far_seq + self.far_dp
        self.canon = self.far + self.team
        self.order = self.far_seq + (self.l,) + self.far_dp + (self.x,)

    def flipped(self, value, axes, dims):
        for axis, dim in zip(axes, dims):
            value = jnp.where(lax.axis_index(axis) == 1, jnp.flip(value, dim), value)
        return value

    def to_far_team(self, value):
        rows, width = value.shape
        parts = value.reshape((rows,) + (2,) * len(self.every) + (-1,))
        order = [0] + [1 + self.every.index(axis) for axis in self.canon] + [1 + len(self.every)]
        return parts.transpose(order).reshape(rows, width)

    def from_far_team(self, value):
        rows, width = value.shape
        parts = value.reshape((rows,) + (2,) * len(self.every) + (-1,))
        order = [0] + [1 + self.canon.index(axis) for axis in self.every] + [1 + len(self.every)]
        return parts.transpose(order).reshape(rows, width)

    def spread_order(self, width):
        own = jnp.arange(width, dtype=jnp.int32).reshape((2,) * len(self.canon) + (-1,))
        own = self.flipped(own, self.canon, range(len(self.canon)))
        axes = (self.c,) + tuple(reversed(self.order))
        return own.transpose([self.canon.index(axis) for axis in axes] + [len(self.canon)]).reshape(-1)

    def grow(self, block, axes):
        for axis in axes:
            block = jnp.concatenate([block, swap(block, axis)], axis=0)
        return block

    def gather_pieces(self, block):
        other = swap(block, self.order[-1])
        return [block, other, swap(block, self.c), swap(other, self.c)]

    def far_team_rows(self, pieces):
        axes = (self.c,) + tuple(reversed(self.order))
        whole = jnp.concatenate(pieces, axis=0)
        whole = whole.reshape((2,) * len(axes) + (-1, whole.shape[-1]))
        whole = whole.transpose([axes.index(axis) for axis in self.canon] + [len(axes), len(axes) + 1])
        whole = self.flipped(whole, self.canon, range(len(self.canon)))
        return whole.reshape((-1, whole.shape[-1]))

    def spread_begin(self, pairs):
        half = pairs[0][0].shape[1] // 2
        away = jnp.concatenate([product_tn(one[:, half:], two).astype(BF16) for one, two in pairs], axis=1)
        kept = jnp.concatenate([product_tn(one[:, :half], two).astype(BF16) for one, two in pairs], axis=1)
        return (kept.astype(F32) + swap(away, self.c).astype(F32)).astype(BF16)

    def spread_step(self, total, axes):
        for axis in axes:
            half = total.shape[0] // 2
            total = total[:half].astype(F32) + swap(total[half:], axis).astype(F32)
            if axis != self.order[0]:
                total = total.astype(BF16)
        return total

    def near_far(self, key, value):
        pair = jnp.stack([key, value])[:, None]
        for axis in reversed(self.far_seq):
            pair = jnp.concatenate([pair, swap(pair, axis)], axis=1)
        return pair

    def near_gather(self, pair):
        key, value = pair[0][None], pair[1][None]
        key = jnp.concatenate([key, swap(key, self.x)], axis=0)
        key = jnp.stack([key, swap(key, self.l)], axis=0)
        value = jnp.concatenate([value, swap(value, self.l)], axis=0)
        value = jnp.stack([value, swap(value, self.x)], axis=1)
        return [one.reshape((-1,) + one.shape[3:]) for one in (key, value)]

    def near_sum(self, key, value):
        def step(total, dim, axis):
            total = total.astype(BF16)
            away = swap(lax.index_in_dim(total, 1, dim, False), axis).astype(F32)
            return lax.index_in_dim(total, 0, dim, False).astype(F32) + away

        shape = (2, 2) + (2,) * len(self.far_seq)
        key, value = [one.reshape(shape + one.shape[1:]) for one in (key, value)]
        key = step(step(key, 0, self.l), 0, self.x)
        value = step(step(value, 1, self.x), 0, self.l)
        pair = jnp.stack([key, value])
        for axis in self.far_seq:
            pair = step(pair, 1, axis)
        return pair

    def near_places(self):
        place = jnp.zeros((1,), jnp.int32)
        for axis in (self.l, self.x) + self.far_seq:
            bit = lax.axis_index(axis)
            weight = 2 ** (len(self.seq) - 1 - self.seq.index(axis))
            place = (place[:, None] + weight * jnp.stack([bit, 1 - bit])[None, :]).reshape(-1)
        return place

    def own_rows(self, sums, local_rows):
        size = 2 ** len(self.team)
        sums = jnp.concatenate([one.reshape(size, local_rows, -1) for one in sums], axis=1)
        moved = lax.all_to_all(sums, self.team, split_axis=0, concat_axis=0, tiled=True)
        return [
            jnp.concatenate([moved[at, first : first + local_rows] for at in range(size)], axis=1).astype(F32)
            for first in range(0, moved.shape[1], local_rows)
        ]

    def total(self, value):
        for axis in reversed(self.every):
            value = value + swap(value, axis)
        return value

    def team_map(self, own, function):
        def chunk_of(piece):
            return jnp.concatenate([piece, swap(piece, self.c)], axis=0)

        by_x, by_l = swap(own, self.x), swap(own, self.l)
        chunks = [chunk_of(own)]
        results = [function(chunks[0])]
        by_x, by_l, results = together(by_x, by_l, results)
        half = own.shape[0] // 2
        both = jnp.concatenate([swap(by_x[:half], self.l), swap(by_l[half:], self.x)], axis=0)
        for piece in (by_x, by_l, both):
            chunks.append(chunk_of(piece))
            results.append(function(chunks[-1]))
        return chunks, results

    def core_sums(self, chunks):
        sums = []
        for chunk in chunks:
            rows = chunk.shape[0] // 2
            other = swap(chunk[rows:].astype(BF16), self.c)
            sums.append(chunk[:rows].astype(F32) + other.astype(F32))
        return sums

    def team_near(self, sums):
        own, by_x, by_l, both = sums
        half = own.shape[0] // 2
        both = both.astype(BF16)
        first = by_l[:half] + swap(both[:half], self.x).astype(F32)
        second = by_x[half:] + swap(both[half:], self.l).astype(F32)
        by_l = jnp.concatenate([first, by_l[half:]], axis=0).astype(BF16)
        by_x = jnp.concatenate([by_x[:half], second], axis=0).astype(BF16)
        return own, by_l, by_x

    def team_far(self, sums):
        own, by_l, by_x = sums
        return own + swap(by_l, self.l).astype(F32) + swap(by_x, self.x).astype(F32)


def product_split(left, pieces):
    width = left.shape[1] // len(pieces)
    return sum(product(left[:, i * width : (i + 1) * width], one) for i, one in enumerate(pieces))


def product_nt_split(left, pieces):
    return jnp.concatenate([product_nt(left, one) for one in pieces], axis=1)


def reorder(values, matrix):
    rows = values.shape[0]
    high = lax.reduce_precision(values, 8, 7)
    parts = jnp.concatenate([high.astype(BF16), (values - high).astype(BF16)], axis=0)
    parts = product_nt(parts, matrix)
    return parts[:rows] + parts[rows:]


def passed_along(value, axes, count, steps):
    initial, last = (max(0, -steps), min(count, count - steps))
    return lax.ppermute(value, axes, [(source, source + steps) for source in range(initial, last)])


def body(
    plan,
    tokens,
    per_layer,
    positions,
    span_start,
    cotangent,
    query_weight,
    key_weight,
    value_weight,
    output_weight,
    laurel_left,
    laurel_right,
    gate_weight,
    up_weight,
    down_weight,
    side_gate,
    side_output,
    norm_input,
    norm_attn,
    norm_laurel,
    norm_before,
    norm_after,
    norm_layer,
    norm_query,
    norm_key,
):
    batch, block, width = tokens.shape
    rows = batch * block
    head_size = norm_query.shape[0]
    heads = query_weight.shape[1] // head_size
    kv_heads = key_weight.shape[1] // head_size
    group = heads // kv_heads
    seq_count = 2 ** len(plan.seq)
    local_rows = gate_weight.shape[0]
    team_size = 2 ** len(plan.team)
    hidden_own = gate_weight.shape[1] // team_size

    kvl_widths = [
        key_weight.shape[1],
        value_weight.shape[1],
        laurel_left.shape[1],
        laurel_right.shape[1],
    ]
    rest_widths = [output_weight.shape[1], side_gate.shape[1], side_output.shape[1]]
    feed_local = jnp.concatenate(
        [
            one.reshape(local_rows, team_size, hidden_own).transpose(1, 0, 2)
            for one in (gate_weight, up_weight, down_weight)
        ],
        axis=1,
    )
    feed_team = lax.all_to_all(feed_local, plan.team, split_axis=0, concat_axis=0, tiled=True)
    feed_team = feed_team.reshape(team_size, 3, local_rows, hidden_own).transpose(1, 0, 2, 3)
    block_widths = [sum(kvl_widths), query_weight.shape[1], sum(rest_widths)]
    attn_block = jnp.concatenate(
        [key_weight, value_weight, laurel_left, laurel_right, query_weight]
        + [output_weight, side_gate, side_output],
        axis=1,
    )
    attn_block = plan.grow(attn_block, plan.far_seq)
    attn_block, feed_team = together(attn_block, feed_team)
    feed_full = lax.all_gather(feed_team.reshape(-1, hidden_own), plan.far, axis=0, tiled=True)
    attn_block = plan.grow(attn_block, (plan.l,))
    kvl_block, query_block, rest_block = split_columns(attn_block, block_widths)
    kvl_block = plan.grow(kvl_block, plan.far_dp)
    query_block = plan.grow(query_block, plan.far_dp)
    kvl_full = plan.gather_pieces(kvl_block)
    kvl_full, query_block, rest_block = together(kvl_full, query_block, rest_block)
    query_full = plan.gather_pieces(query_block)
    rest_block = plan.grow(rest_block, plan.far_dp)
    right_full = plan.far_team_rows([one[:, -kvl_widths[3] :] for one in kvl_full])
    kvl_full = [one[:, : -kvl_widths[3]] for one in kvl_full]

    places = jnp.arange(width, dtype=jnp.int32)
    far_team = plan.to_far_team(places[None])[0]
    to_far_team = (places[:, None] == far_team[None, :]).astype(BF16)
    to_spread = (places[:, None] == plan.spread_order(width)[None, :]).astype(BF16)
    gains = jnp.stack([norm_input, norm_attn, norm_laurel, norm_before, norm_after, norm_layer])
    norm_input, norm_attn, norm_laurel, norm_before, norm_after, norm_layer = plan.to_far_team(gains)
    inputs = product(tokens.reshape(rows, width), to_far_team)
    upstream = product(cotangent.reshape(rows, width), to_far_team)
    side_in = per_layer.astype(F32).reshape(rows, -1)
    normed, pre_pull = jax.vjp(rms, inputs, norm_input)
    normed_low = normed.astype(BF16)
    normed_spread = product(normed_low, to_spread).astype(BF16)
    keys, values, latent = split_columns(
        product_split(normed_spread, kvl_full), kvl_widths[:3]
    )
    queries = product_split(normed_spread, query_full).reshape(batch, block, heads, head_size)
    keys = keys.reshape(batch, block, kv_heads, head_size)
    values = values.reshape(batch, block, kv_heads, head_size)
    latent_low = latent.astype(BF16)

    def head_prep(query_in, key_in, value_in, gain_query, gain_key):
        return (
            rotate(rms(query_in, gain_query), positions),
            rotate(rms(key_in, gain_key), positions),
            rms(value_in, 1.0),
        )

    (rot_query, rot_key, rot_value), prep_pull = jax.vjp(
        head_prep, queries, keys, values, norm_query, norm_key
    )
    query_low = rot_query.astype(BF16)
    key_low = rot_key.astype(BF16)
    value_low = rot_value.astype(BF16)
    left_count = WINDOW // block
    right_count = (SPAN + block - 2) // block
    offsets = list(range(left_count, 0, -1)) + [0] + list(range(-1, -right_count - 1, -1))
    whole_sequence = seq_count <= len(offsets) + 1
    seq_index = lax.axis_index(plan.seq)
    total_length = block * seq_count
    if whole_sequence:
        pair_low = plan.near_far(key_low, value_low)
        keys_all, values_all = [
            one.swapaxes(0, 1).reshape(batch, total_length, kv_heads, head_size)
            for one in plan.near_gather(pair_low)
        ]
        key_blocks = plan.near_places()
    else:
        pair_low = jnp.stack([key_low, value_low])
        gathered = [
            passed_along(pair_low, plan.seq, seq_count, offset) if offset else pair_low
            for offset in offsets
        ]
        keys_all, values_all = jnp.concatenate(gathered, axis=2)
        key_blocks = seq_index - jnp.array(offsets, dtype=jnp.int32)
    key_count = keys_all.shape[1]
    keys_all, values_all, rest_block = together(keys_all, values_all, rest_block)
    rest_full = plan.gather_pieces(rest_block)
    query_places = seq_index * block + jnp.arange(block, dtype=jnp.int32)
    key_places = (key_blocks[:, None] * block + jnp.arange(block, dtype=jnp.int32)).reshape(-1)
    in_query = (query_places[None, :, None] >= span_start[:, None, :]) & (
        query_places[None, :, None] < span_start[:, None, :] + SPAN
    )
    in_key = (key_places[None, :, None] >= span_start[:, None, :]) & (
        key_places[None, :, None] < span_start[:, None, :] + SPAN
    )
    same = jnp.any(in_query[:, :, None, :] & in_key[:, None, :, :], axis=-1)
    near = (key_places[None, :] <= query_places[:, None]) & (
        query_places[:, None] - key_places[None, :] < WINDOW
    )
    valid = (key_places >= 0) & (key_places < total_length)
    allowed = (valid[None, None, :] & (near[None] | same))[:, None, None]
    query_group = query_low.reshape(batch, block, kv_heads, group, head_size)
    scores = jnp.einsum("btkgd,bskd->bkgts", query_group, keys_all, preferred_element_type=F32)
    masked = jnp.where(allowed, scores, -1e30)
    top = jnp.max(masked, axis=-1, keepdims=True)
    expo = jnp.exp(masked - top)
    total = jnp.sum(expo, axis=-1, keepdims=True)
    probs = expo / total
    probs_low = probs.astype(BF16)
    attended = jnp.einsum("bkgts,bskd->btkgd", probs_low, values_all, preferred_element_type=F32)
    attended_low = attended.reshape(rows, heads * head_size).astype(BF16)
    attended_low, feed_full = together(attended_low, feed_full)
    output_full = [one[:, : rest_widths[0]] for one in rest_full]
    side_full = plan.far_team_rows([one[:, rest_widths[0] :] for one in rest_full])
    side_gate_full, side_output_full = split_columns(side_full, rest_widths[1:])
    attn_proj = reorder(product_nt_split(attended_low, output_full), to_spread)
    laurel = product_nt(latent_low, right_full)
    (resid_one, feed_in), mid_pull = jax.vjp(
        middle, inputs, normed, attn_proj, laurel, norm_attn, norm_laurel, norm_before
    )

    feed_low = feed_in.astype(BF16)
    feed_full = feed_full.reshape(-1, 3, team_size * local_rows, hidden_own)
    gate_full, up_full, down_full = [feed_full[:, at].reshape(width, hidden_own) for at in range(3)]
    pulls = []
    hidden_chunks = []

    def forward_chunk(chunk):
        hidden, pull = jax.vjp(gate_act, product(chunk, gate_full), product(chunk, up_full))
        hidden_low = hidden.astype(BF16)
        pulls.append(pull)
        hidden_chunks.append(hidden_low)
        return product_nt(hidden_low, down_full).astype(BF16)

    feed_chunks, feed_parts = plan.team_map(feed_low, forward_chunk)
    feed_out = plan.team_far(plan.team_near(plan.core_sums(feed_parts)))

    resid_two, after_pull = jax.vjp(after_feed, resid_one, feed_out, norm_after)
    resid_low = resid_two.astype(BF16)
    side_pre = product(resid_low, side_gate_full)
    side_val, side_pull = jax.vjp(side_act, side_pre, side_in)
    side_low = side_val.astype(BF16)
    side_out = product_nt(side_low, side_output_full)
    result, final_pull = jax.vjp(finish, resid_two, side_out, norm_layer)
    output = product_nt(result.astype(BF16), to_far_team).astype(BF16).reshape(batch, block, width)

    d_resid_two, d_side_out, grad_norm_layer = final_pull(upstream)
    d_side_out_low = d_side_out.astype(BF16)
    d_side = product(d_side_out_low, side_output_full)
    d_side_pre, d_side_in = side_pull(d_side)
    d_side_pre_low = d_side_pre.astype(BF16)
    d_resid_two = d_resid_two + product_nt(d_side_pre_low, side_gate_full)
    d_resid_one, d_feed_out, grad_norm_after = after_pull(d_resid_two)

    d_out_low = d_feed_out.astype(BF16)
    side_spread = product(jnp.concatenate([resid_low, d_side_out_low], axis=0), to_spread).astype(BF16)
    side_sum = plan.spread_begin(
        [(side_spread[:rows], d_side_pre_low), (side_spread[rows:], side_low)]
    )
    d_gate_chunks = []
    d_up_chunks = []

    def backward_chunk(chunk):
        d_gate, d_up = pulls[len(d_gate_chunks)](product(chunk, down_full))
        d_gate_chunks.append(d_gate.astype(BF16))
        d_up_chunks.append(d_up.astype(BF16))
        part = product_nt(d_gate_chunks[-1], gate_full) + product_nt(d_up_chunks[-1], up_full)
        return part.astype(BF16)

    d_out_chunks, d_feed_parts = plan.team_map(d_out_low, backward_chunk)
    d_feed_sums = plan.core_sums(d_feed_parts)
    d_gate_chunks, d_up_chunks, feed_chunks, d_out_chunks, hidden_chunks, d_feed_sums = together(
        d_gate_chunks, d_up_chunks, feed_chunks, d_out_chunks, hidden_chunks, d_feed_sums
    )
    feed_all = jnp.concatenate(feed_chunks, axis=0)
    d_out_all = jnp.concatenate(d_out_chunks, axis=0)
    feed_terms = jnp.stack(
        [
            product_tn(left, jnp.concatenate(right, axis=0))
            .astype(BF16)
            .reshape(-1, team_size * local_rows, hidden_own)
            for left, right in (
                (feed_all, d_gate_chunks),
                (feed_all, d_up_chunks),
                (d_out_all, hidden_chunks),
            )
        ],
        axis=1,
    )
    d_feed_in = plan.team_far(plan.team_near(d_feed_sums))
    d_feed_in, feed_terms = together(d_feed_in, feed_terms)
    feed_sum = lax.psum_scatter(
        feed_terms.reshape(-1, hidden_own), plan.far, scatter_dimension=0, tiled=True
    )
    feed_sum = jnp.split(feed_sum, 3)
    steps = tuple(reversed(plan.order))
    side_sum = plan.spread_step(side_sum, steps[:1])

    (
        d_inputs,
        d_normed,
        d_attn_proj,
        d_laurel,
        grad_norm_attn,
        grad_norm_laurel,
        grad_norm_before,
    ) = mid_pull((d_resid_one, d_feed_in))
    d_attn_low = d_attn_proj.astype(BF16)
    d_laurel_low = d_laurel.astype(BF16)
    d_attn_spread = product(d_attn_low, to_spread).astype(BF16)
    d_attended_low = product_split(d_attn_spread, output_full).astype(BF16)
    d_latent_low = product(d_laurel_low, right_full).astype(BF16)
    output_sum = plan.spread_begin([(d_attn_spread, attended_low)])
    d_attended_low, output_sum = together(d_attended_low, output_sum)
    output_sum = plan.spread_step(output_sum, steps[:1])

    d_att = d_attended_low.reshape(batch, block, kv_heads, group, head_size)
    d_values_all = jnp.einsum("bkgts,btkgd->bskd", probs_low, d_att, preferred_element_type=F32)
    d_probs = jnp.einsum("btkgd,bskd->bkgts", d_att, values_all, preferred_element_type=F32)
    d_scores = probs * (d_probs - jnp.sum(probs * d_probs, axis=-1, keepdims=True))
    d_scores_low = d_scores.astype(BF16)
    d_query_rot = jnp.einsum("bkgts,bskd->btkgd", d_scores_low, keys_all, preferred_element_type=F32)
    d_keys_all = jnp.einsum(
        "bkgts,btkgd->bskd", d_scores_low, query_group, preferred_element_type=F32
    )
    d_keys_all, d_values_all, d_query_rot, output_sum, side_sum = together(
        d_keys_all, d_values_all, d_query_rot, output_sum, side_sum
    )
    output_sum = jnp.concatenate([output_sum, side_sum], axis=1)
    if whole_sequence:
        d_pair_total = plan.near_sum(
            *[
                one.reshape(batch, seq_count, block, kv_heads, head_size).swapaxes(0, 1)
                for one in (d_keys_all, d_values_all)
            ]
        )
    else:
        d_pairs = jnp.stack([d_keys_all, d_values_all])
        d_pair_total = d_pairs[:, :, left_count * block : (left_count + 1) * block]
        for position, offset in enumerate(offsets):
            if offset != 0:
                piece = d_pairs[:, :, position * block : (position + 1) * block].astype(BF16)
                moved = passed_along(piece, plan.seq, seq_count, -offset)
                d_pair_total = d_pair_total + moved.astype(F32)
    d_queries, d_keys, d_values, grad_norm_query, grad_norm_key = prep_pull(
        (d_query_rot.reshape(batch, block, heads, head_size), d_pair_total[0], d_pair_total[1])
    )
    d_queries_low = d_queries.reshape(rows, -1).astype(BF16)
    query_sum = plan.spread_begin([(normed_spread, d_queries_low)])
    query_sum = plan.spread_step(query_sum, steps[:1])
    d_keys, d_values, query_sum, output_sum = together(d_keys, d_values, query_sum, output_sum)
    grad_gate, grad_up, grad_down = plan.own_rows(feed_sum, local_rows)
    d_kvl_low = jnp.concatenate(
        [
            d_keys.reshape(rows, -1).astype(BF16),
            d_values.reshape(rows, -1).astype(BF16),
            d_latent_low,
        ],
        axis=1,
    )
    laurel_spread = product(d_laurel_low, to_spread).astype(BF16)
    kvl_sum = plan.spread_begin([(normed_spread, d_kvl_low), (laurel_spread, latent_low)])
    kvl_sum = plan.spread_step(kvl_sum, steps[:1])
    kvl_sum, d_queries_low, d_kvl_low = together(kvl_sum, d_queries_low, d_kvl_low)
    d_spread = product_nt_split(d_queries_low, query_full) + product_nt_split(d_kvl_low, kvl_full)
    d_normed = d_normed + reorder(d_spread, to_spread)
    d_inputs_norm, grad_norm_input = pre_pull(d_normed)
    grad_tokens = reorder(d_inputs + d_inputs_norm, to_far_team).reshape(batch, block, width)
    grad_side = d_side_in.reshape(batch, block, -1)
    norm_grads = jnp.stack(
        [
            grad_norm_input,
            grad_norm_attn,
            grad_norm_laurel,
            grad_norm_before,
            grad_norm_after,
            grad_norm_layer,
        ]
    )
    gain_grads = jnp.concatenate(
        [plan.from_far_team(norm_grads).reshape(-1), grad_norm_query, grad_norm_key]
    )
    gain_grads, kvl_sum = together(gain_grads, kvl_sum)
    grad_query = plan.spread_step(query_sum, steps[1:])
    grad_output, grad_side_gate, grad_side_output = split_columns(
        plan.spread_step(output_sum, steps[1:]), rest_widths
    )
    grad_key, grad_value, grad_left, grad_right = split_columns(
        plan.spread_step(kvl_sum, steps[1:]), kvl_widths
    )
    gain_grads = plan.total(gain_grads)
    gain_parts = split_columns(gain_grads, [width] * 6 + [head_size] * 2)
    return (
        output,
        grad_tokens,
        grad_side,
        grad_query,
        grad_key,
        grad_value,
        grad_output,
        grad_left,
        grad_right,
        grad_gate,
        grad_up,
        grad_down,
        grad_side_gate,
        grad_side_output,
    ) + tuple(gain_parts)


def solution(mesh):
    seq_bits = int(math.log2(mesh.shape["seq"]))
    dp_bits = int(math.log2(mesh.shape["dp"]))
    plan = Plan(seq_bits, dp_bits)
    binary = Mesh(mesh.devices.reshape((2,) * (seq_bits + dp_bits)), plan.every)
    token_spec = P(plan.dp, plan.seq, None)
    weight_spec = P(plan.every, None)

    def step(*arrays):
        return body(plan, *arrays)

    return jax.shard_map(
        step,
        mesh=binary,
        in_specs=(token_spec, token_spec, P(plan.dp, plan.seq), P(plan.dp, None), token_spec)
        + (weight_spec,) * 11
        + (P(),) * 8,
        out_specs=(token_spec,) * 3 + (weight_spec,) * 11 + (P(),) * 8,
        check_vma=False,
    )
```

```python
import math

import jax
import jax.numpy as jnp
from jax import lax
from jax.sharding import Mesh
from jax.sharding import PartitionSpec as P

WINDOW = 512
SPAN = 256
EPS = 1e-06
HALF_ROOT = 1.0 / math.sqrt(2.0)
F32 = jnp.float32
BF16 = jnp.bfloat16


def rms(values, gain):
    return values * lax.rsqrt(jnp.mean(values * values, axis=-1, keepdims=True) + EPS) * gain


def gelu_tanh(values):
    return jax.nn.gelu(values, approximate=True)


def product(left, right):
    return jnp.dot(left, right, preferred_element_type=F32)


def product_nt(left, right):
    return lax.dot_general(left, right, (((1,), (1,)), ((), ())), preferred_element_type=F32)


def product_tn(left, right):
    return lax.dot_general(left, right, (((0,), (0,)), ((), ())), preferred_element_type=F32)


def rotate(values, places):
    size = values.shape[-1]
    half = size // 2
    freq = 10000.0 ** (-(2.0 * jnp.arange(half, dtype=F32)) / size)
    angle = places.astype(F32)[..., None] * freq
    cosine = jnp.cos(angle)[..., None, :]
    sine = jnp.sin(angle)[..., None, :]
    first = values[..., :half]
    second = values[..., half:]
    return jnp.concatenate(
        [first * cosine - second * sine, second * cosine + first * sine], axis=-1
    )


def middle(inputs, normed, attn_proj, laurel, gain_attn, gain_laurel, gain_before):
    resid = (inputs + rms(attn_proj, gain_attn) + normed + rms(laurel, gain_laurel)) * HALF_ROOT
    return (resid, rms(resid, gain_before))


def gate_act(gate_val, up_val):
    return gelu_tanh(gate_val) * up_val


def after_feed(resid_one, feed_out, gain_after):
    return resid_one + rms(feed_out, gain_after)


def side_act(side_pre, side_in):
    return gelu_tanh(side_pre) * side_in


def finish(resid_two, side_out, gain_layer):
    return resid_two + rms(side_out, gain_layer)


def swap(value, axis):
    return lax.ppermute(value, axis, [(0, 1), (1, 0)])


def together(*values):
    return lax.optimization_barrier(values)


def split_columns(whole, widths):
    pieces = []
    offset = 0
    for width_one in widths:
        pieces.append(whole[..., offset : offset + width_one])
        offset = offset + width_one
    return pieces


class Plan:
    def __init__(self, seq_bits, dp_bits):
        self.seq = tuple("s%d" % i for i in range(seq_bits))
        self.dp = tuple("d%d" % i for i in range(dp_bits))
        self.every = self.seq + self.dp
        self.l, self.x = self.seq[-2:]
        self.c = self.dp[-1]
        self.team = (self.l, self.x, self.c)
        self.far_seq = self.seq[:-2]
        self.far_dp = self.dp[:-1]
        self.far = self.far_seq + self.far_dp
        self.canon = self.far + self.team
        self.order = self.far_seq + (self.l,) + self.far_dp + (self.x,)

    def flipped(self, value, axes, dims):
        for axis, dim in zip(axes, dims):
            value = jnp.where(lax.axis_index(axis) == 1, jnp.flip(value, dim), value)
        return value

    def to_far_team(self, value):
        rows, width = value.shape
        parts = value.reshape((rows,) + (2,) * len(self.every) + (-1,))
        order = [0] + [1 + self.every.index(axis) for axis in self.canon] + [1 + len(self.every)]
        return parts.transpose(order).reshape(rows, width)

    def from_far_team(self, value):
        rows, width = value.shape
        parts = value.reshape((rows,) + (2,) * len(self.every) + (-1,))
        order = [0] + [1 + self.canon.index(axis) for axis in self.every] + [1 + len(self.every)]
        return parts.transpose(order).reshape(rows, width)

    def spread_order(self, width):
        own = jnp.arange(width, dtype=jnp.int32).reshape((2,) * len(self.canon) + (-1,))
        own = self.flipped(own, self.canon, range(len(self.canon)))
        axes = (self.c,) + tuple(reversed(self.order))
        return own.transpose([self.canon.index(axis) for axis in axes] + [len(self.canon)]).reshape(-1)

    def grow(self, block, axes):
        for axis in axes:
            block = jnp.concatenate([block, swap(block, axis)], axis=0)
        return block

    def gather_pieces(self, block):
        other = swap(block, self.order[-1])
        return [block, other, swap(block, self.c), swap(other, self.c)]

    def far_team_rows(self, pieces):
        axes = (self.c,) + tuple(reversed(self.order))
        whole = jnp.concatenate(pieces, axis=0)
        whole = whole.reshape((2,) * len(axes) + (-1, whole.shape[-1]))
        whole = whole.transpose([axes.index(axis) for axis in self.canon] + [len(axes), len(axes) + 1])
        whole = self.flipped(whole, self.canon, range(len(self.canon)))
        return whole.reshape((-1, whole.shape[-1]))

    def spread_begin(self, pairs):
        half = pairs[0][0].shape[1] // 2
        away = jnp.concatenate([product_tn(one[:, half:], two).astype(BF16) for one, two in pairs], axis=1)
        kept = jnp.concatenate([product_tn(one[:, :half], two).astype(BF16) for one, two in pairs], axis=1)
        return (kept.astype(F32) + swap(away, self.c).astype(F32)).astype(BF16)

    def spread_step(self, total, axes):
        for axis in axes:
            half = total.shape[0] // 2
            total = total[:half].astype(F32) + swap(total[half:], axis).astype(F32)
            if axis != self.order[0]:
                total = total.astype(BF16)
        return total

    def spread_send(self, total, axis):
        half = total.shape[0] // 2
        return total[:half].astype(F32), swap(total[half:], axis).astype(F32)

    def near_far(self, key, value):
        pair = jnp.stack([key, value])[:, None]
        for axis in reversed(self.far_seq):
            pair = jnp.concatenate([pair, swap(pair, axis)], axis=1)
        return pair

    def near_gather(self, pair):
        key, value = pair[0][None], pair[1][None]
        key = jnp.concatenate([key, swap(key, self.x)], axis=0)
        key = jnp.stack([key, swap(key, self.l)], axis=0)
        value = jnp.concatenate([value, swap(value, self.l)], axis=0)
        value = jnp.stack([value, swap(value, self.x)], axis=1)
        return [one.reshape((-1,) + one.shape[3:]) for one in (key, value)]

    def near_sum(self, key, value):
        def step(total, dim, axis):
            total = total.astype(BF16)
            away = swap(lax.index_in_dim(total, 1, dim, False), axis).astype(F32)
            return lax.index_in_dim(total, 0, dim, False).astype(F32) + away

        shape = (2, 2) + (2,) * len(self.far_seq)
        key, value = [one.reshape(shape + one.shape[1:]) for one in (key, value)]
        key = step(step(key, 0, self.l), 0, self.x)
        value = step(step(value, 1, self.x), 0, self.l)
        pair = jnp.stack([key, value])
        for axis in self.far_seq:
            pair = step(pair, 1, axis)
        return pair

    def near_places(self):
        place = jnp.zeros((1,), jnp.int32)
        for axis in (self.l, self.x) + self.far_seq:
            bit = lax.axis_index(axis)
            weight = 2 ** (len(self.seq) - 1 - self.seq.index(axis))
            place = (place[:, None] + weight * jnp.stack([bit, 1 - bit])[None, :]).reshape(-1)
        return place

    def own_rows(self, sums, local_rows):
        size = 2 ** len(self.team)
        sums = jnp.concatenate([one.reshape(size, local_rows, -1) for one in sums], axis=1)
        moved = lax.all_to_all(sums, self.team, split_axis=0, concat_axis=0, tiled=True)
        return [
            jnp.concatenate([moved[at, first : first + local_rows] for at in range(size)], axis=1).astype(F32)
            for first in range(0, moved.shape[1], local_rows)
        ]

    def total(self, value):
        for axis in reversed(self.every):
            value = value + swap(value, axis)
        return value

    def team_map(self, own, function):
        def chunk_of(piece):
            return jnp.concatenate([piece, swap(piece, self.c)], axis=0)

        by_x, by_l = swap(own, self.x), swap(own, self.l)
        chunks = [chunk_of(own)]
        results = [function(chunks[0])]
        by_x, by_l, results = together(by_x, by_l, results)
        half = own.shape[0] // 2
        both = jnp.concatenate([swap(by_x[:half], self.l), swap(by_l[half:], self.x)], axis=0)
        for piece in (by_x, by_l, both):
            chunks.append(chunk_of(piece))
            results.append(function(chunks[-1]))
        return chunks, results

    def core_sums(self, chunks):
        sums = []
        for chunk in chunks:
            rows = chunk.shape[0] // 2
            other = swap(chunk[rows:].astype(BF16), self.c)
            sums.append(chunk[:rows].astype(F32) + other.astype(F32))
        return sums

    def team_near(self, sums):
        own, by_x, by_l, both = sums
        half = own.shape[0] // 2
        both = both.astype(BF16)
        first = by_l[:half] + swap(both[:half], self.x).astype(F32)
        second = by_x[half:] + swap(both[half:], self.l).astype(F32)
        by_l = jnp.concatenate([first, by_l[half:]], axis=0).astype(BF16)
        by_x = jnp.concatenate([by_x[:half], second], axis=0).astype(BF16)
        return own, by_l, by_x

    def team_far(self, sums):
        own, by_l, by_x = sums
        return own + swap(by_l, self.l).astype(F32) + swap(by_x, self.x).astype(F32)


def product_split(left, pieces):
    width = left.shape[1] // len(pieces)
    return sum(product(left[:, i * width : (i + 1) * width], one) for i, one in enumerate(pieces))


def product_nt_split(left, pieces):
    return jnp.concatenate([product_nt(left, one) for one in pieces], axis=1)


def reorder(values, matrix):
    rows = values.shape[0]
    high = lax.reduce_precision(values, 8, 7)
    parts = jnp.concatenate([high.astype(BF16), (values - high).astype(BF16)], axis=0)
    parts = product_nt(parts, matrix)
    return parts[:rows] + parts[rows:]


def passed_along(value, axes, count, steps):
    initial, last = (max(0, -steps), min(count, count - steps))
    return lax.ppermute(value, axes, [(source, source + steps) for source in range(initial, last)])


def body(
    plan,
    tokens,
    per_layer,
    positions,
    span_start,
    cotangent,
    query_weight,
    key_weight,
    value_weight,
    output_weight,
    laurel_left,
    laurel_right,
    gate_weight,
    up_weight,
    down_weight,
    side_gate,
    side_output,
    norm_input,
    norm_attn,
    norm_laurel,
    norm_before,
    norm_after,
    norm_layer,
    norm_query,
    norm_key,
):
    batch, block, width = tokens.shape
    rows = batch * block
    head_size = norm_query.shape[0]
    heads = query_weight.shape[1] // head_size
    kv_heads = key_weight.shape[1] // head_size
    group = heads // kv_heads
    seq_count = 2 ** len(plan.seq)
    local_rows = gate_weight.shape[0]
    team_size = 2 ** len(plan.team)
    hidden_own = gate_weight.shape[1] // team_size

    kvl_widths = [
        key_weight.shape[1],
        value_weight.shape[1],
        laurel_left.shape[1],
        laurel_right.shape[1],
    ]
    rest_widths = [output_weight.shape[1], side_gate.shape[1], side_output.shape[1]]
    feed_local = jnp.concatenate(
        [
            one.reshape(local_rows, team_size, hidden_own).transpose(1, 0, 2)
            for one in (gate_weight, up_weight, down_weight)
        ],
        axis=1,
    )
    feed_team = lax.all_to_all(feed_local, plan.team, split_axis=0, concat_axis=0, tiled=True)
    feed_team = feed_team.reshape(team_size, 3, local_rows, hidden_own).transpose(1, 0, 2, 3)
    block_widths = [sum(kvl_widths), query_weight.shape[1], sum(rest_widths)]
    attn_block = jnp.concatenate(
        [key_weight, value_weight, laurel_left, laurel_right, query_weight]
        + [output_weight, side_gate, side_output],
        axis=1,
    )
    attn_block = plan.grow(attn_block, plan.far_seq)
    attn_block, feed_team = together(attn_block, feed_team)
    feed_full = lax.all_gather(feed_team.reshape(-1, hidden_own), plan.far, axis=0, tiled=True)
    attn_block = plan.grow(attn_block, (plan.l,))
    kvl_block, query_block, rest_block = split_columns(attn_block, block_widths)
    kvl_block = plan.grow(kvl_block, plan.far_dp)
    query_block = plan.grow(query_block, plan.far_dp)
    kvl_full = plan.gather_pieces(kvl_block)
    kvl_full, rest_block = together(kvl_full, rest_block)
    query_full = plan.gather_pieces(query_block)
    rest_block = plan.grow(rest_block, plan.far_dp)
    right_full = plan.far_team_rows([one[:, -kvl_widths[3] :] for one in kvl_full])
    kvl_full = [one[:, : -kvl_widths[3]] for one in kvl_full]

    places = jnp.arange(width, dtype=jnp.int32)
    far_team = plan.to_far_team(places[None])[0]
    to_far_team = (places[:, None] == far_team[None, :]).astype(BF16)
    to_spread = (places[:, None] == plan.spread_order(width)[None, :]).astype(BF16)
    gains = jnp.stack([norm_input, norm_attn, norm_laurel, norm_before, norm_after, norm_layer])
    norm_input, norm_attn, norm_laurel, norm_before, norm_after, norm_layer = plan.to_far_team(gains)
    inputs = product(tokens.reshape(rows, width), to_far_team)
    upstream = product(cotangent.reshape(rows, width), to_far_team)
    side_in = per_layer.astype(F32).reshape(rows, -1)
    normed, pre_pull = jax.vjp(rms, inputs, norm_input)
    normed_low = normed.astype(BF16)
    normed_spread = product(normed_low, to_spread).astype(BF16)
    keys, values, latent = split_columns(
        product_split(normed_spread, kvl_full), kvl_widths[:3]
    )
    queries = product_split(normed_spread, query_full).reshape(batch, block, heads, head_size)
    keys = keys.reshape(batch, block, kv_heads, head_size)
    values = values.reshape(batch, block, kv_heads, head_size)
    latent_low = latent.astype(BF16)

    def head_prep(query_in, key_in, value_in, gain_query, gain_key):
        return (
            rotate(rms(query_in, gain_query), positions),
            rotate(rms(key_in, gain_key), positions),
            rms(value_in, 1.0),
        )

    (rot_query, rot_key, rot_value), prep_pull = jax.vjp(
        head_prep, queries, keys, values, norm_query, norm_key
    )
    query_low = rot_query.astype(BF16)
    key_low = rot_key.astype(BF16)
    value_low = rot_value.astype(BF16)
    left_count = WINDOW // block
    right_count = (SPAN + block - 2) // block
    offsets = list(range(left_count, 0, -1)) + [0] + list(range(-1, -right_count - 1, -1))
    whole_sequence = seq_count <= len(offsets) + 1
    seq_index = lax.axis_index(plan.seq)
    total_length = block * seq_count
    if whole_sequence:
        pair_low = plan.near_far(key_low, value_low)
        keys_all, values_all = [
            one.swapaxes(0, 1).reshape(batch, total_length, kv_heads, head_size)
            for one in plan.near_gather(pair_low)
        ]
        key_blocks = plan.near_places()
    else:
        pair_low = jnp.stack([key_low, value_low])
        gathered = [
            passed_along(pair_low, plan.seq, seq_count, offset) if offset else pair_low
            for offset in offsets
        ]
        keys_all, values_all = jnp.concatenate(gathered, axis=2)
        key_blocks = seq_index - jnp.array(offsets, dtype=jnp.int32)
    key_count = keys_all.shape[1]
    rest_full = plan.gather_pieces(rest_block)
    query_places = seq_index * block + jnp.arange(block, dtype=jnp.int32)
    key_places = (key_blocks[:, None] * block + jnp.arange(block, dtype=jnp.int32)).reshape(-1)
    in_query = (query_places[None, :, None] >= span_start[:, None, :]) & (
        query_places[None, :, None] < span_start[:, None, :] + SPAN
    )
    in_key = (key_places[None, :, None] >= span_start[:, None, :]) & (
        key_places[None, :, None] < span_start[:, None, :] + SPAN
    )
    same = jnp.any(in_query[:, :, None, :] & in_key[:, None, :, :], axis=-1)
    near = (key_places[None, :] <= query_places[:, None]) & (
        query_places[:, None] - key_places[None, :] < WINDOW
    )
    valid = (key_places >= 0) & (key_places < total_length)
    allowed = (valid[None, None, :] & (near[None] | same))[:, None, None]
    query_group = query_low.reshape(batch, block, kv_heads, group, head_size)
    scores = jnp.einsum("btkgd,bskd->bkgts", query_group, keys_all, preferred_element_type=F32)
    masked = jnp.where(allowed, scores, -1e30)
    top = jnp.max(masked, axis=-1, keepdims=True)
    expo = jnp.exp(masked - top)
    total = jnp.sum(expo, axis=-1, keepdims=True)
    probs = expo / total
    probs_low = probs.astype(BF16)
    attended = jnp.einsum("bkgts,bskd->btkgd", probs_low, values_all, preferred_element_type=F32)
    attended_low = attended.reshape(rows, heads * head_size).astype(BF16)
    attended_low, feed_full = together(attended_low, feed_full)
    output_full = [one[:, : rest_widths[0]] for one in rest_full]
    side_full = plan.far_team_rows([one[:, rest_widths[0] :] for one in rest_full])
    side_gate_full, side_output_full = split_columns(side_full, rest_widths[1:])
    attn_proj = reorder(product_nt_split(attended_low, output_full), to_spread)
    laurel = product_nt(latent_low, right_full)
    (resid_one, feed_in), mid_pull = jax.vjp(
        middle, inputs, normed, attn_proj, laurel, norm_attn, norm_laurel, norm_before
    )

    feed_low = feed_in.astype(BF16)
    feed_full = feed_full.reshape(-1, 3, team_size * local_rows, hidden_own)
    gate_full, up_full, down_full = [feed_full[:, at].reshape(width, hidden_own) for at in range(3)]
    pulls = []
    hidden_chunks = []

    def forward_chunk(chunk):
        hidden, pull = jax.vjp(gate_act, product(chunk, gate_full), product(chunk, up_full))
        hidden_low = hidden.astype(BF16)
        pulls.append(pull)
        hidden_chunks.append(hidden_low)
        return product_nt(hidden_low, down_full).astype(BF16)

    feed_chunks, feed_parts = plan.team_map(feed_low, forward_chunk)
    feed_out = plan.team_far(plan.team_near(plan.core_sums(feed_parts)))

    resid_two, after_pull = jax.vjp(after_feed, resid_one, feed_out, norm_after)
    resid_low = resid_two.astype(BF16)
    side_pre = product(resid_low, side_gate_full)
    side_val, side_pull = jax.vjp(side_act, side_pre, side_in)
    side_low = side_val.astype(BF16)
    side_out = product_nt(side_low, side_output_full)
    result, final_pull = jax.vjp(finish, resid_two, side_out, norm_layer)
    output = product_nt(result.astype(BF16), to_far_team).astype(BF16).reshape(batch, block, width)

    d_resid_two, d_side_out, grad_norm_layer = final_pull(upstream)
    d_side_out_low = d_side_out.astype(BF16)
    d_side = product(d_side_out_low, side_output_full)
    d_side_pre, d_side_in = side_pull(d_side)
    d_side_pre_low = d_side_pre.astype(BF16)
    d_resid_two = d_resid_two + product_nt(d_side_pre_low, side_gate_full)
    d_resid_one, d_feed_out, grad_norm_after = after_pull(d_resid_two)

    d_out_low = d_feed_out.astype(BF16)
    side_spread = product(jnp.concatenate([resid_low, d_side_out_low], axis=0), to_spread).astype(BF16)
    side_sum = plan.spread_begin(
        [(side_spread[:rows], d_side_pre_low), (side_spread[rows:], side_low)]
    )
    d_gate_chunks = []
    d_up_chunks = []

    def backward_chunk(chunk):
        d_gate, d_up = pulls[len(d_gate_chunks)](product(chunk, down_full))
        d_gate_chunks.append(d_gate.astype(BF16))
        d_up_chunks.append(d_up.astype(BF16))
        part = product_nt(d_gate_chunks[-1], gate_full) + product_nt(d_up_chunks[-1], up_full)
        return part.astype(BF16)

    d_out_chunks, d_feed_parts = plan.team_map(d_out_low, backward_chunk)
    d_feed_sums = plan.core_sums(d_feed_parts)
    d_gate_chunks, d_up_chunks, feed_chunks, d_out_chunks, hidden_chunks, d_feed_sums = together(
        d_gate_chunks, d_up_chunks, feed_chunks, d_out_chunks, hidden_chunks, d_feed_sums
    )
    feed_all = jnp.concatenate(feed_chunks, axis=0)
    d_out_all = jnp.concatenate(d_out_chunks, axis=0)
    feed_terms = jnp.stack(
        [
            product_tn(left, jnp.concatenate(right, axis=0))
            .astype(BF16)
            .reshape(-1, team_size * local_rows, hidden_own)
            for left, right in (
                (feed_all, d_gate_chunks),
                (feed_all, d_up_chunks),
                (d_out_all, hidden_chunks),
            )
        ],
        axis=1,
    )
    d_feed_in = plan.team_far(plan.team_near(d_feed_sums))
    d_feed_in, feed_terms = together(d_feed_in, feed_terms)
    feed_sum = lax.psum_scatter(
        feed_terms.reshape(-1, hidden_own), plan.far, scatter_dimension=0, tiled=True
    )
    steps = tuple(reversed(plan.order))
    side_sum = plan.spread_step(side_sum, steps[:1])

    (
        d_inputs,
        d_normed,
        d_attn_proj,
        d_laurel,
        grad_norm_attn,
        grad_norm_laurel,
        grad_norm_before,
    ) = mid_pull((d_resid_one, d_feed_in))
    d_attn_low = d_attn_proj.astype(BF16)
    d_laurel_low = d_laurel.astype(BF16)
    d_attn_spread = product(d_attn_low, to_spread).astype(BF16)
    d_attended_low = product_split(d_attn_spread, output_full).astype(BF16)
    d_latent_low = product(d_laurel_low, right_full).astype(BF16)
    output_sum = plan.spread_begin([(d_attn_spread, attended_low)])
    d_attended_low, output_sum = together(d_attended_low, output_sum)
    output_sum = plan.spread_step(output_sum, steps[:1])

    d_att = d_attended_low.reshape(batch, block, kv_heads, group, head_size)
    d_values_all = jnp.einsum("bkgts,btkgd->bskd", probs_low, d_att, preferred_element_type=F32)
    d_probs = jnp.einsum("btkgd,bskd->bkgts", d_att, values_all, preferred_element_type=F32)
    d_scores = probs * (d_probs - jnp.sum(probs * d_probs, axis=-1, keepdims=True))
    d_scores_low = d_scores.astype(BF16)
    d_query_rot = jnp.einsum("bkgts,bskd->btkgd", d_scores_low, keys_all, preferred_element_type=F32)
    d_keys_all = jnp.einsum(
        "bkgts,btkgd->bskd", d_scores_low, query_group, preferred_element_type=F32
    )
    d_keys_all, d_values_all, d_query_rot, output_sum, side_sum = together(
        d_keys_all, d_values_all, d_query_rot, output_sum, side_sum
    )
    output_sum = jnp.concatenate([output_sum, side_sum], axis=1)
    if whole_sequence:
        d_pair_total = plan.near_sum(
            *[
                one.reshape(batch, seq_count, block, kv_heads, head_size).swapaxes(0, 1)
                for one in (d_keys_all, d_values_all)
            ]
        )
    else:
        d_pairs = jnp.stack([d_keys_all, d_values_all])
        d_pair_total = d_pairs[:, :, left_count * block : (left_count + 1) * block]
        for position, offset in enumerate(offsets):
            if offset != 0:
                piece = d_pairs[:, :, position * block : (position + 1) * block].astype(BF16)
                moved = passed_along(piece, plan.seq, seq_count, -offset)
                d_pair_total = d_pair_total + moved.astype(F32)
    d_queries, d_keys, d_values, grad_norm_query, grad_norm_key = prep_pull(
        (d_query_rot.reshape(batch, block, heads, head_size), d_pair_total[0], d_pair_total[1])
    )
    d_queries_low = d_queries.reshape(rows, -1).astype(BF16)
    query_sum = plan.spread_begin([(normed_spread, d_queries_low)])
    query_sum = plan.spread_step(query_sum, steps[:1])
    d_keys, d_values, query_sum, output_sum, feed_sum = together(
        d_keys, d_values, query_sum, output_sum, feed_sum
    )
    grad_gate, grad_up, grad_down = plan.own_rows(jnp.split(feed_sum, 3), local_rows)
    d_kvl_low = jnp.concatenate(
        [
            d_keys.reshape(rows, -1).astype(BF16),
            d_values.reshape(rows, -1).astype(BF16),
            d_latent_low,
        ],
        axis=1,
    )
    laurel_spread = product(d_laurel_low, to_spread).astype(BF16)
    kvl_sum = plan.spread_begin([(normed_spread, d_kvl_low), (laurel_spread, latent_low)])
    query_kept, query_away = plan.spread_send(query_sum, steps[1])
    output_kept, output_away = plan.spread_send(output_sum, steps[1])
    kvl_sum = plan.spread_step(kvl_sum, steps[:1])
    kvl_sum, query_kept, output_kept = together(kvl_sum, query_kept, output_kept)
    query_sum = (query_kept + query_away).astype(BF16)
    output_sum = (output_kept + output_away).astype(BF16)
    kvl_sum, d_queries_low, d_kvl_low = together(kvl_sum, d_queries_low, d_kvl_low)
    d_spread = product_nt_split(d_queries_low, query_full) + product_nt_split(d_kvl_low, kvl_full)
    d_normed = d_normed + reorder(d_spread, to_spread)
    d_inputs_norm, grad_norm_input = pre_pull(d_normed)
    grad_tokens = reorder(d_inputs + d_inputs_norm, to_far_team).reshape(batch, block, width)
    grad_side = d_side_in.reshape(batch, block, -1)
    norm_grads = jnp.stack(
        [
            grad_norm_input,
            grad_norm_attn,
            grad_norm_laurel,
            grad_norm_before,
            grad_norm_after,
            grad_norm_layer,
        ]
    )
    gain_grads = jnp.concatenate(
        [plan.from_far_team(norm_grads).reshape(-1), grad_norm_query, grad_norm_key]
    )
    gain_grads, kvl_sum = together(gain_grads, kvl_sum)
    grad_query = plan.spread_step(query_sum, steps[2:])
    grad_output, grad_side_gate, grad_side_output = split_columns(
        plan.spread_step(output_sum, steps[2:]), rest_widths
    )
    grad_key, grad_value, grad_left, grad_right = split_columns(
        plan.spread_step(kvl_sum, steps[1:]), kvl_widths
    )
    gain_grads = plan.total(gain_grads)
    gain_parts = split_columns(gain_grads, [width] * 6 + [head_size] * 2)
    return (
        output,
        grad_tokens,
        grad_side,
        grad_query,
        grad_key,
        grad_value,
        grad_output,
        grad_left,
        grad_right,
        grad_gate,
        grad_up,
        grad_down,
        grad_side_gate,
        grad_side_output,
    ) + tuple(gain_parts)


def solution(mesh):
    seq_bits = int(math.log2(mesh.shape["seq"]))
    dp_bits = int(math.log2(mesh.shape["dp"]))
    plan = Plan(seq_bits, dp_bits)
    binary = Mesh(mesh.devices.reshape((2,) * (seq_bits + dp_bits)), plan.every)
    token_spec = P(plan.dp, plan.seq, None)
    weight_spec = P(plan.every, None)

    def step(*arrays):
        return body(plan, *arrays)

    return jax.shard_map(
        step,
        mesh=binary,
        in_specs=(token_spec, token_spec, P(plan.dp, plan.seq), P(plan.dp, None), token_spec)
        + (weight_spec,) * 11
        + (P(),) * 8,
        out_specs=(token_spec,) * 3 + (weight_spec,) * 11 + (P(),) * 8,
        check_vma=False,
    )
```

```python
import math

import jax
import jax.numpy as jnp
from jax import lax
from jax.sharding import Mesh
from jax.sharding import PartitionSpec as P

WINDOW = 512
SPAN = 256
EPS = 1e-06
HALF_ROOT = 1.0 / math.sqrt(2.0)
F32 = jnp.float32
BF16 = jnp.bfloat16


def rms(values, gain):
    return values * lax.rsqrt(jnp.mean(values * values, axis=-1, keepdims=True) + EPS) * gain


def gelu_tanh(values):
    return jax.nn.gelu(values, approximate=True)


def product(left, right):
    return jnp.dot(left, right, preferred_element_type=F32)


def product_nt(left, right):
    return lax.dot_general(left, right, (((1,), (1,)), ((), ())), preferred_element_type=F32)


def product_tn(left, right):
    return lax.dot_general(left, right, (((0,), (0,)), ((), ())), preferred_element_type=F32)


def rotate(values, places):
    size = values.shape[-1]
    half = size // 2
    freq = 10000.0 ** (-(2.0 * jnp.arange(half, dtype=F32)) / size)
    angle = places.astype(F32)[..., None] * freq
    cosine = jnp.cos(angle)[..., None, :]
    sine = jnp.sin(angle)[..., None, :]
    first = values[..., :half]
    second = values[..., half:]
    return jnp.concatenate(
        [first * cosine - second * sine, second * cosine + first * sine], axis=-1
    )


def middle(inputs, normed, attn_proj, laurel, gain_attn, gain_laurel, gain_before):
    resid = (inputs + rms(attn_proj, gain_attn) + normed + rms(laurel, gain_laurel)) * HALF_ROOT
    return (resid, rms(resid, gain_before))


def gate_act(gate_val, up_val):
    return gelu_tanh(gate_val) * up_val


def after_feed(resid_one, feed_out, gain_after):
    return resid_one + rms(feed_out, gain_after)


def side_act(side_pre, side_in):
    return gelu_tanh(side_pre) * side_in


def finish(resid_two, side_out, gain_layer):
    return resid_two + rms(side_out, gain_layer)


def swap(value, axis):
    return lax.ppermute(value, axis, [(0, 1), (1, 0)])


def together(*values):
    return lax.optimization_barrier(values)


def split_columns(whole, widths):
    pieces = []
    offset = 0
    for width_one in widths:
        pieces.append(whole[..., offset : offset + width_one])
        offset = offset + width_one
    return pieces


class Plan:
    def __init__(self, seq_bits, dp_bits):
        self.seq = tuple("s%d" % i for i in range(seq_bits))
        self.dp = tuple("d%d" % i for i in range(dp_bits))
        self.every = self.seq + self.dp
        self.l, self.x = self.seq[-2:]
        self.c = self.dp[-1]
        self.team = (self.l, self.x, self.c)
        self.far_seq = self.seq[:-2]
        self.far_dp = self.dp[:-1]
        self.far = self.far_seq + self.far_dp
        self.canon = self.far + self.team
        self.order = self.far_seq + (self.l,) + self.far_dp + (self.x,)

    def flipped(self, value, axes, dims):
        for axis, dim in zip(axes, dims):
            value = jnp.where(lax.axis_index(axis) == 1, jnp.flip(value, dim), value)
        return value

    def to_far_team(self, value):
        rows, width = value.shape
        parts = value.reshape((rows,) + (2,) * len(self.every) + (-1,))
        order = [0] + [1 + self.every.index(axis) for axis in self.canon] + [1 + len(self.every)]
        return parts.transpose(order).reshape(rows, width)

    def from_far_team(self, value):
        rows, width = value.shape
        parts = value.reshape((rows,) + (2,) * len(self.every) + (-1,))
        order = [0] + [1 + self.canon.index(axis) for axis in self.every] + [1 + len(self.every)]
        return parts.transpose(order).reshape(rows, width)

    def spread_order(self, width):
        own = jnp.arange(width, dtype=jnp.int32).reshape((2,) * len(self.canon) + (-1,))
        own = self.flipped(own, self.canon, range(len(self.canon)))
        axes = (self.c,) + tuple(reversed(self.order))
        return own.transpose([self.canon.index(axis) for axis in axes] + [len(self.canon)]).reshape(-1)

    def grow(self, block, axes):
        for axis in axes:
            block = jnp.concatenate([block, swap(block, axis)], axis=0)
        return block

    def gather_pieces(self, block):
        other = swap(block, self.order[-1])
        return [block, other, swap(block, self.c), swap(other, self.c)]

    def far_team_rows(self, pieces):
        axes = (self.c,) + tuple(reversed(self.order))
        whole = jnp.concatenate(pieces, axis=0)
        whole = whole.reshape((2,) * len(axes) + (-1, whole.shape[-1]))
        whole = whole.transpose([axes.index(axis) for axis in self.canon] + [len(axes), len(axes) + 1])
        whole = self.flipped(whole, self.canon, range(len(self.canon)))
        return whole.reshape((-1, whole.shape[-1]))

    def spread_begin(self, pairs):
        half = pairs[0][0].shape[1] // 2
        away = jnp.concatenate([product_tn(one[:, half:], two).astype(BF16) for one, two in pairs], axis=1)
        kept = jnp.concatenate([product_tn(one[:, :half], two).astype(BF16) for one, two in pairs], axis=1)
        return (kept.astype(F32) + swap(away, self.c).astype(F32)).astype(BF16)

    def spread_step(self, total, axes):
        for axis in axes:
            half = total.shape[0] // 2
            total = total[:half].astype(F32) + swap(total[half:], axis).astype(F32)
            if axis != self.order[0]:
                total = total.astype(BF16)
        return total

    def spread_send(self, total, axis):
        half = total.shape[0] // 2
        return total[:half].astype(F32), swap(total[half:], axis).astype(F32)

    def near_far(self, key, value):
        pair = jnp.stack([key, value])[:, None]
        for axis in reversed(self.far_seq):
            pair = jnp.concatenate([pair, swap(pair, axis)], axis=1)
        return pair

    def near_gather(self, pair):
        key, value = pair[0][None], pair[1][None]
        key = jnp.concatenate([key, swap(key, self.x)], axis=0)
        key = jnp.stack([key, swap(key, self.l)], axis=0)
        value = jnp.concatenate([value, swap(value, self.l)], axis=0)
        value = jnp.stack([value, swap(value, self.x)], axis=1)
        return [one.reshape((-1,) + one.shape[3:]) for one in (key, value)]

    def near_sum(self, key, value):
        def step(total, dim, axis):
            total = total.astype(BF16)
            away = swap(lax.index_in_dim(total, 1, dim, False), axis).astype(F32)
            return lax.index_in_dim(total, 0, dim, False).astype(F32) + away

        shape = (2, 2) + (2,) * len(self.far_seq)
        key, value = [one.reshape(shape + one.shape[1:]) for one in (key, value)]
        key = step(step(key, 0, self.l), 0, self.x)
        value = step(step(value, 1, self.x), 0, self.l)
        pair = jnp.stack([key, value])
        for axis in self.far_seq:
            pair = step(pair, 1, axis)
        return pair

    def near_places(self):
        place = jnp.zeros((1,), jnp.int32)
        for axis in (self.l, self.x) + self.far_seq:
            bit = lax.axis_index(axis)
            weight = 2 ** (len(self.seq) - 1 - self.seq.index(axis))
            place = (place[:, None] + weight * jnp.stack([bit, 1 - bit])[None, :]).reshape(-1)
        return place

    def own_rows(self, sums, local_rows):
        size = 2 ** len(self.team)
        sums = jnp.concatenate([one.reshape(size, local_rows, -1) for one in sums], axis=1)
        moved = lax.all_to_all(sums, self.team, split_axis=0, concat_axis=0, tiled=True)
        return [
            jnp.concatenate([moved[at, first : first + local_rows] for at in range(size)], axis=1).astype(F32)
            for first in range(0, moved.shape[1], local_rows)
        ]

    def total(self, value):
        for axis in reversed(self.every):
            value = value + swap(value, axis)
        return value

    def team_map(self, own, function):
        def chunk_of(piece):
            return jnp.concatenate([piece, swap(piece, self.c)], axis=0)

        by_x, by_l = swap(own, self.x), swap(own, self.l)
        chunks = [chunk_of(own)]
        results = [function(chunks[0])]
        by_x, by_l, results = together(by_x, by_l, results)
        half = own.shape[0] // 2
        both = jnp.concatenate([swap(by_x[:half], self.l), swap(by_l[half:], self.x)], axis=0)
        for piece in (by_x, both):
            chunks.append(chunk_of(piece))
            results.append(function(chunks[-1]))
        by_l, results = together(by_l, results)
        chunks.append(chunk_of(by_l))
        results.append(function(chunks[-1]))
        return chunks, results

    def core_sums(self, chunks):
        sums = []
        for chunk in chunks:
            rows = chunk.shape[0] // 2
            other = swap(chunk[rows:].astype(BF16), self.c)
            sums.append(chunk[:rows].astype(F32) + other.astype(F32))
        return sums

    def team_near(self, sums):
        own, by_x, both, by_l = sums
        half = own.shape[0] // 2
        both = both.astype(BF16)
        first = by_l[:half] + swap(both[:half], self.x).astype(F32)
        second = by_x[half:] + swap(both[half:], self.l).astype(F32)
        by_l = jnp.concatenate([first, by_l[half:]], axis=0).astype(BF16)
        by_x = jnp.concatenate([by_x[:half], second], axis=0).astype(BF16)
        return own, by_l, by_x

    def team_far(self, sums):
        own, by_l, by_x = sums
        return own + swap(by_l, self.l).astype(F32) + swap(by_x, self.x).astype(F32)


def product_split(left, pieces):
    width = left.shape[1] // len(pieces)
    return sum(product(left[:, i * width : (i + 1) * width], one) for i, one in enumerate(pieces))


def product_nt_split(left, pieces):
    return jnp.concatenate([product_nt(left, one) for one in pieces], axis=1)


def reorder(values, matrix):
    rows = values.shape[0]
    high = lax.reduce_precision(values, 8, 7)
    parts = jnp.concatenate([high.astype(BF16), (values - high).astype(BF16)], axis=0)
    parts = product_nt(parts, matrix)
    return parts[:rows] + parts[rows:]


def passed_along(value, axes, count, steps):
    initial, last = (max(0, -steps), min(count, count - steps))
    return lax.ppermute(value, axes, [(source, source + steps) for source in range(initial, last)])


def body(
    plan,
    tokens,
    per_layer,
    positions,
    span_start,
    cotangent,
    query_weight,
    key_weight,
    value_weight,
    output_weight,
    laurel_left,
    laurel_right,
    gate_weight,
    up_weight,
    down_weight,
    side_gate,
    side_output,
    norm_input,
    norm_attn,
    norm_laurel,
    norm_before,
    norm_after,
    norm_layer,
    norm_query,
    norm_key,
):
    batch, block, width = tokens.shape
    rows = batch * block
    head_size = norm_query.shape[0]
    heads = query_weight.shape[1] // head_size
    kv_heads = key_weight.shape[1] // head_size
    group = heads // kv_heads
    seq_count = 2 ** len(plan.seq)
    local_rows = gate_weight.shape[0]
    team_size = 2 ** len(plan.team)
    hidden_own = gate_weight.shape[1] // team_size

    kvl_widths = [
        key_weight.shape[1],
        value_weight.shape[1],
        laurel_left.shape[1],
        laurel_right.shape[1],
    ]
    rest_widths = [output_weight.shape[1], side_gate.shape[1], side_output.shape[1]]
    feed_local = jnp.concatenate(
        [
            one.reshape(local_rows, team_size, hidden_own).transpose(1, 0, 2)
            for one in (gate_weight, up_weight, down_weight)
        ],
        axis=1,
    )
    feed_team = lax.all_to_all(feed_local, plan.team, split_axis=0, concat_axis=0, tiled=True)
    feed_team = feed_team.reshape(team_size, 3, local_rows, hidden_own).transpose(1, 0, 2, 3)
    block_widths = [sum(kvl_widths), query_weight.shape[1], sum(rest_widths)]
    attn_block = jnp.concatenate(
        [key_weight, value_weight, laurel_left, laurel_right, query_weight]
        + [output_weight, side_gate, side_output],
        axis=1,
    )
    attn_block = plan.grow(attn_block, plan.far_seq)
    attn_block = plan.grow(attn_block, (plan.l,))
    attn_block, feed_team = together(attn_block, feed_team)
    feed_full = lax.all_gather(feed_team.reshape(-1, hidden_own), plan.far, axis=0, tiled=True)
    kvl_block, query_block, rest_block = split_columns(attn_block, block_widths)
    kvl_block = plan.grow(kvl_block, plan.far_dp)
    query_block = plan.grow(query_block, plan.far_dp)
    kvl_full = plan.gather_pieces(kvl_block)
    kvl_full, rest_block = together(kvl_full, rest_block)
    query_full = plan.gather_pieces(query_block)
    rest_block = plan.grow(rest_block, plan.far_dp)
    right_full = plan.far_team_rows([one[:, -kvl_widths[3] :] for one in kvl_full])
    kvl_full = [one[:, : -kvl_widths[3]] for one in kvl_full]

    places = jnp.arange(width, dtype=jnp.int32)
    far_team = plan.to_far_team(places[None])[0]
    to_far_team = (places[:, None] == far_team[None, :]).astype(BF16)
    to_spread = (places[:, None] == plan.spread_order(width)[None, :]).astype(BF16)
    gains = jnp.stack([norm_input, norm_attn, norm_laurel, norm_before, norm_after, norm_layer])
    norm_input, norm_attn, norm_laurel, norm_before, norm_after, norm_layer = plan.to_far_team(gains)
    inputs = product(tokens.reshape(rows, width), to_far_team)
    upstream = product(cotangent.reshape(rows, width), to_far_team)
    side_in = per_layer.astype(F32).reshape(rows, -1)
    normed, pre_pull = jax.vjp(rms, inputs, norm_input)
    normed_low = normed.astype(BF16)
    normed_spread = product(normed_low, to_spread).astype(BF16)
    keys, values, latent = split_columns(
        product_split(normed_spread, kvl_full), kvl_widths[:3]
    )
    queries = product_split(normed_spread, query_full).reshape(batch, block, heads, head_size)
    keys = keys.reshape(batch, block, kv_heads, head_size)
    values = values.reshape(batch, block, kv_heads, head_size)
    latent_low = latent.astype(BF16)

    def head_prep(query_in, key_in, value_in, gain_query, gain_key):
        return (
            rotate(rms(query_in, gain_query), positions),
            rotate(rms(key_in, gain_key), positions),
            rms(value_in, 1.0),
        )

    (rot_query, rot_key, rot_value), prep_pull = jax.vjp(
        head_prep, queries, keys, values, norm_query, norm_key
    )
    query_low = rot_query.astype(BF16)
    key_low = rot_key.astype(BF16)
    value_low = rot_value.astype(BF16)
    left_count = WINDOW // block
    right_count = (SPAN + block - 2) // block
    offsets = list(range(left_count, 0, -1)) + [0] + list(range(-1, -right_count - 1, -1))
    whole_sequence = seq_count <= len(offsets) + 1
    seq_index = lax.axis_index(plan.seq)
    total_length = block * seq_count
    if whole_sequence:
        pair_low = plan.near_far(key_low, value_low)
        keys_all, values_all = [
            one.swapaxes(0, 1).reshape(batch, total_length, kv_heads, head_size)
            for one in plan.near_gather(pair_low)
        ]
        key_blocks = plan.near_places()
    else:
        pair_low = jnp.stack([key_low, value_low])
        gathered = [
            passed_along(pair_low, plan.seq, seq_count, offset) if offset else pair_low
            for offset in offsets
        ]
        keys_all, values_all = jnp.concatenate(gathered, axis=2)
        key_blocks = seq_index - jnp.array(offsets, dtype=jnp.int32)
    key_count = keys_all.shape[1]
    rest_full = plan.gather_pieces(rest_block)
    query_places = seq_index * block + jnp.arange(block, dtype=jnp.int32)
    key_places = (key_blocks[:, None] * block + jnp.arange(block, dtype=jnp.int32)).reshape(-1)
    in_query = (query_places[None, :, None] >= span_start[:, None, :]) & (
        query_places[None, :, None] < span_start[:, None, :] + SPAN
    )
    in_key = (key_places[None, :, None] >= span_start[:, None, :]) & (
        key_places[None, :, None] < span_start[:, None, :] + SPAN
    )
    same = jnp.any(in_query[:, :, None, :] & in_key[:, None, :, :], axis=-1)
    near = (key_places[None, :] <= query_places[:, None]) & (
        query_places[:, None] - key_places[None, :] < WINDOW
    )
    valid = (key_places >= 0) & (key_places < total_length)
    allowed = (valid[None, None, :] & (near[None] | same))[:, None, None]
    query_group = query_low.reshape(batch, block, kv_heads, group, head_size)
    scores = jnp.einsum("btkgd,bskd->bkgts", query_group, keys_all, preferred_element_type=F32)
    masked = jnp.where(allowed, scores, -1e30)
    top = jnp.max(masked, axis=-1, keepdims=True)
    expo = jnp.exp(masked - top)
    total = jnp.sum(expo, axis=-1, keepdims=True)
    probs = expo / total
    probs_low = probs.astype(BF16)
    attended = jnp.einsum("bkgts,bskd->btkgd", probs_low, values_all, preferred_element_type=F32)
    attended_low = attended.reshape(rows, heads * head_size).astype(BF16)
    attended_low, feed_full = together(attended_low, feed_full)
    output_full = [one[:, : rest_widths[0]] for one in rest_full]
    side_full = plan.far_team_rows([one[:, rest_widths[0] :] for one in rest_full])
    side_gate_full, side_output_full = split_columns(side_full, rest_widths[1:])
    attn_proj = reorder(product_nt_split(attended_low, output_full), to_spread)
    laurel = product_nt(latent_low, right_full)
    (resid_one, feed_in), mid_pull = jax.vjp(
        middle, inputs, normed, attn_proj, laurel, norm_attn, norm_laurel, norm_before
    )

    feed_low = feed_in.astype(BF16)
    feed_full = feed_full.reshape(-1, 3, team_size * local_rows, hidden_own)
    gate_full, up_full, down_full = [feed_full[:, at].reshape(width, hidden_own) for at in range(3)]
    pulls = []
    hidden_chunks = []

    def forward_chunk(chunk):
        hidden, pull = jax.vjp(gate_act, product(chunk, gate_full), product(chunk, up_full))
        hidden_low = hidden.astype(BF16)
        pulls.append(pull)
        hidden_chunks.append(hidden_low)
        return product_nt(hidden_low, down_full).astype(BF16)

    feed_chunks, feed_parts = plan.team_map(feed_low, forward_chunk)
    feed_out = plan.team_far(plan.team_near(plan.core_sums(feed_parts)))

    resid_two, after_pull = jax.vjp(after_feed, resid_one, feed_out, norm_after)
    resid_low = resid_two.astype(BF16)
    side_pre = product(resid_low, side_gate_full)
    side_val, side_pull = jax.vjp(side_act, side_pre, side_in)
    side_low = side_val.astype(BF16)
    side_out = product_nt(side_low, side_output_full)
    result, final_pull = jax.vjp(finish, resid_two, side_out, norm_layer)
    output = product_nt(result.astype(BF16), to_far_team).astype(BF16).reshape(batch, block, width)

    d_resid_two, d_side_out, grad_norm_layer = final_pull(upstream)
    d_side_out_low = d_side_out.astype(BF16)
    d_side = product(d_side_out_low, side_output_full)
    d_side_pre, d_side_in = side_pull(d_side)
    d_side_pre_low = d_side_pre.astype(BF16)
    d_resid_two = d_resid_two + product_nt(d_side_pre_low, side_gate_full)
    d_resid_one, d_feed_out, grad_norm_after = after_pull(d_resid_two)

    d_out_low = d_feed_out.astype(BF16)
    d_gate_chunks = []
    d_up_chunks = []

    def backward_chunk(chunk):
        d_gate, d_up = pulls[len(d_gate_chunks)](product(chunk, down_full))
        d_gate_chunks.append(d_gate.astype(BF16))
        d_up_chunks.append(d_up.astype(BF16))
        part = product_nt(d_gate_chunks[-1], gate_full) + product_nt(d_up_chunks[-1], up_full)
        return part.astype(BF16)

    d_out_chunks, d_feed_parts = plan.team_map(d_out_low, backward_chunk)
    d_feed_sums = plan.core_sums(d_feed_parts)
    d_gate_chunks, d_up_chunks, feed_chunks, d_out_chunks, hidden_chunks, d_feed_sums = together(
        d_gate_chunks, d_up_chunks, feed_chunks, d_out_chunks, hidden_chunks, d_feed_sums
    )
    feed_all = jnp.concatenate(feed_chunks, axis=0)
    d_out_all = jnp.concatenate(d_out_chunks, axis=0)
    feed_terms = jnp.stack(
        [
            product_tn(left, jnp.concatenate(right, axis=0))
            .astype(BF16)
            .reshape(-1, team_size * local_rows, hidden_own)
            for left, right in (
                (feed_all, d_gate_chunks),
                (feed_all, d_up_chunks),
                (d_out_all, hidden_chunks),
            )
        ],
        axis=1,
    )
    d_feed_in = plan.team_far(plan.team_near(d_feed_sums))
    d_feed_in, feed_terms = together(d_feed_in, feed_terms)
    feed_sum = lax.psum_scatter(
        feed_terms.reshape(-1, hidden_own), plan.far, scatter_dimension=0, tiled=True
    )
    steps = tuple(reversed(plan.order))

    (
        d_inputs,
        d_normed,
        d_attn_proj,
        d_laurel,
        grad_norm_attn,
        grad_norm_laurel,
        grad_norm_before,
    ) = mid_pull((d_resid_one, d_feed_in))
    d_attn_low = d_attn_proj.astype(BF16)
    d_laurel_low = d_laurel.astype(BF16)
    d_attn_spread = product(d_attn_low, to_spread).astype(BF16)
    d_attended_low = product_split(d_attn_spread, output_full).astype(BF16)
    d_latent_low = product(d_laurel_low, right_full).astype(BF16)
    output_sum = plan.spread_begin([(d_attn_spread, attended_low)])
    d_attended_low, output_sum = together(d_attended_low, output_sum)
    output_sum = plan.spread_step(output_sum, steps[:1])

    d_att = d_attended_low.reshape(batch, block, kv_heads, group, head_size)
    d_values_all = jnp.einsum("bkgts,btkgd->bskd", probs_low, d_att, preferred_element_type=F32)
    d_probs = jnp.einsum("btkgd,bskd->bkgts", d_att, values_all, preferred_element_type=F32)
    d_scores = probs * (d_probs - jnp.sum(probs * d_probs, axis=-1, keepdims=True))
    d_scores_low = d_scores.astype(BF16)
    d_query_rot = jnp.einsum("bkgts,bskd->btkgd", d_scores_low, keys_all, preferred_element_type=F32)
    d_keys_all = jnp.einsum(
        "bkgts,btkgd->bskd", d_scores_low, query_group, preferred_element_type=F32
    )
    d_keys_all, d_values_all, d_query_rot, output_sum, side_left = together(
        d_keys_all,
        d_values_all,
        d_query_rot,
        output_sum,
        jnp.concatenate([resid_low, d_side_out_low], axis=0),
    )
    side_left = product(side_left, to_spread).astype(BF16)
    side_sum = plan.spread_begin([(side_left[:rows], d_side_pre_low), (side_left[rows:], side_low)])
    side_sum = plan.spread_step(side_sum, steps[:1])
    if whole_sequence:
        d_pair_total = plan.near_sum(
            *[
                one.reshape(batch, seq_count, block, kv_heads, head_size).swapaxes(0, 1)
                for one in (d_keys_all, d_values_all)
            ]
        )
    else:
        d_pairs = jnp.stack([d_keys_all, d_values_all])
        d_pair_total = d_pairs[:, :, left_count * block : (left_count + 1) * block]
        for position, offset in enumerate(offsets):
            if offset != 0:
                piece = d_pairs[:, :, position * block : (position + 1) * block].astype(BF16)
                moved = passed_along(piece, plan.seq, seq_count, -offset)
                d_pair_total = d_pair_total + moved.astype(F32)
    d_queries, d_keys, d_values, grad_norm_query, grad_norm_key = prep_pull(
        (d_query_rot.reshape(batch, block, heads, head_size), d_pair_total[0], d_pair_total[1])
    )
    d_queries_low = d_queries.reshape(rows, -1).astype(BF16)
    query_sum = plan.spread_begin([(normed_spread, d_queries_low)])
    query_sum = plan.spread_step(query_sum, steps[:1])
    d_spread = product_nt_split(d_queries_low, query_full)
    d_keys, d_values, query_sum, output_sum, side_sum, d_spread, feed_sum = together(
        d_keys, d_values, query_sum, output_sum, side_sum, d_spread, feed_sum
    )
    output_sum = jnp.concatenate([output_sum, side_sum], axis=1)
    grad_gate, grad_up, grad_down = plan.own_rows(jnp.split(feed_sum, 3), local_rows)
    d_kvl_low = jnp.concatenate(
        [
            d_keys.reshape(rows, -1).astype(BF16),
            d_values.reshape(rows, -1).astype(BF16),
            d_latent_low,
        ],
        axis=1,
    )
    laurel_spread = product(d_laurel_low, to_spread).astype(BF16)
    kvl_sum = plan.spread_begin([(normed_spread, d_kvl_low), (laurel_spread, latent_low)])
    query_kept, query_away = plan.spread_send(query_sum, steps[1])
    output_kept, output_away = plan.spread_send(output_sum, steps[1])
    kvl_sum = plan.spread_step(kvl_sum, steps[:1])
    kvl_sum, query_kept, output_kept = together(kvl_sum, query_kept, output_kept)
    query_sum = (query_kept + query_away).astype(BF16)
    output_sum = (output_kept + output_away).astype(BF16)
    kvl_sum = plan.spread_step(kvl_sum, steps[1:2])
    query_sum = plan.spread_step(query_sum, steps[2:3])
    output_sum = plan.spread_step(output_sum, steps[2:3])
    kvl_sum, query_sum, output_sum, d_kvl_low = together(kvl_sum, query_sum, output_sum, d_kvl_low)
    d_spread = d_spread + product_nt_split(d_kvl_low, kvl_full)
    d_normed = d_normed + reorder(d_spread, to_spread)
    d_inputs_norm, grad_norm_input = pre_pull(d_normed)
    grad_tokens = reorder(d_inputs + d_inputs_norm, to_far_team).reshape(batch, block, width)
    grad_side = d_side_in.reshape(batch, block, -1)
    norm_grads = jnp.stack(
        [
            grad_norm_input,
            grad_norm_attn,
            grad_norm_laurel,
            grad_norm_before,
            grad_norm_after,
            grad_norm_layer,
        ]
    )
    gain_grads = jnp.concatenate(
        [plan.from_far_team(norm_grads).reshape(-1), grad_norm_query, grad_norm_key]
    )
    grad_query = plan.spread_step(query_sum, steps[3:])
    grad_output, grad_side_gate, grad_side_output = split_columns(
        plan.spread_step(output_sum, steps[3:]), rest_widths
    )
    grad_key, grad_value, grad_left, grad_right = split_columns(
        plan.spread_step(kvl_sum, steps[2:]), kvl_widths
    )
    gain_grads = plan.total(gain_grads)
    gain_parts = split_columns(gain_grads, [width] * 6 + [head_size] * 2)
    return (
        output,
        grad_tokens,
        grad_side,
        grad_query,
        grad_key,
        grad_value,
        grad_output,
        grad_left,
        grad_right,
        grad_gate,
        grad_up,
        grad_down,
        grad_side_gate,
        grad_side_output,
    ) + tuple(gain_parts)


def solution(mesh):
    seq_bits = int(math.log2(mesh.shape["seq"]))
    dp_bits = int(math.log2(mesh.shape["dp"]))
    plan = Plan(seq_bits, dp_bits)
    binary = Mesh(mesh.devices.reshape((2,) * (seq_bits + dp_bits)), plan.every)
    token_spec = P(plan.dp, plan.seq, None)
    weight_spec = P(plan.every, None)

    def step(*arrays):
        return body(plan, *arrays)

    return jax.shard_map(
        step,
        mesh=binary,
        in_specs=(token_spec, token_spec, P(plan.dp, plan.seq), P(plan.dp, None), token_spec)
        + (weight_spec,) * 11
        + (P(),) * 8,
        out_specs=(token_spec,) * 3 + (weight_spec,) * 11 + (P(),) * 8,
        check_vma=False,
    )
```

```python
import math

import jax
import jax.numpy as jnp
from jax import lax
from jax.sharding import Mesh
from jax.sharding import PartitionSpec as P

WINDOW = 512
SPAN = 256
EPS = 1e-06
HALF_ROOT = 1.0 / math.sqrt(2.0)
F32 = jnp.float32
BF16 = jnp.bfloat16


def rms(values, gain):
    return values * lax.rsqrt(jnp.mean(values * values, axis=-1, keepdims=True) + EPS) * gain


def gelu_tanh(values):
    return jax.nn.gelu(values, approximate=True)


def product(left, right):
    return jnp.dot(left, right, preferred_element_type=F32)


def product_nt(left, right):
    return lax.dot_general(left, right, (((1,), (1,)), ((), ())), preferred_element_type=F32)


def product_tn(left, right):
    return lax.dot_general(left, right, (((0,), (0,)), ((), ())), preferred_element_type=F32)


def rotate(values, places):
    size = values.shape[-1]
    half = size // 2
    freq = 10000.0 ** (-(2.0 * jnp.arange(half, dtype=F32)) / size)
    angle = places.astype(F32)[..., None] * freq
    cosine = jnp.cos(angle)[..., None, :]
    sine = jnp.sin(angle)[..., None, :]
    first = values[..., :half]
    second = values[..., half:]
    return jnp.concatenate(
        [first * cosine - second * sine, second * cosine + first * sine], axis=-1
    )


def middle(inputs, normed, attn_proj, laurel, gain_attn, gain_laurel, gain_before):
    resid = (inputs + rms(attn_proj, gain_attn) + normed + rms(laurel, gain_laurel)) * HALF_ROOT
    return (resid, rms(resid, gain_before))


def gate_act(gate_val, up_val):
    return gelu_tanh(gate_val) * up_val


def after_feed(resid_one, feed_out, gain_after):
    return resid_one + rms(feed_out, gain_after)


def side_act(side_pre, side_in):
    return gelu_tanh(side_pre) * side_in


def finish(resid_two, side_out, gain_layer):
    return resid_two + rms(side_out, gain_layer)


def swap(value, axis):
    return lax.ppermute(value, axis, [(0, 1), (1, 0)])


def together(*values):
    return lax.optimization_barrier(values)


def split_columns(whole, widths):
    pieces = []
    offset = 0
    for width_one in widths:
        pieces.append(whole[..., offset : offset + width_one])
        offset = offset + width_one
    return pieces


class Plan:
    def __init__(self, seq_bits, dp_bits):
        self.seq = tuple("s%d" % i for i in range(seq_bits))
        self.dp = tuple("d%d" % i for i in range(dp_bits))
        self.every = self.seq + self.dp
        self.l, self.x = self.seq[-2:]
        self.c = self.dp[-1]
        self.team = (self.l, self.x, self.c)
        self.far_seq = self.seq[:-2]
        self.far_dp = self.dp[:-1]
        self.far = self.far_seq + self.far_dp
        self.canon = self.far + self.team
        self.order = self.far_seq + (self.l,) + self.far_dp + (self.x,)

    def flipped(self, value, axes, dims):
        for axis, dim in zip(axes, dims):
            value = jnp.where(lax.axis_index(axis) == 1, jnp.flip(value, dim), value)
        return value

    def to_far_team(self, value):
        rows, width = value.shape
        parts = value.reshape((rows,) + (2,) * len(self.every) + (-1,))
        order = [0] + [1 + self.every.index(axis) for axis in self.canon] + [1 + len(self.every)]
        return parts.transpose(order).reshape(rows, width)

    def from_far_team(self, value):
        rows, width = value.shape
        parts = value.reshape((rows,) + (2,) * len(self.every) + (-1,))
        order = [0] + [1 + self.canon.index(axis) for axis in self.every] + [1 + len(self.every)]
        return parts.transpose(order).reshape(rows, width)

    def spread_order(self, width):
        own = jnp.arange(width, dtype=jnp.int32).reshape((2,) * len(self.canon) + (-1,))
        own = self.flipped(own, self.canon, range(len(self.canon)))
        axes = (self.c,) + tuple(reversed(self.order))
        return own.transpose([self.canon.index(axis) for axis in axes] + [len(self.canon)]).reshape(-1)

    def grow(self, block, axes):
        for axis in axes:
            block = jnp.concatenate([block, swap(block, axis)], axis=0)
        return block

    def gather_pieces(self, block):
        return self.core_pieces(block, swap(block, self.order[-1]))

    def core_pieces(self, block, other):
        return [block, other, swap(block, self.c), swap(other, self.c)]

    def far_team_rows(self, pieces):
        axes = (self.c,) + tuple(reversed(self.order))
        whole = jnp.concatenate(pieces, axis=0)
        whole = whole.reshape((2,) * len(axes) + (-1, whole.shape[-1]))
        whole = whole.transpose([axes.index(axis) for axis in self.canon] + [len(axes), len(axes) + 1])
        whole = self.flipped(whole, self.canon, range(len(self.canon)))
        return whole.reshape((-1, whole.shape[-1]))

    def spread_begin(self, pairs):
        half = pairs[0][0].shape[1] // 2
        away = jnp.concatenate([product_tn(one[:, half:], two).astype(BF16) for one, two in pairs], axis=1)
        kept = jnp.concatenate([product_tn(one[:, :half], two).astype(BF16) for one, two in pairs], axis=1)
        return (kept.astype(F32) + swap(away, self.c).astype(F32)).astype(BF16)

    def spread_step(self, total, axes):
        for axis in axes:
            half = total.shape[0] // 2
            total = total[:half].astype(F32) + swap(total[half:], axis).astype(F32)
            if axis != self.order[0]:
                total = total.astype(BF16)
        return total

    def spread_send(self, total, axis):
        half = total.shape[0] // 2
        return total[:half].astype(F32), swap(total[half:], axis).astype(F32)

    def near_far(self, key, value):
        pair = jnp.stack([key, value])[:, None]
        for axis in reversed(self.far_seq):
            pair = jnp.concatenate([pair, swap(pair, axis)], axis=1)
        return pair

    def near_gather(self, pair):
        key, value = pair[0][None], pair[1][None]
        key = jnp.concatenate([key, swap(key, self.x)], axis=0)
        key = jnp.stack([key, swap(key, self.l)], axis=0)
        value = jnp.concatenate([value, swap(value, self.l)], axis=0)
        value = jnp.stack([value, swap(value, self.x)], axis=1)
        return [one.reshape((-1,) + one.shape[3:]) for one in (key, value)]

    def near_sum(self, key, value):
        def step(total, dim, axis):
            total = total.astype(BF16)
            away = swap(lax.index_in_dim(total, 1, dim, False), axis).astype(F32)
            return lax.index_in_dim(total, 0, dim, False).astype(F32) + away

        shape = (2, 2) + (2,) * len(self.far_seq)
        key, value = [one.reshape(shape + one.shape[1:]) for one in (key, value)]
        key = step(step(key, 0, self.l), 0, self.x)
        value = step(step(value, 1, self.x), 0, self.l)
        pair = jnp.stack([key, value])
        for axis in self.far_seq:
            pair = step(pair, 1, axis)
        return pair

    def near_places(self):
        place = jnp.zeros((1,), jnp.int32)
        for axis in (self.l, self.x) + self.far_seq:
            bit = lax.axis_index(axis)
            weight = 2 ** (len(self.seq) - 1 - self.seq.index(axis))
            place = (place[:, None] + weight * jnp.stack([bit, 1 - bit])[None, :]).reshape(-1)
        return place

    def own_rows(self, sums, local_rows):
        size = 2 ** len(self.team)
        sums = jnp.concatenate([one.reshape(size, local_rows, -1) for one in sums], axis=1)
        moved = lax.all_to_all(sums, self.team, split_axis=0, concat_axis=0, tiled=True)
        return [
            jnp.concatenate([moved[at, first : first + local_rows] for at in range(size)], axis=1).astype(F32)
            for first in range(0, moved.shape[1], local_rows)
        ]

    def total(self, value):
        for axis in reversed(self.every):
            value = value + swap(value, axis)
        return value

    def team_map(self, own, function):
        def chunk_of(piece):
            return jnp.concatenate([piece, swap(piece, self.c)], axis=0)

        by_x, by_l = swap(own, self.x), swap(own, self.l)
        chunks = [chunk_of(own)]
        results = [function(chunks[0])]
        by_x, by_l, results = together(by_x, by_l, results)
        half = own.shape[0] // 2
        both = jnp.concatenate([swap(by_x[:half], self.l), swap(by_l[half:], self.x)], axis=0)
        for piece in (by_x, by_l, both):
            chunks.append(chunk_of(piece))
            results.append(function(chunks[-1]))
        return chunks, results

    def core_sums(self, chunks):
        sums = []
        for chunk in chunks:
            rows = chunk.shape[0] // 2
            other = swap(chunk[rows:].astype(BF16), self.c)
            sums.append(chunk[:rows].astype(F32) + other.astype(F32))
        return sums

    def team_near(self, sums):
        own, by_x, by_l, both = sums
        half = own.shape[0] // 2
        both = both.astype(BF16)
        first = by_l[:half] + swap(both[:half], self.x).astype(F32)
        second = by_x[half:] + swap(both[half:], self.l).astype(F32)
        by_l = jnp.concatenate([first, by_l[half:]], axis=0).astype(BF16)
        by_x = jnp.concatenate([by_x[:half], second], axis=0).astype(BF16)
        return own, by_l, by_x

    def team_far(self, sums):
        own, by_l, by_x = sums
        return own + swap(by_l, self.l).astype(F32) + swap(by_x, self.x).astype(F32)


def product_split(left, pieces):
    width = left.shape[1] // len(pieces)
    return sum(product(left[:, i * width : (i + 1) * width], one) for i, one in enumerate(pieces))


def product_nt_split(left, pieces):
    return jnp.concatenate([product_nt(left, one) for one in pieces], axis=1)


def reorder(values, matrix):
    rows = values.shape[0]
    high = lax.reduce_precision(values, 8, 7)
    parts = jnp.concatenate([high.astype(BF16), (values - high).astype(BF16)], axis=0)
    parts = product_nt(parts, matrix)
    return parts[:rows] + parts[rows:]


def passed_along(value, axes, count, steps):
    initial, last = (max(0, -steps), min(count, count - steps))
    return lax.ppermute(value, axes, [(source, source + steps) for source in range(initial, last)])


def body(
    plan,
    tokens,
    per_layer,
    positions,
    span_start,
    cotangent,
    query_weight,
    key_weight,
    value_weight,
    output_weight,
    laurel_left,
    laurel_right,
    gate_weight,
    up_weight,
    down_weight,
    side_gate,
    side_output,
    norm_input,
    norm_attn,
    norm_laurel,
    norm_before,
    norm_after,
    norm_layer,
    norm_query,
    norm_key,
):
    batch, block, width = tokens.shape
    rows = batch * block
    head_size = norm_query.shape[0]
    heads = query_weight.shape[1] // head_size
    kv_heads = key_weight.shape[1] // head_size
    group = heads // kv_heads
    seq_count = 2 ** len(plan.seq)
    local_rows = gate_weight.shape[0]
    team_size = 2 ** len(plan.team)
    hidden_own = gate_weight.shape[1] // team_size

    kvl_widths = [
        key_weight.shape[1],
        value_weight.shape[1],
        laurel_left.shape[1],
        laurel_right.shape[1],
    ]
    rest_widths = [output_weight.shape[1], side_gate.shape[1], side_output.shape[1]]
    feed_local = jnp.concatenate(
        [
            one.reshape(local_rows, team_size, hidden_own).transpose(1, 0, 2)
            for one in (gate_weight, up_weight, down_weight)
        ],
        axis=1,
    )
    feed_team = lax.all_to_all(feed_local, plan.team, split_axis=0, concat_axis=0, tiled=True)
    feed_team = feed_team.reshape(team_size, 3, local_rows, hidden_own).transpose(1, 0, 2, 3)
    block_widths = [sum(kvl_widths), query_weight.shape[1], sum(rest_widths)]
    attn_block = jnp.concatenate(
        [key_weight, value_weight, laurel_left, laurel_right, query_weight]
        + [output_weight, side_gate, side_output],
        axis=1,
    )
    attn_block = plan.grow(attn_block, plan.far_seq)
    attn_block, feed_team = together(attn_block, feed_team)
    feed_full = lax.all_gather(feed_team.reshape(-1, hidden_own), plan.far, axis=0, tiled=True)
    attn_block = plan.grow(attn_block, (plan.l,))
    kvl_block, query_block, rest_block = split_columns(attn_block, block_widths)
    kvl_block = plan.grow(kvl_block, plan.far_dp)
    query_block = plan.grow(query_block, plan.far_dp)
    kvl_full = plan.gather_pieces(kvl_block)
    kvl_full, rest_block = together(kvl_full, rest_block)
    query_full = plan.gather_pieces(query_block)
    rest_block = plan.grow(rest_block, plan.far_dp)
    right_full = plan.far_team_rows([one[:, -kvl_widths[3] :] for one in kvl_full])
    kvl_full = [one[:, : -kvl_widths[3]] for one in kvl_full]

    places = jnp.arange(width, dtype=jnp.int32)
    far_team = plan.to_far_team(places[None])[0]
    to_far_team = (places[:, None] == far_team[None, :]).astype(BF16)
    to_spread = (places[:, None] == plan.spread_order(width)[None, :]).astype(BF16)
    gains = jnp.stack([norm_input, norm_attn, norm_laurel, norm_before, norm_after, norm_layer])
    norm_input, norm_attn, norm_laurel, norm_before, norm_after, norm_layer = plan.to_far_team(gains)
    inputs = product(tokens.reshape(rows, width), to_far_team)
    upstream = product(cotangent.reshape(rows, width), to_far_team)
    side_in = per_layer.astype(F32).reshape(rows, -1)
    normed, pre_pull = jax.vjp(rms, inputs, norm_input)
    normed_low = normed.astype(BF16)
    normed_spread = product(normed_low, to_spread).astype(BF16)
    keys, values, latent = split_columns(
        product_split(normed_spread, kvl_full), kvl_widths[:3]
    )
    queries = product_split(normed_spread, query_full).reshape(batch, block, heads, head_size)
    keys = keys.reshape(batch, block, kv_heads, head_size)
    values = values.reshape(batch, block, kv_heads, head_size)
    latent_low = latent.astype(BF16)

    def head_prep(query_in, key_in, value_in, gain_query, gain_key):
        return (
            rotate(rms(query_in, gain_query), positions),
            rotate(rms(key_in, gain_key), positions),
            rms(value_in, 1.0),
        )

    (rot_query, rot_key, rot_value), prep_pull = jax.vjp(
        head_prep, queries, keys, values, norm_query, norm_key
    )
    query_low = rot_query.astype(BF16)
    key_low = rot_key.astype(BF16)
    value_low = rot_value.astype(BF16)
    left_count = WINDOW // block
    right_count = (SPAN + block - 2) // block
    offsets = list(range(left_count, 0, -1)) + [0] + list(range(-1, -right_count - 1, -1))
    whole_sequence = seq_count <= len(offsets) + 1
    seq_index = lax.axis_index(plan.seq)
    total_length = block * seq_count
    if whole_sequence:
        key_low, value_low, rest_block = together(key_low, value_low, rest_block)
        pair_low = plan.near_far(key_low, value_low)
        keys_all, values_all = [
            one.swapaxes(0, 1).reshape(batch, total_length, kv_heads, head_size)
            for one in plan.near_gather(pair_low)
        ]
        key_blocks = plan.near_places()
    else:
        pair_low = jnp.stack([key_low, value_low])
        gathered = [
            passed_along(pair_low, plan.seq, seq_count, offset) if offset else pair_low
            for offset in offsets
        ]
        keys_all, values_all = jnp.concatenate(gathered, axis=2)
        key_blocks = seq_index - jnp.array(offsets, dtype=jnp.int32)
    key_count = keys_all.shape[1]
    rest_other = swap(rest_block, plan.order[-1])
    keys_all, values_all, rest_other = together(keys_all, values_all, rest_other)
    rest_full = plan.core_pieces(rest_block, rest_other)
    query_places = seq_index * block + jnp.arange(block, dtype=jnp.int32)
    key_places = (key_blocks[:, None] * block + jnp.arange(block, dtype=jnp.int32)).reshape(-1)
    in_query = (query_places[None, :, None] >= span_start[:, None, :]) & (
        query_places[None, :, None] < span_start[:, None, :] + SPAN
    )
    in_key = (key_places[None, :, None] >= span_start[:, None, :]) & (
        key_places[None, :, None] < span_start[:, None, :] + SPAN
    )
    same = jnp.any(in_query[:, :, None, :] & in_key[:, None, :, :], axis=-1)
    near = (key_places[None, :] <= query_places[:, None]) & (
        query_places[:, None] - key_places[None, :] < WINDOW
    )
    valid = (key_places >= 0) & (key_places < total_length)
    allowed = (valid[None, None, :] & (near[None] | same))[:, None, None]
    query_group = query_low.reshape(batch, block, kv_heads, group, head_size)
    scores = jnp.einsum("btkgd,bskd->bkgts", query_group, keys_all, preferred_element_type=F32)
    masked = jnp.where(allowed, scores, -1e30)
    top = jnp.max(masked, axis=-1, keepdims=True)
    expo = jnp.exp(masked - top)
    total = jnp.sum(expo, axis=-1, keepdims=True)
    probs = expo / total
    probs_low = probs.astype(BF16)
    attended = jnp.einsum("bkgts,bskd->btkgd", probs_low, values_all, preferred_element_type=F32)
    attended_low = attended.reshape(rows, heads * head_size).astype(BF16)
    attended_low, feed_full = together(attended_low, feed_full)
    output_full = [one[:, : rest_widths[0]] for one in rest_full]
    side_full = plan.far_team_rows([one[:, rest_widths[0] :] for one in rest_full])
    side_gate_full, side_output_full = split_columns(side_full, rest_widths[1:])
    attn_proj = reorder(product_nt_split(attended_low, output_full), to_spread)
    laurel = product_nt(latent_low, right_full)
    (resid_one, feed_in), mid_pull = jax.vjp(
        middle, inputs, normed, attn_proj, laurel, norm_attn, norm_laurel, norm_before
    )

    feed_low = feed_in.astype(BF16)
    feed_full = feed_full.reshape(-1, 3, team_size * local_rows, hidden_own)
    gate_full, up_full, down_full = [feed_full[:, at].reshape(width, hidden_own) for at in range(3)]
    pulls = []
    hidden_chunks = []

    def forward_chunk(chunk):
        hidden, pull = jax.vjp(gate_act, product(chunk, gate_full), product(chunk, up_full))
        hidden_low = hidden.astype(BF16)
        pulls.append(pull)
        hidden_chunks.append(hidden_low)
        return product_nt(hidden_low, down_full).astype(BF16)

    feed_chunks, feed_parts = plan.team_map(feed_low, forward_chunk)
    feed_out = plan.team_far(plan.team_near(plan.core_sums(feed_parts)))

    resid_two, after_pull = jax.vjp(after_feed, resid_one, feed_out, norm_after)
    resid_low = resid_two.astype(BF16)
    side_pre = product(resid_low, side_gate_full)
    side_val, side_pull = jax.vjp(side_act, side_pre, side_in)
    side_low = side_val.astype(BF16)
    side_out = product_nt(side_low, side_output_full)
    result, final_pull = jax.vjp(finish, resid_two, side_out, norm_layer)
    output = product_nt(result.astype(BF16), to_far_team).astype(BF16).reshape(batch, block, width)

    d_resid_two, d_side_out, grad_norm_layer = final_pull(upstream)
    d_side_out_low = d_side_out.astype(BF16)
    d_side = product(d_side_out_low, side_output_full)
    d_side_pre, d_side_in = side_pull(d_side)
    d_side_pre_low = d_side_pre.astype(BF16)
    d_resid_two = d_resid_two + product_nt(d_side_pre_low, side_gate_full)
    d_resid_one, d_feed_out, grad_norm_after = after_pull(d_resid_two)

    d_out_low = d_feed_out.astype(BF16)
    d_gate_chunks = []
    d_up_chunks = []

    def backward_chunk(chunk):
        d_gate, d_up = pulls[len(d_gate_chunks)](product(chunk, down_full))
        d_gate_chunks.append(d_gate.astype(BF16))
        d_up_chunks.append(d_up.astype(BF16))
        part = product_nt(d_gate_chunks[-1], gate_full) + product_nt(d_up_chunks[-1], up_full)
        return part.astype(BF16)

    d_out_chunks, d_feed_parts = plan.team_map(d_out_low, backward_chunk)
    d_feed_sums = plan.core_sums(d_feed_parts)
    d_gate_chunks, d_up_chunks, feed_chunks, d_out_chunks, hidden_chunks, d_feed_sums = together(
        d_gate_chunks, d_up_chunks, feed_chunks, d_out_chunks, hidden_chunks, d_feed_sums
    )
    feed_all = jnp.concatenate(feed_chunks, axis=0)
    d_out_all = jnp.concatenate(d_out_chunks, axis=0)
    feed_terms = jnp.stack(
        [
            product_tn(left, jnp.concatenate(right, axis=0))
            .astype(BF16)
            .reshape(-1, team_size * local_rows, hidden_own)
            for left, right in (
                (feed_all, d_gate_chunks),
                (feed_all, d_up_chunks),
                (d_out_all, hidden_chunks),
            )
        ],
        axis=1,
    )
    d_feed_in = plan.team_far(plan.team_near(d_feed_sums))
    d_feed_in, feed_terms = together(d_feed_in, feed_terms)
    feed_sum = lax.psum_scatter(
        feed_terms.reshape(-1, hidden_own), plan.far, scatter_dimension=0, tiled=True
    )
    steps = tuple(reversed(plan.order))

    (
        d_inputs,
        d_normed,
        d_attn_proj,
        d_laurel,
        grad_norm_attn,
        grad_norm_laurel,
        grad_norm_before,
    ) = mid_pull((d_resid_one, d_feed_in))
    d_attn_low = d_attn_proj.astype(BF16)
    d_laurel_low = d_laurel.astype(BF16)
    d_attn_spread = product(d_attn_low, to_spread).astype(BF16)
    d_latent_low = product(d_laurel_low, right_full).astype(BF16)
    output_sum = plan.spread_begin([(d_attn_spread, attended_low)])
    d_attn_spread, output_sum = together(d_attn_spread, output_sum)
    d_attended_low = product_split(d_attn_spread, output_full).astype(BF16)
    output_sum = plan.spread_step(output_sum, steps[:1])

    d_att = d_attended_low.reshape(batch, block, kv_heads, group, head_size)
    d_values_all = jnp.einsum("bkgts,btkgd->bskd", probs_low, d_att, preferred_element_type=F32)
    d_probs = jnp.einsum("btkgd,bskd->bkgts", d_att, values_all, preferred_element_type=F32)
    d_scores = probs * (d_probs - jnp.sum(probs * d_probs, axis=-1, keepdims=True))
    d_scores_low = d_scores.astype(BF16)
    d_query_rot = jnp.einsum("bkgts,bskd->btkgd", d_scores_low, keys_all, preferred_element_type=F32)
    d_keys_all = jnp.einsum(
        "bkgts,btkgd->bskd", d_scores_low, query_group, preferred_element_type=F32
    )
    d_keys_all, d_values_all, d_query_rot, output_sum, side_left = together(
        d_keys_all,
        d_values_all,
        d_query_rot,
        output_sum,
        jnp.concatenate([resid_low, d_side_out_low], axis=0),
    )
    side_left = product(side_left, to_spread).astype(BF16)
    side_sum = plan.spread_begin([(side_left[:rows], d_side_pre_low), (side_left[rows:], side_low)])
    side_sum = plan.spread_step(side_sum, steps[:1])
    if whole_sequence:
        d_pair_total = plan.near_sum(
            *[
                one.reshape(batch, seq_count, block, kv_heads, head_size).swapaxes(0, 1)
                for one in (d_keys_all, d_values_all)
            ]
        )
    else:
        d_pairs = jnp.stack([d_keys_all, d_values_all])
        d_pair_total = d_pairs[:, :, left_count * block : (left_count + 1) * block]
        for position, offset in enumerate(offsets):
            if offset != 0:
                piece = d_pairs[:, :, position * block : (position + 1) * block].astype(BF16)
                moved = passed_along(piece, plan.seq, seq_count, -offset)
                d_pair_total = d_pair_total + moved.astype(F32)
    d_queries, d_keys, d_values, grad_norm_query, grad_norm_key = prep_pull(
        (d_query_rot.reshape(batch, block, heads, head_size), d_pair_total[0], d_pair_total[1])
    )
    d_queries_low = d_queries.reshape(rows, -1).astype(BF16)
    query_sum = plan.spread_begin([(normed_spread, d_queries_low)])
    query_sum = plan.spread_step(query_sum, steps[:1])
    d_spread = product_nt_split(d_queries_low, query_full)
    d_keys, d_values, query_sum, output_sum, side_sum, d_spread, feed_sum = together(
        d_keys, d_values, query_sum, output_sum, side_sum, d_spread, feed_sum
    )
    output_sum = jnp.concatenate([output_sum, side_sum], axis=1)
    grad_gate, grad_up, grad_down = plan.own_rows(jnp.split(feed_sum, 3), local_rows)
    d_kvl_low = jnp.concatenate(
        [
            d_keys.reshape(rows, -1).astype(BF16),
            d_values.reshape(rows, -1).astype(BF16),
            d_latent_low,
        ],
        axis=1,
    )
    laurel_spread = product(d_laurel_low, to_spread).astype(BF16)
    kvl_sum = plan.spread_begin([(normed_spread, d_kvl_low), (laurel_spread, latent_low)])
    query_kept, query_away = plan.spread_send(query_sum, steps[1])
    output_kept, output_away = plan.spread_send(output_sum, steps[1])
    kvl_sum = plan.spread_step(kvl_sum, steps[:1])
    kvl_sum, query_kept, output_kept = together(kvl_sum, query_kept, output_kept)
    query_sum = (query_kept + query_away).astype(BF16)
    output_sum = (output_kept + output_away).astype(BF16)
    kvl_sum = plan.spread_step(kvl_sum, steps[1:2])
    query_sum = plan.spread_step(query_sum, steps[2:3])
    output_sum = plan.spread_step(output_sum, steps[2:3])
    kvl_sum, query_sum, output_sum, d_kvl_low = together(kvl_sum, query_sum, output_sum, d_kvl_low)
    d_spread = d_spread + product_nt_split(d_kvl_low, kvl_full)
    d_normed = d_normed + reorder(d_spread, to_spread)
    d_inputs_norm, grad_norm_input = pre_pull(d_normed)
    grad_tokens = reorder(d_inputs + d_inputs_norm, to_far_team).reshape(batch, block, width)
    grad_side = d_side_in.reshape(batch, block, -1)
    norm_grads = jnp.stack(
        [
            grad_norm_input,
            grad_norm_attn,
            grad_norm_laurel,
            grad_norm_before,
            grad_norm_after,
            grad_norm_layer,
        ]
    )
    gain_grads = jnp.concatenate(
        [plan.from_far_team(norm_grads).reshape(-1), grad_norm_query, grad_norm_key]
    )
    grad_query = plan.spread_step(query_sum, steps[3:])
    output_sum = plan.spread_step(output_sum, steps[3:])
    kvl_sum = plan.spread_step(kvl_sum, steps[2:3])
    gain_grads, grad_query, output_sum, kvl_sum = together(
        gain_grads, grad_query, output_sum, kvl_sum
    )
    grad_output, grad_side_gate, grad_side_output = split_columns(output_sum, rest_widths)
    grad_key, grad_value, grad_left, grad_right = split_columns(
        plan.spread_step(kvl_sum, steps[3:]), kvl_widths
    )
    gain_grads = plan.total(gain_grads)
    gain_parts = split_columns(gain_grads, [width] * 6 + [head_size] * 2)
    return (
        output,
        grad_tokens,
        grad_side,
        grad_query,
        grad_key,
        grad_value,
        grad_output,
        grad_left,
        grad_right,
        grad_gate,
        grad_up,
        grad_down,
        grad_side_gate,
        grad_side_output,
    ) + tuple(gain_parts)


def solution(mesh):
    seq_bits = int(math.log2(mesh.shape["seq"]))
    dp_bits = int(math.log2(mesh.shape["dp"]))
    plan = Plan(seq_bits, dp_bits)
    binary = Mesh(mesh.devices.reshape((2,) * (seq_bits + dp_bits)), plan.every)
    token_spec = P(plan.dp, plan.seq, None)
    weight_spec = P(plan.every, None)

    def step(*arrays):
        return body(plan, *arrays)

    return jax.shard_map(
        step,
        mesh=binary,
        in_specs=(token_spec, token_spec, P(plan.dp, plan.seq), P(plan.dp, None), token_spec)
        + (weight_spec,) * 11
        + (P(),) * 8,
        out_specs=(token_spec,) * 3 + (weight_spec,) * 11 + (P(),) * 8,
        check_vma=False,
    )
```

```python
import math

import jax
import jax.numpy as jnp
from jax import lax
from jax.sharding import Mesh
from jax.sharding import PartitionSpec as P

WINDOW = 512
SPAN = 256
EPS = 1e-06
HALF_ROOT = 1.0 / math.sqrt(2.0)
F32 = jnp.float32
BF16 = jnp.bfloat16


def rms(values, gain):
    return values * lax.rsqrt(jnp.mean(values * values, axis=-1, keepdims=True) + EPS) * gain


def gelu_tanh(values):
    return jax.nn.gelu(values, approximate=True)


def product(left, right):
    return jnp.dot(left, right, preferred_element_type=F32)


def product_nt(left, right):
    return lax.dot_general(left, right, (((1,), (1,)), ((), ())), preferred_element_type=F32)


def product_tn(left, right):
    return lax.dot_general(left, right, (((0,), (0,)), ((), ())), preferred_element_type=F32)


def rotate(values, places):
    size = values.shape[-1]
    half = size // 2
    freq = 10000.0 ** (-(2.0 * jnp.arange(half, dtype=F32)) / size)
    angle = places.astype(F32)[..., None] * freq
    cosine = jnp.cos(angle)[..., None, :]
    sine = jnp.sin(angle)[..., None, :]
    first = values[..., :half]
    second = values[..., half:]
    return jnp.concatenate(
        [first * cosine - second * sine, second * cosine + first * sine], axis=-1
    )


def middle(inputs, normed, attn_proj, laurel, gain_attn, gain_laurel, gain_before):
    resid = (inputs + rms(attn_proj, gain_attn) + normed + rms(laurel, gain_laurel)) * HALF_ROOT
    return (resid, rms(resid, gain_before))


def gate_act(gate_val, up_val):
    return gelu_tanh(gate_val) * up_val


def after_feed(resid_one, feed_out, gain_after):
    return resid_one + rms(feed_out, gain_after)


def side_act(side_pre, side_in):
    return gelu_tanh(side_pre) * side_in


def finish(resid_two, side_out, gain_layer):
    return resid_two + rms(side_out, gain_layer)


def swap(value, axis):
    return lax.ppermute(value, axis, [(0, 1), (1, 0)])


def together(*values):
    return lax.optimization_barrier(values)


def split_columns(whole, widths):
    pieces = []
    offset = 0
    for width_one in widths:
        pieces.append(whole[..., offset : offset + width_one])
        offset = offset + width_one
    return pieces


class Plan:
    def __init__(self, seq_bits, dp_bits):
        self.seq = tuple("s%d" % i for i in range(seq_bits))
        self.dp = tuple("d%d" % i for i in range(dp_bits))
        self.every = self.seq + self.dp
        self.l, self.x = self.seq[-2:]
        self.c = self.dp[-1]
        self.team = (self.l, self.x, self.c)
        self.far_seq = self.seq[:-2]
        self.far_dp = self.dp[:-1]
        self.far = self.far_seq + self.far_dp
        self.canon = self.far + self.team
        self.order = self.far_seq + (self.l,) + self.far_dp + (self.x,)

    def flipped(self, value, axes, dims):
        for axis, dim in zip(axes, dims):
            value = jnp.where(lax.axis_index(axis) == 1, jnp.flip(value, dim), value)
        return value

    def to_far_team(self, value):
        rows, width = value.shape
        parts = value.reshape((rows,) + (2,) * len(self.every) + (-1,))
        order = [0] + [1 + self.every.index(axis) for axis in self.canon] + [1 + len(self.every)]
        return parts.transpose(order).reshape(rows, width)

    def from_far_team(self, value):
        rows, width = value.shape
        parts = value.reshape((rows,) + (2,) * len(self.every) + (-1,))
        order = [0] + [1 + self.canon.index(axis) for axis in self.every] + [1 + len(self.every)]
        return parts.transpose(order).reshape(rows, width)

    def spread_order(self, width):
        own = jnp.arange(width, dtype=jnp.int32).reshape((2,) * len(self.canon) + (-1,))
        own = self.flipped(own, self.canon, range(len(self.canon)))
        axes = (self.c,) + tuple(reversed(self.order))
        return own.transpose([self.canon.index(axis) for axis in axes] + [len(self.canon)]).reshape(-1)

    def grow(self, block, axes):
        for axis in axes:
            block = jnp.concatenate([block, swap(block, axis)], axis=0)
        return block

    def gather_pieces(self, block):
        return self.core_pieces(block, swap(block, self.order[-1]))

    def core_pieces(self, block, other):
        return [block, other, swap(block, self.c), swap(other, self.c)]

    def far_team_rows(self, pieces):
        axes = (self.c,) + tuple(reversed(self.order))
        whole = jnp.concatenate(pieces, axis=0)
        whole = whole.reshape((2,) * len(axes) + (-1, whole.shape[-1]))
        whole = whole.transpose([axes.index(axis) for axis in self.canon] + [len(axes), len(axes) + 1])
        whole = self.flipped(whole, self.canon, range(len(self.canon)))
        return whole.reshape((-1, whole.shape[-1]))

    def spread_begin(self, pairs):
        half = pairs[0][0].shape[1] // 2
        away = jnp.concatenate([product_tn(one[:, half:], two).astype(BF16) for one, two in pairs], axis=1)
        kept = jnp.concatenate([product_tn(one[:, :half], two).astype(BF16) for one, two in pairs], axis=1)
        return (kept.astype(F32) + swap(away, self.c).astype(F32)).astype(BF16)

    def spread_step(self, total, axes):
        for axis in axes:
            half = total.shape[0] // 2
            total = total[:half].astype(F32) + swap(total[half:], axis).astype(F32)
            if axis != self.order[0]:
                total = total.astype(BF16)
        return total

    def spread_send(self, total, axis):
        half = total.shape[0] // 2
        return total[:half].astype(F32), swap(total[half:], axis).astype(F32)

    def near_far(self, key, value):
        pair = jnp.stack([key, value])[:, None]
        for axis in reversed(self.far_seq):
            pair = jnp.concatenate([pair, swap(pair, axis)], axis=1)
        return pair

    def near_gather(self, pair):
        key, value = pair[0][None], pair[1][None]
        key = jnp.concatenate([key, swap(key, self.x)], axis=0)
        key = jnp.stack([key, swap(key, self.l)], axis=0)
        value = jnp.concatenate([value, swap(value, self.l)], axis=0)
        value = jnp.stack([value, swap(value, self.x)], axis=1)
        return [one.reshape((-1,) + one.shape[3:]) for one in (key, value)]

    def near_sum(self, key, value):
        def step(total, dim, axis):
            total = total.astype(BF16)
            away = swap(lax.index_in_dim(total, 1, dim, False), axis).astype(F32)
            return lax.index_in_dim(total, 0, dim, False).astype(F32) + away

        shape = (2, 2) + (2,) * len(self.far_seq)
        key, value = [one.reshape(shape + one.shape[1:]) for one in (key, value)]
        key = step(step(key, 0, self.l), 0, self.x)
        value = step(step(value, 1, self.x), 0, self.l)
        pair = jnp.stack([key, value])
        for axis in self.far_seq:
            pair = step(pair, 1, axis)
        return pair

    def near_places(self):
        place = jnp.zeros((1,), jnp.int32)
        for axis in (self.l, self.x) + self.far_seq:
            bit = lax.axis_index(axis)
            weight = 2 ** (len(self.seq) - 1 - self.seq.index(axis))
            place = (place[:, None] + weight * jnp.stack([bit, 1 - bit])[None, :]).reshape(-1)
        return place

    def to_rows(self, sums, local_rows):
        blocks = sums.reshape(2 ** len(self.team), local_rows, -1)
        return lax.all_to_all(blocks, self.team, split_axis=0, concat_axis=0, tiled=True)

    def total(self, value):
        for axis in reversed(self.every):
            value = value + swap(value, axis)
        return value

    def team_map(self, own, function):
        def chunk_of(piece):
            return jnp.concatenate([piece, swap(piece, self.c)], axis=0)

        by_x, by_l = swap(own, self.x), swap(own, self.l)
        chunks = [chunk_of(own)]
        results = [function(chunks[0])]
        by_x, by_l, results = together(by_x, by_l, results)
        half = own.shape[0] // 2
        both = jnp.concatenate([swap(by_x[:half], self.l), swap(by_l[half:], self.x)], axis=0)
        for piece in (by_x, by_l, both):
            chunks.append(chunk_of(piece))
            results.append(function(chunks[-1]))
        return chunks, results

    def core_sums(self, chunks):
        sums = []
        for chunk in chunks:
            rows = chunk.shape[0] // 2
            other = swap(chunk[rows:].astype(BF16), self.c)
            sums.append(chunk[:rows].astype(F32) + other.astype(F32))
        return sums

    def team_near(self, sums):
        own, by_x, by_l, both = sums
        half = own.shape[0] // 2
        both = both.astype(BF16)
        first = by_l[:half] + swap(both[:half], self.x).astype(F32)
        second = by_x[half:] + swap(both[half:], self.l).astype(F32)
        by_l = jnp.concatenate([first, by_l[half:]], axis=0).astype(BF16)
        by_x = jnp.concatenate([by_x[:half], second], axis=0).astype(BF16)
        return own, by_l, by_x

    def team_far(self, sums):
        own, by_l, by_x = sums
        return own + swap(by_l, self.l).astype(F32) + swap(by_x, self.x).astype(F32)


def product_split(left, pieces):
    width = left.shape[1] // len(pieces)
    return sum(product(left[:, i * width : (i + 1) * width], one) for i, one in enumerate(pieces))


def product_nt_split(left, pieces):
    return jnp.concatenate([product_nt(left, one) for one in pieces], axis=1)


def reorder(values, matrix):
    rows = values.shape[0]
    high = lax.reduce_precision(values, 8, 7)
    parts = jnp.concatenate([high.astype(BF16), (values - high).astype(BF16)], axis=0)
    parts = product_nt(parts, matrix)
    return parts[:rows] + parts[rows:]


def passed_along(value, axes, count, steps):
    initial, last = (max(0, -steps), min(count, count - steps))
    return lax.ppermute(value, axes, [(source, source + steps) for source in range(initial, last)])


def body(
    plan,
    tokens,
    per_layer,
    positions,
    span_start,
    cotangent,
    query_weight,
    key_weight,
    value_weight,
    output_weight,
    laurel_left,
    laurel_right,
    gate_weight,
    up_weight,
    down_weight,
    side_gate,
    side_output,
    norm_input,
    norm_attn,
    norm_laurel,
    norm_before,
    norm_after,
    norm_layer,
    norm_query,
    norm_key,
):
    batch, block, width = tokens.shape
    rows = batch * block
    head_size = norm_query.shape[0]
    heads = query_weight.shape[1] // head_size
    kv_heads = key_weight.shape[1] // head_size
    group = heads // kv_heads
    seq_count = 2 ** len(plan.seq)
    local_rows = gate_weight.shape[0]
    team_size = 2 ** len(plan.team)
    hidden_own = gate_weight.shape[1] // team_size

    kvl_widths = [
        key_weight.shape[1],
        value_weight.shape[1],
        laurel_left.shape[1],
        laurel_right.shape[1],
    ]
    rest_widths = [output_weight.shape[1], side_gate.shape[1], side_output.shape[1]]
    feed_local = jnp.concatenate(
        [
            one.reshape(local_rows, team_size, hidden_own).transpose(1, 0, 2)
            for one in (gate_weight, up_weight, down_weight)
        ],
        axis=2,
    )
    feed_team = lax.all_to_all(feed_local, plan.team, split_axis=0, concat_axis=0, tiled=True)
    block_widths = [sum(kvl_widths), query_weight.shape[1], sum(rest_widths)]
    attn_block = jnp.concatenate(
        [key_weight, value_weight, laurel_left, laurel_right, query_weight]
        + [output_weight, side_gate, side_output],
        axis=1,
    )
    attn_block = plan.grow(attn_block, plan.far_seq)
    attn_block, feed_team = together(attn_block, feed_team)
    feed_full = lax.all_gather(feed_team.reshape(-1, 3 * hidden_own), plan.far, axis=0, tiled=True)
    attn_block = plan.grow(attn_block, (plan.l,))
    kvl_block, query_block, rest_block = split_columns(attn_block, block_widths)
    kvl_block = plan.grow(kvl_block, plan.far_dp)
    query_block = plan.grow(query_block, plan.far_dp)
    kvl_full = plan.gather_pieces(kvl_block)
    kvl_full, rest_block = together(kvl_full, rest_block)
    query_full = plan.gather_pieces(query_block)
    rest_block = plan.grow(rest_block, plan.far_dp)
    right_full = plan.far_team_rows([one[:, -kvl_widths[3] :] for one in kvl_full])
    kvl_full = [one[:, : -kvl_widths[3]] for one in kvl_full]

    places = jnp.arange(width, dtype=jnp.int32)
    far_team = plan.to_far_team(places[None])[0]
    to_far_team = (places[:, None] == far_team[None, :]).astype(BF16)
    to_spread = (places[:, None] == plan.spread_order(width)[None, :]).astype(BF16)
    gains = jnp.stack([norm_input, norm_attn, norm_laurel, norm_before, norm_after, norm_layer])
    norm_input, norm_attn, norm_laurel, norm_before, norm_after, norm_layer = plan.to_far_team(gains)
    inputs = product(tokens.reshape(rows, width), to_far_team)
    upstream = product(cotangent.reshape(rows, width), to_far_team)
    side_in = per_layer.astype(F32).reshape(rows, -1)
    normed, pre_pull = jax.vjp(rms, inputs, norm_input)
    normed_low = normed.astype(BF16)
    normed_spread = product(normed_low, to_spread).astype(BF16)
    keys, values, latent = split_columns(
        product_split(normed_spread, kvl_full), kvl_widths[:3]
    )
    queries = product_split(normed_spread, query_full).reshape(batch, block, heads, head_size)
    keys = keys.reshape(batch, block, kv_heads, head_size)
    values = values.reshape(batch, block, kv_heads, head_size)
    latent_low = latent.astype(BF16)

    def head_prep(query_in, key_in, value_in, gain_query, gain_key):
        return (
            rotate(rms(query_in, gain_query), positions),
            rotate(rms(key_in, gain_key), positions),
            rms(value_in, 1.0),
        )

    (rot_query, rot_key, rot_value), prep_pull = jax.vjp(
        head_prep, queries, keys, values, norm_query, norm_key
    )
    query_low = rot_query.astype(BF16)
    key_low = rot_key.astype(BF16)
    value_low = rot_value.astype(BF16)
    left_count = WINDOW // block
    right_count = (SPAN + block - 2) // block
    offsets = list(range(left_count, 0, -1)) + [0] + list(range(-1, -right_count - 1, -1))
    whole_sequence = seq_count <= len(offsets) + 1
    seq_index = lax.axis_index(plan.seq)
    total_length = block * seq_count
    if whole_sequence:
        key_low, value_low, rest_block = together(key_low, value_low, rest_block)
        pair_low = plan.near_far(key_low, value_low)
        keys_all, values_all = [
            one.swapaxes(0, 1).reshape(batch, total_length, kv_heads, head_size)
            for one in plan.near_gather(pair_low)
        ]
        key_blocks = plan.near_places()
    else:
        pair_low = jnp.stack([key_low, value_low])
        gathered = [
            passed_along(pair_low, plan.seq, seq_count, offset) if offset else pair_low
            for offset in offsets
        ]
        keys_all, values_all = jnp.concatenate(gathered, axis=2)
        key_blocks = seq_index - jnp.array(offsets, dtype=jnp.int32)
    key_count = keys_all.shape[1]
    rest_other = swap(rest_block, plan.order[-1])
    keys_all, values_all, rest_other = together(keys_all, values_all, rest_other)
    rest_full = plan.core_pieces(rest_block, rest_other)
    query_places = seq_index * block + jnp.arange(block, dtype=jnp.int32)
    key_places = (key_blocks[:, None] * block + jnp.arange(block, dtype=jnp.int32)).reshape(-1)
    in_query = (query_places[None, :, None] >= span_start[:, None, :]) & (
        query_places[None, :, None] < span_start[:, None, :] + SPAN
    )
    in_key = (key_places[None, :, None] >= span_start[:, None, :]) & (
        key_places[None, :, None] < span_start[:, None, :] + SPAN
    )
    same = jnp.any(in_query[:, :, None, :] & in_key[:, None, :, :], axis=-1)
    near = (key_places[None, :] <= query_places[:, None]) & (
        query_places[:, None] - key_places[None, :] < WINDOW
    )
    valid = (key_places >= 0) & (key_places < total_length)
    allowed = (valid[None, None, :] & (near[None] | same))[:, None, None]
    query_group = query_low.reshape(batch, block, kv_heads, group, head_size)
    scores = jnp.einsum("btkgd,bskd->bkgts", query_group, keys_all, preferred_element_type=F32)
    masked = jnp.where(allowed, scores, -1e30)
    top = jnp.max(masked, axis=-1, keepdims=True)
    expo = jnp.exp(masked - top)
    total = jnp.sum(expo, axis=-1, keepdims=True)
    probs = expo / total
    probs_low = probs.astype(BF16)
    attended = jnp.einsum("bkgts,bskd->btkgd", probs_low, values_all, preferred_element_type=F32)
    attended_low = attended.reshape(rows, heads * head_size).astype(BF16)
    attended_low, feed_full = together(attended_low, feed_full)
    output_full = [one[:, : rest_widths[0]] for one in rest_full]
    side_full = plan.far_team_rows([one[:, rest_widths[0] :] for one in rest_full])
    side_gate_full, side_output_full = split_columns(side_full, rest_widths[1:])
    attn_proj = reorder(product_nt_split(attended_low, output_full), to_spread)
    laurel = product_nt(latent_low, right_full)
    (resid_one, feed_in), mid_pull = jax.vjp(
        middle, inputs, normed, attn_proj, laurel, norm_attn, norm_laurel, norm_before
    )

    feed_low = feed_in.astype(BF16)
    gate_full, up_full, down_full = split_columns(feed_full, [hidden_own] * 3)
    pulls = []
    hidden_chunks = []

    def forward_chunk(chunk):
        hidden, pull = jax.vjp(gate_act, product(chunk, gate_full), product(chunk, up_full))
        hidden_low = hidden.astype(BF16)
        pulls.append(pull)
        hidden_chunks.append(hidden_low)
        return product_nt(hidden_low, down_full).astype(BF16)

    feed_chunks, feed_parts = plan.team_map(feed_low, forward_chunk)
    feed_out = plan.team_far(plan.team_near(plan.core_sums(feed_parts)))

    resid_two, after_pull = jax.vjp(after_feed, resid_one, feed_out, norm_after)
    resid_low = resid_two.astype(BF16)
    side_pre = product(resid_low, side_gate_full)
    side_val, side_pull = jax.vjp(side_act, side_pre, side_in)
    side_low = side_val.astype(BF16)
    side_out = product_nt(side_low, side_output_full)
    result, final_pull = jax.vjp(finish, resid_two, side_out, norm_layer)
    output = product_nt(result.astype(BF16), to_far_team).astype(BF16).reshape(batch, block, width)

    d_resid_two, d_side_out, grad_norm_layer = final_pull(upstream)
    d_side_out_low = d_side_out.astype(BF16)
    d_side = product(d_side_out_low, side_output_full)
    d_side_pre, d_side_in = side_pull(d_side)
    d_side_pre_low = d_side_pre.astype(BF16)
    d_resid_two = d_resid_two + product_nt(d_side_pre_low, side_gate_full)
    d_resid_one, d_feed_out, grad_norm_after = after_pull(d_resid_two)

    d_out_low = d_feed_out.astype(BF16)
    d_gate_chunks = []
    d_up_chunks = []

    def backward_chunk(chunk):
        d_gate, d_up = pulls[len(d_gate_chunks)](product(chunk, down_full))
        d_gate_chunks.append(d_gate.astype(BF16))
        d_up_chunks.append(d_up.astype(BF16))
        part = product_nt(d_gate_chunks[-1], gate_full) + product_nt(d_up_chunks[-1], up_full)
        return part.astype(BF16)

    d_out_chunks, d_feed_parts = plan.team_map(d_out_low, backward_chunk)
    d_feed_sums = plan.core_sums(d_feed_parts)
    d_gate_chunks, d_up_chunks, feed_chunks, d_out_chunks, hidden_chunks, d_feed_sums = together(
        d_gate_chunks, d_up_chunks, feed_chunks, d_out_chunks, hidden_chunks, d_feed_sums
    )
    feed_all = jnp.concatenate(feed_chunks, axis=0)
    d_out_all = jnp.concatenate(d_out_chunks, axis=0)
    feed_terms = jnp.concatenate(
        [
            product_tn(left, jnp.concatenate(right, axis=0)).astype(BF16)
            for left, right in (
                (feed_all, d_gate_chunks),
                (feed_all, d_up_chunks),
                (d_out_all, hidden_chunks),
            )
        ],
        axis=1,
    )
    d_feed_in = plan.team_far(plan.team_near(d_feed_sums))
    d_feed_in, feed_terms = together(d_feed_in, feed_terms)
    feed_sum = lax.psum_scatter(feed_terms, plan.far, scatter_dimension=0, tiled=True)
    steps = tuple(reversed(plan.order))

    (
        d_inputs,
        d_normed,
        d_attn_proj,
        d_laurel,
        grad_norm_attn,
        grad_norm_laurel,
        grad_norm_before,
    ) = mid_pull((d_resid_one, d_feed_in))
    d_attn_low = d_attn_proj.astype(BF16)
    d_laurel_low = d_laurel.astype(BF16)
    d_attn_spread = product(d_attn_low, to_spread).astype(BF16)
    d_latent_low = product(d_laurel_low, right_full).astype(BF16)
    output_sum = plan.spread_begin([(d_attn_spread, attended_low)])
    d_attn_spread, output_sum = together(d_attn_spread, output_sum)
    d_attended_low = product_split(d_attn_spread, output_full).astype(BF16)
    output_sum = plan.spread_step(output_sum, steps[:1])

    d_att = d_attended_low.reshape(batch, block, kv_heads, group, head_size)
    d_values_all = jnp.einsum("bkgts,btkgd->bskd", probs_low, d_att, preferred_element_type=F32)
    d_probs = jnp.einsum("btkgd,bskd->bkgts", d_att, values_all, preferred_element_type=F32)
    d_scores = probs * (d_probs - jnp.sum(probs * d_probs, axis=-1, keepdims=True))
    d_scores_low = d_scores.astype(BF16)
    d_query_rot = jnp.einsum("bkgts,bskd->btkgd", d_scores_low, keys_all, preferred_element_type=F32)
    d_keys_all = jnp.einsum(
        "bkgts,btkgd->bskd", d_scores_low, query_group, preferred_element_type=F32
    )
    d_keys_all, d_values_all, d_query_rot, output_sum, side_left = together(
        d_keys_all,
        d_values_all,
        d_query_rot,
        output_sum,
        jnp.concatenate([resid_low, d_side_out_low], axis=0),
    )
    side_left = product(side_left, to_spread).astype(BF16)
    side_sum = plan.spread_begin([(side_left[:rows], d_side_pre_low), (side_left[rows:], side_low)])
    side_sum = plan.spread_step(side_sum, steps[:1])
    if whole_sequence:
        d_pair_total = plan.near_sum(
            *[
                one.reshape(batch, seq_count, block, kv_heads, head_size).swapaxes(0, 1)
                for one in (d_keys_all, d_values_all)
            ]
        )
    else:
        d_pairs = jnp.stack([d_keys_all, d_values_all])
        d_pair_total = d_pairs[:, :, left_count * block : (left_count + 1) * block]
        for position, offset in enumerate(offsets):
            if offset != 0:
                piece = d_pairs[:, :, position * block : (position + 1) * block].astype(BF16)
                moved = passed_along(piece, plan.seq, seq_count, -offset)
                d_pair_total = d_pair_total + moved.astype(F32)
    d_queries, d_keys, d_values, grad_norm_query, grad_norm_key = prep_pull(
        (d_query_rot.reshape(batch, block, heads, head_size), d_pair_total[0], d_pair_total[1])
    )
    d_queries_low = d_queries.reshape(rows, -1).astype(BF16)
    query_sum = plan.spread_begin([(normed_spread, d_queries_low)])
    query_sum = plan.spread_step(query_sum, steps[:1])
    d_spread = product_nt_split(d_queries_low, query_full)
    d_keys, d_values, query_sum, output_sum, side_sum, d_spread, feed_sum = together(
        d_keys, d_values, query_sum, output_sum, side_sum, d_spread, feed_sum
    )
    output_sum = jnp.concatenate([output_sum, side_sum], axis=1)
    d_kvl_low = jnp.concatenate(
        [
            d_keys.reshape(rows, -1).astype(BF16),
            d_values.reshape(rows, -1).astype(BF16),
            d_latent_low,
        ],
        axis=1,
    )
    laurel_spread = product(d_laurel_low, to_spread).astype(BF16)
    kvl_sum = plan.spread_begin([(normed_spread, d_kvl_low), (laurel_spread, latent_low)])
    query_kept, query_away = plan.spread_send(query_sum, steps[1])
    output_kept, output_away = plan.spread_send(output_sum, steps[1])
    kvl_sum = plan.spread_step(kvl_sum, steps[:1])
    kvl_sum, query_kept, output_kept, feed_sum = together(
        kvl_sum, query_kept, output_kept, feed_sum
    )
    feed_grads = plan.to_rows(feed_sum, local_rows)
    query_sum = (query_kept + query_away).astype(BF16)
    output_sum = (output_kept + output_away).astype(BF16)
    kvl_sum = plan.spread_step(kvl_sum, steps[1:2])
    query_sum = plan.spread_step(query_sum, steps[2:3])
    output_sum = plan.spread_step(output_sum, steps[2:3])
    kvl_sum, query_sum, output_sum, d_kvl_low = together(kvl_sum, query_sum, output_sum, d_kvl_low)
    d_spread = d_spread + product_nt_split(d_kvl_low, kvl_full)
    d_normed = d_normed + reorder(d_spread, to_spread)
    d_inputs_norm, grad_norm_input = pre_pull(d_normed)
    grad_tokens = reorder(d_inputs + d_inputs_norm, to_far_team).reshape(batch, block, width)
    grad_side = d_side_in.reshape(batch, block, -1)
    norm_grads = jnp.stack(
        [
            grad_norm_input,
            grad_norm_attn,
            grad_norm_laurel,
            grad_norm_before,
            grad_norm_after,
            grad_norm_layer,
        ]
    )
    gain_grads = jnp.concatenate(
        [plan.from_far_team(norm_grads).reshape(-1), grad_norm_query, grad_norm_key]
    )
    grad_query = plan.spread_step(query_sum, steps[3:])
    output_sum = plan.spread_step(output_sum, steps[3:])
    kvl_sum = plan.spread_step(kvl_sum, steps[2:3])
    gain_grads, grad_query, output_sum, kvl_sum, feed_grads = together(
        gain_grads, grad_query, output_sum, kvl_sum, feed_grads
    )
    grad_gate, grad_up, grad_down = [
        jnp.concatenate(
            [feed_grads[at, :, first : first + hidden_own] for at in range(team_size)], axis=1
        ).astype(F32)
        for first in range(0, 3 * hidden_own, hidden_own)
    ]
    grad_output, grad_side_gate, grad_side_output = split_columns(output_sum, rest_widths)
    grad_key, grad_value, grad_left, grad_right = split_columns(
        plan.spread_step(kvl_sum, steps[3:]), kvl_widths
    )
    gain_grads = plan.total(gain_grads)
    gain_parts = split_columns(gain_grads, [width] * 6 + [head_size] * 2)
    return (
        output,
        grad_tokens,
        grad_side,
        grad_query,
        grad_key,
        grad_value,
        grad_output,
        grad_left,
        grad_right,
        grad_gate,
        grad_up,
        grad_down,
        grad_side_gate,
        grad_side_output,
    ) + tuple(gain_parts)


def solution(mesh):
    seq_bits = int(math.log2(mesh.shape["seq"]))
    dp_bits = int(math.log2(mesh.shape["dp"]))
    plan = Plan(seq_bits, dp_bits)
    binary = Mesh(mesh.devices.reshape((2,) * (seq_bits + dp_bits)), plan.every)
    token_spec = P(plan.dp, plan.seq, None)
    weight_spec = P(plan.every, None)

    def step(*arrays):
        return body(plan, *arrays)

    return jax.shard_map(
        step,
        mesh=binary,
        in_specs=(token_spec, token_spec, P(plan.dp, plan.seq), P(plan.dp, None), token_spec)
        + (weight_spec,) * 11
        + (P(),) * 8,
        out_specs=(token_spec,) * 3 + (weight_spec,) * 11 + (P(),) * 8,
        check_vma=False,
    )
```

```python
import math

import jax
import jax.numpy as jnp
from jax import lax
from jax.sharding import Mesh
from jax.sharding import PartitionSpec as P

WINDOW = 512
SPAN = 256
EPS = 1e-06
HALF_ROOT = 1.0 / math.sqrt(2.0)
F32 = jnp.float32
BF16 = jnp.bfloat16


def rms(values, gain):
    return values * lax.rsqrt(jnp.mean(values * values, axis=-1, keepdims=True) + EPS) * gain


def gelu_tanh(values):
    return jax.nn.gelu(values, approximate=True)


def product(left, right):
    return jnp.dot(left, right, preferred_element_type=F32)


def product_nt(left, right):
    return lax.dot_general(left, right, (((1,), (1,)), ((), ())), preferred_element_type=F32)


def product_tn(left, right):
    return lax.dot_general(left, right, (((0,), (0,)), ((), ())), preferred_element_type=F32)


def rotate(values, places):
    size = values.shape[-1]
    half = size // 2
    freq = 10000.0 ** (-(2.0 * jnp.arange(half, dtype=F32)) / size)
    angle = places.astype(F32)[..., None] * freq
    cosine = jnp.cos(angle)[..., None, :]
    sine = jnp.sin(angle)[..., None, :]
    first = values[..., :half]
    second = values[..., half:]
    return jnp.concatenate(
        [first * cosine - second * sine, second * cosine + first * sine], axis=-1
    )


def middle(inputs, normed, attn_proj, laurel, gain_attn, gain_laurel, gain_before):
    resid = (inputs + rms(attn_proj, gain_attn) + normed + rms(laurel, gain_laurel)) * HALF_ROOT
    return (resid, rms(resid, gain_before))


def gate_act(gate_val, up_val):
    return gelu_tanh(gate_val) * up_val


def after_feed(resid_one, feed_out, gain_after):
    return resid_one + rms(feed_out, gain_after)


def side_act(side_pre, side_in):
    return gelu_tanh(side_pre) * side_in


def finish(resid_two, side_out, gain_layer):
    return resid_two + rms(side_out, gain_layer)


def swap(value, axis):
    return lax.ppermute(value, axis, [(0, 1), (1, 0)])


def together(*values):
    return lax.optimization_barrier(values)


def split_columns(whole, widths):
    pieces = []
    offset = 0
    for width_one in widths:
        pieces.append(whole[..., offset : offset + width_one])
        offset = offset + width_one
    return pieces


class Plan:
    def __init__(self, seq_bits, dp_bits):
        self.seq = tuple("s%d" % i for i in range(seq_bits))
        self.dp = tuple("d%d" % i for i in range(dp_bits))
        self.every = self.seq + self.dp
        self.l, self.x = self.seq[-2:]
        self.c = self.dp[-1]
        self.team = (self.l, self.x, self.c)
        self.far_seq = self.seq[:-2]
        self.far_dp = self.dp[:-1]
        self.far = self.far_seq + self.far_dp
        self.canon = self.far + self.team
        self.order = self.far_seq + (self.l,) + self.far_dp + (self.x,)

    def flipped(self, value, axes, dims):
        for axis, dim in zip(axes, dims):
            value = jnp.where(lax.axis_index(axis) == 1, jnp.flip(value, dim), value)
        return value

    def to_far_team(self, value):
        rows, width = value.shape
        parts = value.reshape((rows,) + (2,) * len(self.every) + (-1,))
        order = [0] + [1 + self.every.index(axis) for axis in self.canon] + [1 + len(self.every)]
        return parts.transpose(order).reshape(rows, width)

    def from_far_team(self, value):
        rows, width = value.shape
        parts = value.reshape((rows,) + (2,) * len(self.every) + (-1,))
        order = [0] + [1 + self.canon.index(axis) for axis in self.every] + [1 + len(self.every)]
        return parts.transpose(order).reshape(rows, width)

    def spread_order(self, width):
        own = jnp.arange(width, dtype=jnp.int32).reshape((2,) * len(self.canon) + (-1,))
        own = self.flipped(own, self.canon, range(len(self.canon)))
        axes = (self.c,) + tuple(reversed(self.order))
        return own.transpose([self.canon.index(axis) for axis in axes] + [len(self.canon)]).reshape(-1)

    def grow(self, block, axes):
        for axis in axes:
            block = jnp.concatenate([block, swap(block, axis)], axis=0)
        return block

    def gather_pieces(self, block):
        return self.core_pieces(block, swap(block, self.order[-1]))

    def core_pieces(self, block, other):
        return [block, other, swap(block, self.c), swap(other, self.c)]

    def far_team_rows(self, pieces):
        axes = (self.c,) + tuple(reversed(self.order))
        whole = jnp.concatenate(pieces, axis=0)
        whole = whole.reshape((2,) * len(axes) + (-1, whole.shape[-1]))
        whole = whole.transpose([axes.index(axis) for axis in self.canon] + [len(axes), len(axes) + 1])
        whole = self.flipped(whole, self.canon, range(len(self.canon)))
        return whole.reshape((-1, whole.shape[-1]))

    def spread_begin(self, pairs):
        half = pairs[0][0].shape[1] // 2
        away = jnp.concatenate([product_tn(one[:, half:], two).astype(BF16) for one, two in pairs], axis=1)
        kept = jnp.concatenate([product_tn(one[:, :half], two).astype(BF16) for one, two in pairs], axis=1)
        return (kept.astype(F32) + swap(away, self.c).astype(F32)).astype(BF16)

    def spread_step(self, total, axes):
        for axis in axes:
            half = total.shape[0] // 2
            total = total[:half].astype(F32) + swap(total[half:], axis).astype(F32)
            if axis != self.order[0]:
                total = total.astype(BF16)
        return total

    def spread_send(self, total, axis):
        half = total.shape[0] // 2
        return total[:half].astype(F32), swap(total[half:], axis).astype(F32)

    def near_far(self, key, value):
        pair = jnp.stack([key, value])[:, None]
        for axis in reversed(self.far_seq):
            pair = jnp.concatenate([pair, swap(pair, axis)], axis=1)
        return pair

    def near_gather(self, pair):
        key, value = pair[0][None], pair[1][None]
        key = jnp.concatenate([key, swap(key, self.x)], axis=0)
        key = jnp.stack([key, swap(key, self.l)], axis=0)
        value = jnp.concatenate([value, swap(value, self.l)], axis=0)
        value = jnp.stack([value, swap(value, self.x)], axis=1)
        return [one.reshape((-1,) + one.shape[3:]) for one in (key, value)]

    def near_sum(self, key, value):
        def step(total, dim, axis):
            total = total.astype(BF16)
            away = swap(lax.index_in_dim(total, 1, dim, False), axis).astype(F32)
            return lax.index_in_dim(total, 0, dim, False).astype(F32) + away

        shape = (2, 2) + (2,) * len(self.far_seq)
        key, value = [one.reshape(shape + one.shape[1:]) for one in (key, value)]
        key = step(step(key, 0, self.l), 0, self.x)
        value = step(step(value, 1, self.x), 0, self.l)
        pair = jnp.stack([key, value])
        for axis in self.far_seq:
            pair = step(pair, 1, axis)
        return pair

    def near_places(self):
        place = jnp.zeros((1,), jnp.int32)
        for axis in (self.l, self.x) + self.far_seq:
            bit = lax.axis_index(axis)
            weight = 2 ** (len(self.seq) - 1 - self.seq.index(axis))
            place = (place[:, None] + weight * jnp.stack([bit, 1 - bit])[None, :]).reshape(-1)
        return place

    def own_rows(self, sums, local_rows):
        size = 2 ** len(self.team)
        sums = jnp.concatenate([one.reshape(size, local_rows, -1) for one in sums], axis=1)
        moved = lax.all_to_all(sums, self.team, split_axis=0, concat_axis=0, tiled=True)
        return [
            jnp.concatenate([moved[at, first : first + local_rows] for at in range(size)], axis=1).astype(F32)
            for first in range(0, moved.shape[1], local_rows)
        ]

    def total(self, value):
        for axis in reversed(self.every):
            value = value + swap(value, axis)
        return value

    def team_map(self, own, function):
        def chunk_of(piece):
            return jnp.concatenate([piece, swap(piece, self.c)], axis=0)

        by_x, by_l = swap(own, self.x), swap(own, self.l)
        chunks = [chunk_of(own)]
        results = [function(chunks[0])]
        by_x, by_l, results = together(by_x, by_l, results)
        half = own.shape[0] // 2
        both = jnp.concatenate([swap(by_x[:half], self.l), swap(by_l[half:], self.x)], axis=0)
        for piece in (by_x, by_l, both):
            chunks.append(chunk_of(piece))
            results.append(function(chunks[-1]))
        return chunks, results

    def core_sums(self, chunks):
        sums = []
        for chunk in chunks:
            rows = chunk.shape[0] // 2
            other = swap(chunk[rows:].astype(BF16), self.c)
            sums.append(chunk[:rows].astype(F32) + other.astype(F32))
        return sums

    def team_near(self, sums):
        own, by_x, by_l, both = sums
        half = own.shape[0] // 2
        both = both.astype(BF16)
        first = by_l[:half] + swap(both[:half], self.x).astype(F32)
        second = by_x[half:] + swap(both[half:], self.l).astype(F32)
        by_l = jnp.concatenate([first, by_l[half:]], axis=0).astype(BF16)
        by_x = jnp.concatenate([by_x[:half], second], axis=0).astype(BF16)
        return own, by_l, by_x

    def team_far(self, sums):
        own, by_l, by_x = sums
        return own + swap(by_l, self.l).astype(F32) + swap(by_x, self.x).astype(F32)


def product_split(left, pieces):
    width = left.shape[1] // len(pieces)
    return sum(product(left[:, i * width : (i + 1) * width], one) for i, one in enumerate(pieces))


def product_nt_split(left, pieces):
    return jnp.concatenate([product_nt(left, one) for one in pieces], axis=1)


def reorder(values, matrix):
    rows = values.shape[0]
    high = lax.reduce_precision(values, 8, 7)
    parts = jnp.concatenate([high.astype(BF16), (values - high).astype(BF16)], axis=0)
    parts = product_nt(parts, matrix)
    return parts[:rows] + parts[rows:]


def passed_along(value, axes, count, steps):
    initial, last = (max(0, -steps), min(count, count - steps))
    return lax.ppermute(value, axes, [(source, source + steps) for source in range(initial, last)])


def body(
    plan,
    tokens,
    per_layer,
    positions,
    span_start,
    cotangent,
    query_weight,
    key_weight,
    value_weight,
    output_weight,
    laurel_left,
    laurel_right,
    gate_weight,
    up_weight,
    down_weight,
    side_gate,
    side_output,
    norm_input,
    norm_attn,
    norm_laurel,
    norm_before,
    norm_after,
    norm_layer,
    norm_query,
    norm_key,
):
    batch, block, width = tokens.shape
    rows = batch * block
    head_size = norm_query.shape[0]
    heads = query_weight.shape[1] // head_size
    kv_heads = key_weight.shape[1] // head_size
    group = heads // kv_heads
    seq_count = 2 ** len(plan.seq)
    local_rows = gate_weight.shape[0]
    team_size = 2 ** len(plan.team)
    hidden_own = gate_weight.shape[1] // team_size

    kvl_widths = [
        key_weight.shape[1],
        value_weight.shape[1],
        laurel_left.shape[1],
        laurel_right.shape[1],
    ]
    rest_widths = [output_weight.shape[1], side_gate.shape[1], side_output.shape[1]]
    feed_local = jnp.concatenate(
        [
            one.reshape(local_rows, team_size, hidden_own).transpose(1, 0, 2)
            for one in (gate_weight, up_weight, down_weight)
        ],
        axis=1,
    )
    feed_team = lax.all_to_all(feed_local, plan.team, split_axis=0, concat_axis=0, tiled=True)
    feed_team = feed_team.reshape(team_size, 3, local_rows, hidden_own).transpose(1, 0, 2, 3)
    block_widths = [sum(kvl_widths), query_weight.shape[1], sum(rest_widths)]
    attn_block = jnp.concatenate(
        [key_weight, value_weight, laurel_left, laurel_right, query_weight]
        + [output_weight, side_gate, side_output],
        axis=1,
    )
    attn_block = plan.grow(attn_block, plan.far_seq)
    attn_block, feed_team = together(attn_block, feed_team)
    feed_full = lax.all_gather(feed_team.reshape(-1, hidden_own), plan.far, axis=0, tiled=True)
    attn_block = plan.grow(attn_block, (plan.l,))
    kvl_block, query_block, rest_block = split_columns(attn_block, block_widths)
    kvl_block = plan.grow(kvl_block, plan.far_dp)
    query_block = plan.grow(query_block, plan.far_dp)
    kvl_full = plan.gather_pieces(kvl_block)
    kvl_full, rest_block = together(kvl_full, rest_block)
    query_full = plan.gather_pieces(query_block)
    rest_block = plan.grow(rest_block, plan.far_dp)
    right_full = plan.far_team_rows([one[:, -kvl_widths[3] :] for one in kvl_full])
    kvl_full = [one[:, : -kvl_widths[3]] for one in kvl_full]

    places = jnp.arange(width, dtype=jnp.int32)
    far_team = plan.to_far_team(places[None])[0]
    to_far_team = (places[:, None] == far_team[None, :]).astype(BF16)
    to_spread = (places[:, None] == plan.spread_order(width)[None, :]).astype(BF16)
    gains = jnp.stack([norm_input, norm_attn, norm_laurel, norm_before, norm_after, norm_layer])
    norm_input, norm_attn, norm_laurel, norm_before, norm_after, norm_layer = plan.to_far_team(gains)
    inputs = product(tokens.reshape(rows, width), to_far_team)
    upstream = product(cotangent.reshape(rows, width), to_far_team)
    side_in = per_layer.astype(F32).reshape(rows, -1)
    normed, pre_pull = jax.vjp(rms, inputs, norm_input)
    normed_low = normed.astype(BF16)
    normed_spread = product(normed_low, to_spread).astype(BF16)
    keys, values, latent = split_columns(
        product_split(normed_spread, kvl_full), kvl_widths[:3]
    )
    queries = product_split(normed_spread, query_full).reshape(batch, block, heads, head_size)
    keys = keys.reshape(batch, block, kv_heads, head_size)
    values = values.reshape(batch, block, kv_heads, head_size)
    latent_low = latent.astype(BF16)

    def head_prep(query_in, key_in, value_in, gain_query, gain_key):
        return (
            rotate(rms(query_in, gain_query), positions),
            rotate(rms(key_in, gain_key), positions),
            rms(value_in, 1.0),
        )

    (rot_query, rot_key, rot_value), prep_pull = jax.vjp(
        head_prep, queries, keys, values, norm_query, norm_key
    )
    query_low = rot_query.astype(BF16)
    key_low = rot_key.astype(BF16)
    value_low = rot_value.astype(BF16)
    left_count = WINDOW // block
    right_count = (SPAN + block - 2) // block
    offsets = list(range(left_count, 0, -1)) + [0] + list(range(-1, -right_count - 1, -1))
    whole_sequence = seq_count <= len(offsets) + 1
    seq_index = lax.axis_index(plan.seq)
    total_length = block * seq_count
    if whole_sequence:
        key_low, value_low, rest_block = together(key_low, value_low, rest_block)
        pair_low = plan.near_far(key_low, value_low)
        keys_all, values_all = [
            one.swapaxes(0, 1).reshape(batch, total_length, kv_heads, head_size)
            for one in plan.near_gather(pair_low)
        ]
        key_blocks = plan.near_places()
    else:
        pair_low = jnp.stack([key_low, value_low])
        gathered = [
            passed_along(pair_low, plan.seq, seq_count, offset) if offset else pair_low
            for offset in offsets
        ]
        keys_all, values_all = jnp.concatenate(gathered, axis=2)
        key_blocks = seq_index - jnp.array(offsets, dtype=jnp.int32)
    key_count = keys_all.shape[1]
    rest_other = swap(rest_block, plan.order[-1])
    keys_all, values_all, rest_other = together(keys_all, values_all, rest_other)
    rest_full = plan.core_pieces(rest_block, rest_other)
    query_places = seq_index * block + jnp.arange(block, dtype=jnp.int32)
    key_places = (key_blocks[:, None] * block + jnp.arange(block, dtype=jnp.int32)).reshape(-1)
    in_query = (query_places[None, :, None] >= span_start[:, None, :]) & (
        query_places[None, :, None] < span_start[:, None, :] + SPAN
    )
    in_key = (key_places[None, :, None] >= span_start[:, None, :]) & (
        key_places[None, :, None] < span_start[:, None, :] + SPAN
    )
    same = jnp.any(in_query[:, :, None, :] & in_key[:, None, :, :], axis=-1)
    near = (key_places[None, :] <= query_places[:, None]) & (
        query_places[:, None] - key_places[None, :] < WINDOW
    )
    valid = (key_places >= 0) & (key_places < total_length)
    allowed = (valid[None, None, :] & (near[None] | same))[:, None, None]
    query_group = query_low.reshape(batch, block, kv_heads, group, head_size)
    scores = jnp.einsum("btkgd,bskd->bkgts", query_group, keys_all, preferred_element_type=F32)
    masked = jnp.where(allowed, scores, -1e30)
    top = jnp.max(masked, axis=-1, keepdims=True)
    expo = jnp.exp(masked - top)
    total = jnp.sum(expo, axis=-1, keepdims=True)
    probs = expo / total
    probs_low = probs.astype(BF16)
    attended = jnp.einsum("bkgts,bskd->btkgd", probs_low, values_all, preferred_element_type=F32)
    attended_low = attended.reshape(rows, heads * head_size).astype(BF16)
    attended_low, feed_full = together(attended_low, feed_full)
    output_full = [one[:, : rest_widths[0]] for one in rest_full]
    side_full = plan.far_team_rows([one[:, rest_widths[0] :] for one in rest_full])
    side_gate_full, side_output_full = split_columns(side_full, rest_widths[1:])
    attn_proj = reorder(product_nt_split(attended_low, output_full), to_spread)
    laurel = product_nt(latent_low, right_full)
    (resid_one, feed_in), mid_pull = jax.vjp(
        middle, inputs, normed, attn_proj, laurel, norm_attn, norm_laurel, norm_before
    )

    feed_low = feed_in.astype(BF16)
    feed_full = feed_full.reshape(-1, 3, team_size * local_rows, hidden_own)
    gate_full, up_full, down_full = [feed_full[:, at].reshape(width, hidden_own) for at in range(3)]
    pulls = []
    hidden_chunks = []

    def forward_chunk(chunk):
        hidden, pull = jax.vjp(gate_act, product(chunk, gate_full), product(chunk, up_full))
        hidden_low = hidden.astype(BF16)
        pulls.append(pull)
        hidden_chunks.append(hidden_low)
        return product_nt(hidden_low, down_full).astype(BF16)

    feed_chunks, feed_parts = plan.team_map(feed_low, forward_chunk)
    feed_out = plan.team_far(plan.team_near(plan.core_sums(feed_parts)))

    resid_two, after_pull = jax.vjp(after_feed, resid_one, feed_out, norm_after)
    resid_low = resid_two.astype(BF16)
    side_pre = product(resid_low, side_gate_full)
    side_val, side_pull = jax.vjp(side_act, side_pre, side_in)
    side_low = side_val.astype(BF16)
    side_out = product_nt(side_low, side_output_full)
    result, final_pull = jax.vjp(finish, resid_two, side_out, norm_layer)
    output = product_nt(result.astype(BF16), to_far_team).astype(BF16).reshape(batch, block, width)

    d_resid_two, d_side_out, grad_norm_layer = final_pull(upstream)
    d_side_out_low = d_side_out.astype(BF16)
    d_side = product(d_side_out_low, side_output_full)
    d_side_pre, d_side_in = side_pull(d_side)
    d_side_pre_low = d_side_pre.astype(BF16)
    d_resid_two = d_resid_two + product_nt(d_side_pre_low, side_gate_full)
    d_resid_one, d_feed_out, grad_norm_after = after_pull(d_resid_two)

    d_out_low = d_feed_out.astype(BF16)
    d_gate_chunks = []
    d_up_chunks = []

    def backward_chunk(chunk):
        d_gate, d_up = pulls[len(d_gate_chunks)](product(chunk, down_full))
        d_gate_chunks.append(d_gate.astype(BF16))
        d_up_chunks.append(d_up.astype(BF16))
        part = product_nt(d_gate_chunks[-1], gate_full) + product_nt(d_up_chunks[-1], up_full)
        return part.astype(BF16)

    d_out_chunks, d_feed_parts = plan.team_map(d_out_low, backward_chunk)
    d_feed_sums = plan.core_sums(d_feed_parts)
    d_gate_chunks, d_up_chunks, feed_chunks, d_out_chunks, hidden_chunks, d_feed_sums = together(
        d_gate_chunks, d_up_chunks, feed_chunks, d_out_chunks, hidden_chunks, d_feed_sums
    )
    feed_all = jnp.concatenate(feed_chunks, axis=0)
    d_out_all = jnp.concatenate(d_out_chunks, axis=0)
    feed_terms = jnp.stack(
        [
            product_tn(left, jnp.concatenate(right, axis=0))
            .astype(BF16)
            .reshape(-1, team_size * local_rows, hidden_own)
            for left, right in (
                (feed_all, d_gate_chunks),
                (feed_all, d_up_chunks),
                (d_out_all, hidden_chunks),
            )
        ],
        axis=1,
    )
    d_feed_in = plan.team_far(plan.team_near(d_feed_sums))
    d_feed_in, feed_terms = together(d_feed_in, feed_terms)
    feed_sum = lax.psum_scatter(
        feed_terms.reshape(-1, hidden_own), plan.far, scatter_dimension=0, tiled=True
    )
    steps = tuple(reversed(plan.order))

    (
        d_inputs,
        d_normed,
        d_attn_proj,
        d_laurel,
        grad_norm_attn,
        grad_norm_laurel,
        grad_norm_before,
    ) = mid_pull((d_resid_one, d_feed_in))
    d_attn_low = d_attn_proj.astype(BF16)
    d_laurel_low = d_laurel.astype(BF16)
    d_attn_spread = product(d_attn_low, to_spread).astype(BF16)
    d_latent_low = product(d_laurel_low, right_full).astype(BF16)
    output_sum = plan.spread_begin([(d_attn_spread, attended_low)])
    d_attn_spread, output_sum = together(d_attn_spread, output_sum)
    d_attended_low = product_split(d_attn_spread, output_full).astype(BF16)
    output_sum = plan.spread_step(output_sum, steps[:1])

    d_att = d_attended_low.reshape(batch, block, kv_heads, group, head_size)
    d_values_all = jnp.einsum("bkgts,btkgd->bskd", probs_low, d_att, preferred_element_type=F32)
    d_probs = jnp.einsum("btkgd,bskd->bkgts", d_att, values_all, preferred_element_type=F32)
    d_scores = probs * (d_probs - jnp.sum(probs * d_probs, axis=-1, keepdims=True))
    d_scores_low = d_scores.astype(BF16)
    d_query_rot = jnp.einsum("bkgts,bskd->btkgd", d_scores_low, keys_all, preferred_element_type=F32)
    d_keys_all = jnp.einsum(
        "bkgts,btkgd->bskd", d_scores_low, query_group, preferred_element_type=F32
    )
    d_keys_all, d_values_all, d_query_rot, output_sum, side_left = together(
        d_keys_all,
        d_values_all,
        d_query_rot,
        output_sum,
        jnp.concatenate([resid_low, d_side_out_low], axis=0),
    )
    side_left = product(side_left, to_spread).astype(BF16)
    side_sum = plan.spread_begin([(side_left[:rows], d_side_pre_low), (side_left[rows:], side_low)])
    side_sum = plan.spread_step(side_sum, steps[:1])
    if whole_sequence:
        d_pair_total = plan.near_sum(
            *[
                one.reshape(batch, seq_count, block, kv_heads, head_size).swapaxes(0, 1)
                for one in (d_keys_all, d_values_all)
            ]
        )
    else:
        d_pairs = jnp.stack([d_keys_all, d_values_all])
        d_pair_total = d_pairs[:, :, left_count * block : (left_count + 1) * block]
        for position, offset in enumerate(offsets):
            if offset != 0:
                piece = d_pairs[:, :, position * block : (position + 1) * block].astype(BF16)
                moved = passed_along(piece, plan.seq, seq_count, -offset)
                d_pair_total = d_pair_total + moved.astype(F32)
    d_queries, d_keys, d_values, grad_norm_query, grad_norm_key = prep_pull(
        (d_query_rot.reshape(batch, block, heads, head_size), d_pair_total[0], d_pair_total[1])
    )
    d_queries_low = d_queries.reshape(rows, -1).astype(BF16)
    query_sum = plan.spread_begin([(normed_spread, d_queries_low)])
    query_sum = plan.spread_step(query_sum, steps[:1])
    d_spread = product_nt_split(d_queries_low, query_full)
    d_keys, d_values, query_sum, output_sum, side_sum, d_spread, feed_sum = together(
        d_keys, d_values, query_sum, output_sum, side_sum, d_spread, feed_sum
    )
    output_sum = jnp.concatenate([output_sum, side_sum], axis=1)
    d_kvl_low = jnp.concatenate(
        [
            d_keys.reshape(rows, -1).astype(BF16),
            d_values.reshape(rows, -1).astype(BF16),
            d_latent_low,
        ],
        axis=1,
    )
    laurel_spread = product(d_laurel_low, to_spread).astype(BF16)
    kvl_sum = plan.spread_begin([(normed_spread, d_kvl_low), (laurel_spread, latent_low)])
    kvl_sum, d_kvl_low = together(kvl_sum, d_kvl_low)
    query_kept, query_away = plan.spread_send(query_sum, steps[1])
    output_kept, output_away = plan.spread_send(output_sum, steps[1])
    kvl_sum = plan.spread_step(kvl_sum, steps[:1])
    kvl_sum, query_kept, output_kept, feed_sum = together(
        kvl_sum, query_kept, output_kept, feed_sum
    )
    grad_gate, grad_up, grad_down = plan.own_rows(jnp.split(feed_sum, 3), local_rows)
    query_sum = (query_kept + query_away).astype(BF16)
    output_sum = (output_kept + output_away).astype(BF16)
    kvl_sum = plan.spread_step(kvl_sum, steps[1:2])
    query_sum = plan.spread_step(query_sum, steps[2:3])
    output_sum = plan.spread_step(output_sum, steps[2:3])
    d_spread = d_spread + product_nt_split(d_kvl_low, kvl_full)
    d_normed = d_normed + reorder(d_spread, to_spread)
    d_inputs_norm, grad_norm_input = pre_pull(d_normed)
    grad_tokens = reorder(d_inputs + d_inputs_norm, to_far_team).reshape(batch, block, width)
    grad_side = d_side_in.reshape(batch, block, -1)
    norm_grads = jnp.stack(
        [
            grad_norm_input,
            grad_norm_attn,
            grad_norm_laurel,
            grad_norm_before,
            grad_norm_after,
            grad_norm_layer,
        ]
    )
    gain_grads = jnp.concatenate(
        [plan.from_far_team(norm_grads).reshape(-1), grad_norm_query, grad_norm_key]
    )
    gain_grads, query_sum, output_sum, kvl_sum = together(
        gain_grads, query_sum, output_sum, kvl_sum
    )
    grad_query = plan.spread_step(query_sum, steps[3:])
    output_sum = plan.spread_step(output_sum, steps[3:])
    grad_output, grad_side_gate, grad_side_output = split_columns(output_sum, rest_widths)
    grad_key, grad_value, grad_left, grad_right = split_columns(
        plan.spread_step(kvl_sum, steps[2:]), kvl_widths
    )
    gain_grads = plan.total(gain_grads)
    gain_parts = split_columns(gain_grads, [width] * 6 + [head_size] * 2)
    return (
        output,
        grad_tokens,
        grad_side,
        grad_query,
        grad_key,
        grad_value,
        grad_output,
        grad_left,
        grad_right,
        grad_gate,
        grad_up,
        grad_down,
        grad_side_gate,
        grad_side_output,
    ) + tuple(gain_parts)


def solution(mesh):
    seq_bits = int(math.log2(mesh.shape["seq"]))
    dp_bits = int(math.log2(mesh.shape["dp"]))
    plan = Plan(seq_bits, dp_bits)
    binary = Mesh(mesh.devices.reshape((2,) * (seq_bits + dp_bits)), plan.every)
    token_spec = P(plan.dp, plan.seq, None)
    weight_spec = P(plan.every, None)

    def step(*arrays):
        return body(plan, *arrays)

    return jax.shard_map(
        step,
        mesh=binary,
        in_specs=(token_spec, token_spec, P(plan.dp, plan.seq), P(plan.dp, None), token_spec)
        + (weight_spec,) * 11
        + (P(),) * 8,
        out_specs=(token_spec,) * 3 + (weight_spec,) * 11 + (P(),) * 8,
        check_vma=False,
    )
```

```python
import math

import jax
import jax.numpy as jnp
from jax import lax
from jax.sharding import Mesh
from jax.sharding import PartitionSpec as P

WINDOW = 512
SPAN = 256
EPS = 1e-06
HALF_ROOT = 1.0 / math.sqrt(2.0)
F32 = jnp.float32
BF16 = jnp.bfloat16


def rms(values, gain):
    return values * lax.rsqrt(jnp.mean(values * values, axis=-1, keepdims=True) + EPS) * gain


def gelu_tanh(values):
    return jax.nn.gelu(values, approximate=True)


def product(left, right):
    return jnp.dot(left, right, preferred_element_type=F32)


def product_nt(left, right):
    return lax.dot_general(left, right, (((1,), (1,)), ((), ())), preferred_element_type=F32)


def product_tn(left, right):
    return lax.dot_general(left, right, (((0,), (0,)), ((), ())), preferred_element_type=F32)


def rotate(values, places):
    size = values.shape[-1]
    half = size // 2
    freq = 10000.0 ** (-(2.0 * jnp.arange(half, dtype=F32)) / size)
    angle = places.astype(F32)[..., None] * freq
    cosine = jnp.cos(angle)[..., None, :]
    sine = jnp.sin(angle)[..., None, :]
    first = values[..., :half]
    second = values[..., half:]
    return jnp.concatenate(
        [first * cosine - second * sine, second * cosine + first * sine], axis=-1
    )


def middle(inputs, normed, attn_proj, laurel, gain_attn, gain_laurel, gain_before):
    resid = (inputs + rms(attn_proj, gain_attn) + normed + rms(laurel, gain_laurel)) * HALF_ROOT
    return (resid, rms(resid, gain_before))


def gate_act(gate_val, up_val):
    return gelu_tanh(gate_val) * up_val


def after_feed(resid_one, feed_out, gain_after):
    return resid_one + rms(feed_out, gain_after)


def side_act(side_pre, side_in):
    return gelu_tanh(side_pre) * side_in


def finish(resid_two, side_out, gain_layer):
    return resid_two + rms(side_out, gain_layer)


def swap(value, axis):
    return lax.ppermute(value, axis, [(0, 1), (1, 0)])


def together(*values):
    return lax.optimization_barrier(values)


def split_columns(whole, widths):
    pieces = []
    offset = 0
    for width_one in widths:
        pieces.append(whole[..., offset : offset + width_one])
        offset = offset + width_one
    return pieces


class Plan:
    def __init__(self, seq_bits, dp_bits):
        self.seq = tuple("s%d" % i for i in range(seq_bits))
        self.dp = tuple("d%d" % i for i in range(dp_bits))
        self.every = self.seq + self.dp
        self.l, self.x = self.seq[-2:]
        self.c = self.dp[-1]
        self.team = (self.l, self.x, self.c)
        self.far_seq = self.seq[:-2]
        self.far_dp = self.dp[:-1]
        self.far = self.far_seq + self.far_dp
        self.canon = self.far + self.team
        self.order = self.far_seq + (self.l,) + self.far_dp + (self.x,)

    def flipped(self, value, axes, dims):
        for axis, dim in zip(axes, dims):
            value = jnp.where(lax.axis_index(axis) == 1, jnp.flip(value, dim), value)
        return value

    def to_far_team(self, value):
        rows, width = value.shape
        parts = value.reshape((rows,) + (2,) * len(self.every) + (-1,))
        order = [0] + [1 + self.every.index(axis) for axis in self.canon] + [1 + len(self.every)]
        return parts.transpose(order).reshape(rows, width)

    def from_far_team(self, value):
        rows, width = value.shape
        parts = value.reshape((rows,) + (2,) * len(self.every) + (-1,))
        order = [0] + [1 + self.canon.index(axis) for axis in self.every] + [1 + len(self.every)]
        return parts.transpose(order).reshape(rows, width)

    def spread_order(self, width):
        own = jnp.arange(width, dtype=jnp.int32).reshape((2,) * len(self.canon) + (-1,))
        own = self.flipped(own, self.canon, range(len(self.canon)))
        axes = (self.c,) + tuple(reversed(self.order))
        return own.transpose([self.canon.index(axis) for axis in axes] + [len(self.canon)]).reshape(-1)

    def grow(self, block, axes):
        for axis in axes:
            block = jnp.concatenate([block, swap(block, axis)], axis=0)
        return block

    def gather_pieces(self, block):
        return self.core_pieces(block, swap(block, self.order[-1]))

    def core_pieces(self, block, other):
        return [block, other, swap(block, self.c), swap(other, self.c)]

    def far_team_rows(self, pieces):
        axes = (self.c,) + tuple(reversed(self.order))
        whole = jnp.concatenate(pieces, axis=0)
        whole = whole.reshape((2,) * len(axes) + (-1, whole.shape[-1]))
        whole = whole.transpose([axes.index(axis) for axis in self.canon] + [len(axes), len(axes) + 1])
        whole = self.flipped(whole, self.canon, range(len(self.canon)))
        return whole.reshape((-1, whole.shape[-1]))

    def spread_begin(self, pairs):
        half = pairs[0][0].shape[1] // 2
        away = jnp.concatenate([product_tn(one[:, half:], two).astype(BF16) for one, two in pairs], axis=1)
        kept = jnp.concatenate([product_tn(one[:, :half], two).astype(BF16) for one, two in pairs], axis=1)
        return (kept.astype(F32) + swap(away, self.c).astype(F32)).astype(BF16)

    def spread_step(self, total, axes):
        for axis in axes:
            half = total.shape[0] // 2
            total = total[:half].astype(F32) + swap(total[half:], axis).astype(F32)
            if axis != self.order[0]:
                total = total.astype(BF16)
        return total

    def spread_send(self, total, axis):
        half = total.shape[0] // 2
        return total[:half].astype(F32), swap(total[half:], axis).astype(F32)

    def near_far(self, key, value):
        pair = jnp.stack([key, value])[:, None]
        for axis in reversed(self.far_seq):
            pair = jnp.concatenate([pair, swap(pair, axis)], axis=1)
        return pair

    def near_gather(self, pair):
        key, value = pair[0][None], pair[1][None]
        key = jnp.concatenate([key, swap(key, self.x)], axis=0)
        key = jnp.stack([key, swap(key, self.l)], axis=0)
        value = jnp.concatenate([value, swap(value, self.l)], axis=0)
        value = jnp.stack([value, swap(value, self.x)], axis=1)
        return [one.reshape((-1,) + one.shape[3:]) for one in (key, value)]

    def near_sum(self, key, value):
        def step(total, dim, axis):
            total = total.astype(BF16)
            away = swap(lax.index_in_dim(total, 1, dim, False), axis).astype(F32)
            return lax.index_in_dim(total, 0, dim, False).astype(F32) + away

        shape = (2, 2) + (2,) * len(self.far_seq)
        key, value = [one.reshape(shape + one.shape[1:]) for one in (key, value)]
        key = step(step(key, 0, self.l), 0, self.x)
        value = step(step(value, 1, self.x), 0, self.l)
        pair = jnp.stack([key, value])
        for axis in self.far_seq:
            pair = step(pair, 1, axis)
        return pair

    def near_places(self):
        place = jnp.zeros((1,), jnp.int32)
        for axis in (self.l, self.x) + self.far_seq:
            bit = lax.axis_index(axis)
            weight = 2 ** (len(self.seq) - 1 - self.seq.index(axis))
            place = (place[:, None] + weight * jnp.stack([bit, 1 - bit])[None, :]).reshape(-1)
        return place

    def to_rows(self, sums, local_rows):
        size = 2 ** len(self.team)
        sums = jnp.concatenate([one.reshape(size, local_rows, -1) for one in sums], axis=1)
        return lax.all_to_all(sums, self.team, split_axis=0, concat_axis=0, tiled=True)

    def total(self, value):
        for axis in reversed(self.every):
            value = value + swap(value, axis)
        return value

    def team_map(self, own, function):
        def chunk_of(piece):
            return jnp.concatenate([piece, swap(piece, self.c)], axis=0)

        by_x, by_l = swap(own, self.x), swap(own, self.l)
        chunks = [chunk_of(own)]
        results = [function(chunks[0])]
        by_x, by_l, results = together(by_x, by_l, results)
        half = own.shape[0] // 2
        both = jnp.concatenate([swap(by_x[:half], self.l), swap(by_l[half:], self.x)], axis=0)
        for piece in (by_x, by_l, both):
            chunks.append(chunk_of(piece))
            results.append(function(chunks[-1]))
        return chunks, results

    def core_sums(self, chunks):
        sums = []
        for chunk in chunks:
            rows = chunk.shape[0] // 2
            other = swap(chunk[rows:].astype(BF16), self.c)
            sums.append(chunk[:rows].astype(F32) + other.astype(F32))
        return sums

    def team_near(self, sums):
        own, by_x, by_l, both = sums
        half = own.shape[0] // 2
        both = both.astype(BF16)
        first = by_l[:half] + swap(both[:half], self.x).astype(F32)
        second = by_x[half:] + swap(both[half:], self.l).astype(F32)
        by_l = jnp.concatenate([first, by_l[half:]], axis=0).astype(BF16)
        by_x = jnp.concatenate([by_x[:half], second], axis=0).astype(BF16)
        return own, by_l, by_x

    def team_far(self, sums):
        own, by_l, by_x = sums
        return own + swap(by_l, self.l).astype(F32) + swap(by_x, self.x).astype(F32)


def product_split(left, pieces):
    width = left.shape[1] // len(pieces)
    return sum(product(left[:, i * width : (i + 1) * width], one) for i, one in enumerate(pieces))


def product_nt_split(left, pieces):
    return jnp.concatenate([product_nt(left, one) for one in pieces], axis=1)


def reorder(values, matrix):
    rows = values.shape[0]
    high = lax.reduce_precision(values, 8, 7)
    parts = jnp.concatenate([high.astype(BF16), (values - high).astype(BF16)], axis=0)
    parts = product_nt(parts, matrix)
    return parts[:rows] + parts[rows:]


def passed_along(value, axes, count, steps):
    initial, last = (max(0, -steps), min(count, count - steps))
    return lax.ppermute(value, axes, [(source, source + steps) for source in range(initial, last)])


def body(
    plan,
    tokens,
    per_layer,
    positions,
    span_start,
    cotangent,
    query_weight,
    key_weight,
    value_weight,
    output_weight,
    laurel_left,
    laurel_right,
    gate_weight,
    up_weight,
    down_weight,
    side_gate,
    side_output,
    norm_input,
    norm_attn,
    norm_laurel,
    norm_before,
    norm_after,
    norm_layer,
    norm_query,
    norm_key,
):
    batch, block, width = tokens.shape
    rows = batch * block
    head_size = norm_query.shape[0]
    heads = query_weight.shape[1] // head_size
    kv_heads = key_weight.shape[1] // head_size
    group = heads // kv_heads
    seq_count = 2 ** len(plan.seq)
    local_rows = gate_weight.shape[0]
    team_size = 2 ** len(plan.team)
    hidden_own = gate_weight.shape[1] // team_size

    kvl_widths = [
        key_weight.shape[1],
        value_weight.shape[1],
        laurel_left.shape[1],
        laurel_right.shape[1],
    ]
    rest_widths = [output_weight.shape[1], side_gate.shape[1], side_output.shape[1]]
    feed_local = jnp.concatenate(
        [
            one.reshape(local_rows, team_size, hidden_own).transpose(1, 0, 2)
            for one in (gate_weight, up_weight, down_weight)
        ],
        axis=1,
    )
    feed_team = lax.all_to_all(feed_local, plan.team, split_axis=0, concat_axis=0, tiled=True)
    feed_team = feed_team.reshape(team_size, 3, local_rows, hidden_own).transpose(1, 0, 2, 3)
    block_widths = [sum(kvl_widths), query_weight.shape[1], sum(rest_widths)]
    attn_block = jnp.concatenate(
        [key_weight, value_weight, laurel_left, laurel_right, query_weight]
        + [output_weight, side_gate, side_output],
        axis=1,
    )
    attn_block = plan.grow(attn_block, plan.far_seq)
    attn_block, feed_team = together(attn_block, feed_team)
    feed_full = lax.all_gather(feed_team.reshape(-1, hidden_own), plan.far, axis=0, tiled=True)
    attn_block = plan.grow(attn_block, (plan.l,))
    kvl_block, query_block, rest_block = split_columns(attn_block, block_widths)
    kvl_block = plan.grow(kvl_block, plan.far_dp)
    query_block = plan.grow(query_block, plan.far_dp)
    kvl_full = plan.gather_pieces(kvl_block)
    kvl_full, rest_block = together(kvl_full, rest_block)
    query_full = plan.gather_pieces(query_block)
    rest_block = plan.grow(rest_block, plan.far_dp)
    right_full = plan.far_team_rows([one[:, -kvl_widths[3] :] for one in kvl_full])
    kvl_full = [one[:, : -kvl_widths[3]] for one in kvl_full]

    places = jnp.arange(width, dtype=jnp.int32)
    far_team = plan.to_far_team(places[None])[0]
    to_far_team = (places[:, None] == far_team[None, :]).astype(BF16)
    to_spread = (places[:, None] == plan.spread_order(width)[None, :]).astype(BF16)
    gains = jnp.stack([norm_input, norm_attn, norm_laurel, norm_before, norm_after, norm_layer])
    norm_input, norm_attn, norm_laurel, norm_before, norm_after, norm_layer = plan.to_far_team(gains)
    inputs = product(tokens.reshape(rows, width), to_far_team)
    upstream = product(cotangent.reshape(rows, width), to_far_team)
    side_in = per_layer.astype(F32).reshape(rows, -1)
    normed, pre_pull = jax.vjp(rms, inputs, norm_input)
    normed_low = normed.astype(BF16)
    normed_spread = product(normed_low, to_spread).astype(BF16)
    keys, values, latent = split_columns(
        product_split(normed_spread, kvl_full), kvl_widths[:3]
    )
    queries = product_split(normed_spread, query_full).reshape(batch, block, heads, head_size)
    keys = keys.reshape(batch, block, kv_heads, head_size)
    values = values.reshape(batch, block, kv_heads, head_size)
    latent_low = latent.astype(BF16)

    def head_prep(query_in, key_in, value_in, gain_query, gain_key):
        return (
            rotate(rms(query_in, gain_query), positions),
            rotate(rms(key_in, gain_key), positions),
            rms(value_in, 1.0),
        )

    (rot_query, rot_key, rot_value), prep_pull = jax.vjp(
        head_prep, queries, keys, values, norm_query, norm_key
    )
    query_low = rot_query.astype(BF16)
    key_low = rot_key.astype(BF16)
    value_low = rot_value.astype(BF16)
    left_count = WINDOW // block
    right_count = (SPAN + block - 2) // block
    offsets = list(range(left_count, 0, -1)) + [0] + list(range(-1, -right_count - 1, -1))
    whole_sequence = seq_count <= len(offsets) + 1
    seq_index = lax.axis_index(plan.seq)
    total_length = block * seq_count
    if whole_sequence:
        key_low, value_low, rest_block = together(key_low, value_low, rest_block)
        pair_low = plan.near_far(key_low, value_low)
        keys_all, values_all = [
            one.swapaxes(0, 1).reshape(batch, total_length, kv_heads, head_size)
            for one in plan.near_gather(pair_low)
        ]
        key_blocks = plan.near_places()
    else:
        pair_low = jnp.stack([key_low, value_low])
        gathered = [
            passed_along(pair_low, plan.seq, seq_count, offset) if offset else pair_low
            for offset in offsets
        ]
        keys_all, values_all = jnp.concatenate(gathered, axis=2)
        key_blocks = seq_index - jnp.array(offsets, dtype=jnp.int32)
    key_count = keys_all.shape[1]
    rest_other = swap(rest_block, plan.order[-1])
    keys_all, values_all, rest_other = together(keys_all, values_all, rest_other)
    rest_full = plan.core_pieces(rest_block, rest_other)
    query_places = seq_index * block + jnp.arange(block, dtype=jnp.int32)
    key_places = (key_blocks[:, None] * block + jnp.arange(block, dtype=jnp.int32)).reshape(-1)
    in_query = (query_places[None, :, None] >= span_start[:, None, :]) & (
        query_places[None, :, None] < span_start[:, None, :] + SPAN
    )
    in_key = (key_places[None, :, None] >= span_start[:, None, :]) & (
        key_places[None, :, None] < span_start[:, None, :] + SPAN
    )
    same = jnp.any(in_query[:, :, None, :] & in_key[:, None, :, :], axis=-1)
    near = (key_places[None, :] <= query_places[:, None]) & (
        query_places[:, None] - key_places[None, :] < WINDOW
    )
    valid = (key_places >= 0) & (key_places < total_length)
    allowed = (valid[None, None, :] & (near[None] | same))[:, None, None]
    query_group = query_low.reshape(batch, block, kv_heads, group, head_size)
    scores = jnp.einsum("btkgd,bskd->bkgts", query_group, keys_all, preferred_element_type=F32)
    masked = jnp.where(allowed, scores, -1e30)
    top = jnp.max(masked, axis=-1, keepdims=True)
    expo = jnp.exp(masked - top)
    total = jnp.sum(expo, axis=-1, keepdims=True)
    probs = expo / total
    probs_low = probs.astype(BF16)
    attended = jnp.einsum("bkgts,bskd->btkgd", probs_low, values_all, preferred_element_type=F32)
    attended_low = attended.reshape(rows, heads * head_size).astype(BF16)
    attended_low, feed_full = together(attended_low, feed_full)
    output_full = [one[:, : rest_widths[0]] for one in rest_full]
    side_full = plan.far_team_rows([one[:, rest_widths[0] :] for one in rest_full])
    side_gate_full, side_output_full = split_columns(side_full, rest_widths[1:])
    attn_proj = reorder(product_nt_split(attended_low, output_full), to_spread)
    laurel = product_nt(latent_low, right_full)
    (resid_one, feed_in), mid_pull = jax.vjp(
        middle, inputs, normed, attn_proj, laurel, norm_attn, norm_laurel, norm_before
    )

    feed_low = feed_in.astype(BF16)
    feed_full = feed_full.reshape(-1, 3, team_size * local_rows, hidden_own)
    gate_full, up_full, down_full = [feed_full[:, at].reshape(width, hidden_own) for at in range(3)]
    pulls = []
    hidden_chunks = []

    def forward_chunk(chunk):
        hidden, pull = jax.vjp(gate_act, product(chunk, gate_full), product(chunk, up_full))
        hidden_low = hidden.astype(BF16)
        pulls.append(pull)
        hidden_chunks.append(hidden_low)
        return product_nt(hidden_low, down_full).astype(BF16)

    feed_chunks, feed_parts = plan.team_map(feed_low, forward_chunk)
    feed_out = plan.team_far(plan.team_near(plan.core_sums(feed_parts)))

    resid_two, after_pull = jax.vjp(after_feed, resid_one, feed_out, norm_after)
    resid_low = resid_two.astype(BF16)
    side_pre = product(resid_low, side_gate_full)
    side_val, side_pull = jax.vjp(side_act, side_pre, side_in)
    side_low = side_val.astype(BF16)
    side_out = product_nt(side_low, side_output_full)
    result, final_pull = jax.vjp(finish, resid_two, side_out, norm_layer)
    output = product_nt(result.astype(BF16), to_far_team).astype(BF16).reshape(batch, block, width)

    d_resid_two, d_side_out, grad_norm_layer = final_pull(upstream)
    d_side_out_low = d_side_out.astype(BF16)
    d_side = product(d_side_out_low, side_output_full)
    d_side_pre, d_side_in = side_pull(d_side)
    d_side_pre_low = d_side_pre.astype(BF16)
    d_resid_two = d_resid_two + product_nt(d_side_pre_low, side_gate_full)
    d_resid_one, d_feed_out, grad_norm_after = after_pull(d_resid_two)

    d_out_low = d_feed_out.astype(BF16)
    d_gate_chunks = []
    d_up_chunks = []

    def backward_chunk(chunk):
        d_gate, d_up = pulls[len(d_gate_chunks)](product(chunk, down_full))
        d_gate_chunks.append(d_gate.astype(BF16))
        d_up_chunks.append(d_up.astype(BF16))
        part = product_nt(d_gate_chunks[-1], gate_full) + product_nt(d_up_chunks[-1], up_full)
        return part.astype(BF16)

    d_out_chunks, d_feed_parts = plan.team_map(d_out_low, backward_chunk)
    d_feed_sums = plan.core_sums(d_feed_parts)
    d_gate_chunks, d_up_chunks, feed_chunks, d_out_chunks, hidden_chunks, d_feed_sums = together(
        d_gate_chunks, d_up_chunks, feed_chunks, d_out_chunks, hidden_chunks, d_feed_sums
    )
    feed_all = jnp.concatenate(feed_chunks, axis=0)
    d_out_all = jnp.concatenate(d_out_chunks, axis=0)
    feed_terms = jnp.stack(
        [
            product_tn(left, jnp.concatenate(right, axis=0))
            .astype(BF16)
            .reshape(-1, team_size * local_rows, hidden_own)
            for left, right in (
                (feed_all, d_gate_chunks),
                (feed_all, d_up_chunks),
                (d_out_all, hidden_chunks),
            )
        ],
        axis=1,
    )
    d_feed_in = plan.team_far(plan.team_near(d_feed_sums))
    d_feed_in, feed_terms = together(d_feed_in, feed_terms)
    feed_sum = lax.psum_scatter(
        feed_terms.reshape(-1, hidden_own), plan.far, scatter_dimension=0, tiled=True
    )
    steps = tuple(reversed(plan.order))

    (
        d_inputs,
        d_normed,
        d_attn_proj,
        d_laurel,
        grad_norm_attn,
        grad_norm_laurel,
        grad_norm_before,
    ) = mid_pull((d_resid_one, d_feed_in))
    d_attn_low = d_attn_proj.astype(BF16)
    d_laurel_low = d_laurel.astype(BF16)
    d_attn_spread = product(d_attn_low, to_spread).astype(BF16)
    d_latent_low = product(d_laurel_low, right_full).astype(BF16)
    output_sum = plan.spread_begin([(d_attn_spread, attended_low)])
    d_attn_spread, output_sum = together(d_attn_spread, output_sum)
    d_attended_low = product_split(d_attn_spread, output_full).astype(BF16)
    output_sum = plan.spread_step(output_sum, steps[:1])

    d_att = d_attended_low.reshape(batch, block, kv_heads, group, head_size)
    d_values_all = jnp.einsum("bkgts,btkgd->bskd", probs_low, d_att, preferred_element_type=F32)
    d_probs = jnp.einsum("btkgd,bskd->bkgts", d_att, values_all, preferred_element_type=F32)
    d_scores = probs * (d_probs - jnp.sum(probs * d_probs, axis=-1, keepdims=True))
    d_scores_low = d_scores.astype(BF16)
    d_query_rot = jnp.einsum("bkgts,bskd->btkgd", d_scores_low, keys_all, preferred_element_type=F32)
    d_keys_all = jnp.einsum(
        "bkgts,btkgd->bskd", d_scores_low, query_group, preferred_element_type=F32
    )
    d_keys_all, d_values_all, d_query_rot, output_sum, side_left = together(
        d_keys_all,
        d_values_all,
        d_query_rot,
        output_sum,
        jnp.concatenate([resid_low, d_side_out_low], axis=0),
    )
    side_left = product(side_left, to_spread).astype(BF16)
    side_sum = plan.spread_begin([(side_left[:rows], d_side_pre_low), (side_left[rows:], side_low)])
    side_sum = plan.spread_step(side_sum, steps[:1])
    if whole_sequence:
        d_pair_total = plan.near_sum(
            *[
                one.reshape(batch, seq_count, block, kv_heads, head_size).swapaxes(0, 1)
                for one in (d_keys_all, d_values_all)
            ]
        )
    else:
        d_pairs = jnp.stack([d_keys_all, d_values_all])
        d_pair_total = d_pairs[:, :, left_count * block : (left_count + 1) * block]
        for position, offset in enumerate(offsets):
            if offset != 0:
                piece = d_pairs[:, :, position * block : (position + 1) * block].astype(BF16)
                moved = passed_along(piece, plan.seq, seq_count, -offset)
                d_pair_total = d_pair_total + moved.astype(F32)
    d_queries, d_keys, d_values, grad_norm_query, grad_norm_key = prep_pull(
        (d_query_rot.reshape(batch, block, heads, head_size), d_pair_total[0], d_pair_total[1])
    )
    d_queries_low = d_queries.reshape(rows, -1).astype(BF16)
    query_sum = plan.spread_begin([(normed_spread, d_queries_low)])
    query_sum = plan.spread_step(query_sum, steps[:1])
    d_spread = product_nt_split(d_queries_low, query_full)
    d_keys, d_values, query_sum, output_sum, side_sum, d_spread, feed_sum = together(
        d_keys, d_values, query_sum, output_sum, side_sum, d_spread, feed_sum
    )
    output_sum = jnp.concatenate([output_sum, side_sum], axis=1)
    d_kvl_low = jnp.concatenate(
        [
            d_keys.reshape(rows, -1).astype(BF16),
            d_values.reshape(rows, -1).astype(BF16),
            d_latent_low,
        ],
        axis=1,
    )
    laurel_spread = product(d_laurel_low, to_spread).astype(BF16)
    kvl_sum = plan.spread_begin([(normed_spread, d_kvl_low), (laurel_spread, latent_low)])
    kvl_sum, d_kvl_low = together(kvl_sum, d_kvl_low)
    query_kept, query_away = plan.spread_send(query_sum, steps[1])
    output_kept, output_away = plan.spread_send(output_sum, steps[1])
    kvl_sum = plan.spread_step(kvl_sum, steps[:1])
    feed_rows = plan.to_rows(jnp.split(feed_sum, 3), local_rows)
    kvl_sum, query_kept, output_kept = together(kvl_sum, query_kept, output_kept)
    query_sum = (query_kept + query_away).astype(BF16)
    output_sum = (output_kept + output_away).astype(BF16)
    kvl_sum = plan.spread_step(kvl_sum, steps[1:2])
    query_sum = plan.spread_step(query_sum, steps[2:3])
    output_sum = plan.spread_step(output_sum, steps[2:3])
    d_spread = d_spread + product_nt_split(d_kvl_low, kvl_full)
    d_normed = d_normed + reorder(d_spread, to_spread)
    d_inputs_norm, grad_norm_input = pre_pull(d_normed)
    grad_tokens = reorder(d_inputs + d_inputs_norm, to_far_team).reshape(batch, block, width)
    grad_side = d_side_in.reshape(batch, block, -1)
    norm_grads = jnp.stack(
        [
            grad_norm_input,
            grad_norm_attn,
            grad_norm_laurel,
            grad_norm_before,
            grad_norm_after,
            grad_norm_layer,
        ]
    )
    gain_grads = jnp.concatenate(
        [plan.from_far_team(norm_grads).reshape(-1), grad_norm_query, grad_norm_key]
    )
    grad_query = plan.spread_step(query_sum, steps[3:])
    output_sum = plan.spread_step(output_sum, steps[3:])
    kvl_sum = plan.spread_step(kvl_sum, steps[2:3])
    gain_grads, grad_query, output_sum, kvl_sum, feed_rows = together(
        gain_grads, grad_query, output_sum, kvl_sum, feed_rows
    )
    grad_gate, grad_up, grad_down = [
        jnp.concatenate(
            [feed_rows[at, first : first + local_rows] for at in range(team_size)], axis=1
        ).astype(F32)
        for first in range(0, 3 * local_rows, local_rows)
    ]
    grad_output, grad_side_gate, grad_side_output = split_columns(output_sum, rest_widths)
    grad_key, grad_value, grad_left, grad_right = split_columns(
        plan.spread_step(kvl_sum, steps[3:]), kvl_widths
    )
    gain_grads = plan.total(gain_grads)
    gain_parts = split_columns(gain_grads, [width] * 6 + [head_size] * 2)
    return (
        output,
        grad_tokens,
        grad_side,
        grad_query,
        grad_key,
        grad_value,
        grad_output,
        grad_left,
        grad_right,
        grad_gate,
        grad_up,
        grad_down,
        grad_side_gate,
        grad_side_output,
    ) + tuple(gain_parts)


def solution(mesh):
    seq_bits = int(math.log2(mesh.shape["seq"]))
    dp_bits = int(math.log2(mesh.shape["dp"]))
    plan = Plan(seq_bits, dp_bits)
    binary = Mesh(mesh.devices.reshape((2,) * (seq_bits + dp_bits)), plan.every)
    token_spec = P(plan.dp, plan.seq, None)
    weight_spec = P(plan.every, None)

    def step(*arrays):
        return body(plan, *arrays)

    return jax.shard_map(
        step,
        mesh=binary,
        in_specs=(token_spec, token_spec, P(plan.dp, plan.seq), P(plan.dp, None), token_spec)
        + (weight_spec,) * 11
        + (P(),) * 8,
        out_specs=(token_spec,) * 3 + (weight_spec,) * 11 + (P(),) * 8,
        check_vma=False,
    )
```

```python
import math

import jax
import jax.numpy as jnp
from jax import lax
from jax.sharding import Mesh
from jax.sharding import PartitionSpec as P

WINDOW = 512
SPAN = 256
EPS = 1e-06
HALF_ROOT = 1.0 / math.sqrt(2.0)
F32 = jnp.float32
BF16 = jnp.bfloat16


def rms(values, gain):
    return values * lax.rsqrt(jnp.mean(values * values, axis=-1, keepdims=True) + EPS) * gain


def gelu_tanh(values):
    return jax.nn.gelu(values, approximate=True)


def product(left, right):
    return jnp.dot(left, right, preferred_element_type=F32)


def product_nt(left, right):
    return lax.dot_general(left, right, (((1,), (1,)), ((), ())), preferred_element_type=F32)


def product_tn(left, right):
    return lax.dot_general(left, right, (((0,), (0,)), ((), ())), preferred_element_type=F32)


def rotate(values, places):
    size = values.shape[-1]
    half = size // 2
    freq = 10000.0 ** (-(2.0 * jnp.arange(half, dtype=F32)) / size)
    angle = places.astype(F32)[..., None] * freq
    cosine = jnp.cos(angle)[..., None, :]
    sine = jnp.sin(angle)[..., None, :]
    first = values[..., :half]
    second = values[..., half:]
    return jnp.concatenate(
        [first * cosine - second * sine, second * cosine + first * sine], axis=-1
    )


def middle(inputs, normed, attn_proj, laurel, gain_attn, gain_laurel, gain_before):
    resid = (inputs + rms(attn_proj, gain_attn) + normed + rms(laurel, gain_laurel)) * HALF_ROOT
    return (resid, rms(resid, gain_before))


def gate_act(gate_val, up_val):
    return gelu_tanh(gate_val) * up_val


def after_feed(resid_one, feed_out, gain_after):
    return resid_one + rms(feed_out, gain_after)


def side_act(side_pre, side_in):
    return gelu_tanh(side_pre) * side_in


def finish(resid_two, side_out, gain_layer):
    return resid_two + rms(side_out, gain_layer)


def swap(value, axis):
    return lax.ppermute(value, axis, [(0, 1), (1, 0)])


def together(*values):
    return lax.optimization_barrier(values)


def split_columns(whole, widths):
    pieces = []
    offset = 0
    for width_one in widths:
        pieces.append(whole[..., offset : offset + width_one])
        offset = offset + width_one
    return pieces


class Plan:
    def __init__(self, seq_bits, dp_bits):
        self.seq = tuple("s%d" % i for i in range(seq_bits))
        self.dp = tuple("d%d" % i for i in range(dp_bits))
        self.every = self.seq + self.dp
        self.l, self.x = self.seq[-2:]
        self.c = self.dp[-1]
        self.team = (self.l, self.x, self.c)
        self.far_seq = self.seq[:-2]
        self.far_dp = self.dp[:-1]
        self.far = self.far_seq + self.far_dp
        self.canon = self.far + self.team
        self.order = self.far_seq + (self.l,) + self.far_dp + (self.x,)

    def flipped(self, value, axes, dims):
        for axis, dim in zip(axes, dims):
            value = jnp.where(lax.axis_index(axis) == 1, jnp.flip(value, dim), value)
        return value

    def to_far_team(self, value):
        rows, width = value.shape
        parts = value.reshape((rows,) + (2,) * len(self.every) + (-1,))
        order = [0] + [1 + self.every.index(axis) for axis in self.canon] + [1 + len(self.every)]
        return parts.transpose(order).reshape(rows, width)

    def from_far_team(self, value):
        rows, width = value.shape
        parts = value.reshape((rows,) + (2,) * len(self.every) + (-1,))
        order = [0] + [1 + self.canon.index(axis) for axis in self.every] + [1 + len(self.every)]
        return parts.transpose(order).reshape(rows, width)

    def spread_order(self, width):
        own = jnp.arange(width, dtype=jnp.int32).reshape((2,) * len(self.canon) + (-1,))
        own = self.flipped(own, self.canon, range(len(self.canon)))
        axes = (self.c,) + tuple(reversed(self.order))
        return own.transpose([self.canon.index(axis) for axis in axes] + [len(self.canon)]).reshape(-1)

    def grow(self, block, axes):
        for axis in axes:
            block = jnp.concatenate([block, swap(block, axis)], axis=0)
        return block

    def gather_pieces(self, block):
        return self.core_pieces(block, swap(block, self.order[-1]))

    def core_pieces(self, block, other):
        return [block, other, swap(block, self.c), swap(other, self.c)]

    def far_team_rows(self, pieces):
        axes = (self.c,) + tuple(reversed(self.order))
        whole = jnp.concatenate(pieces, axis=0)
        whole = whole.reshape((2,) * len(axes) + (-1, whole.shape[-1]))
        whole = whole.transpose([axes.index(axis) for axis in self.canon] + [len(axes), len(axes) + 1])
        whole = self.flipped(whole, self.canon, range(len(self.canon)))
        return whole.reshape((-1, whole.shape[-1]))

    def spread_begin(self, pairs):
        half = pairs[0][0].shape[1] // 2
        away = jnp.concatenate([product_tn(one[:, half:], two).astype(BF16) for one, two in pairs], axis=1)
        kept = jnp.concatenate([product_tn(one[:, :half], two).astype(BF16) for one, two in pairs], axis=1)
        return (kept.astype(F32) + swap(away, self.c).astype(F32)).astype(BF16)

    def spread_step(self, total, axes):
        for axis in axes:
            half = total.shape[0] // 2
            total = total[:half].astype(F32) + swap(total[half:], axis).astype(F32)
            if axis != self.order[0]:
                total = total.astype(BF16)
        return total

    def spread_send(self, total, axis):
        half = total.shape[0] // 2
        return total[:half].astype(F32), swap(total[half:], axis).astype(F32)

    def near_far(self, key, value):
        pair = jnp.stack([key, value])[:, None]
        for axis in reversed(self.far_seq):
            pair = jnp.concatenate([pair, swap(pair, axis)], axis=1)
        return pair

    def near_gather(self, pair):
        key, value = pair[0][None], pair[1][None]
        key = jnp.concatenate([key, swap(key, self.x)], axis=0)
        key = jnp.stack([key, swap(key, self.l)], axis=0)
        value = jnp.concatenate([value, swap(value, self.l)], axis=0)
        value = jnp.stack([value, swap(value, self.x)], axis=1)
        return [one.reshape((-1,) + one.shape[3:]) for one in (key, value)]

    def near_sum(self, key, value):
        def step(total, dim, axis):
            total = total.astype(BF16)
            away = swap(lax.index_in_dim(total, 1, dim, False), axis).astype(F32)
            return lax.index_in_dim(total, 0, dim, False).astype(F32) + away

        shape = (2, 2) + (2,) * len(self.far_seq)
        key, value = [one.reshape(shape + one.shape[1:]) for one in (key, value)]
        key = step(step(key, 0, self.l), 0, self.x)
        value = step(step(value, 1, self.x), 0, self.l)
        pair = jnp.stack([key, value])
        for axis in self.far_seq:
            pair = step(pair, 1, axis)
        return pair

    def near_places(self):
        place = jnp.zeros((1,), jnp.int32)
        for axis in (self.l, self.x) + self.far_seq:
            bit = lax.axis_index(axis)
            weight = 2 ** (len(self.seq) - 1 - self.seq.index(axis))
            place = (place[:, None] + weight * jnp.stack([bit, 1 - bit])[None, :]).reshape(-1)
        return place

    def to_rows(self, sums, local_rows):
        size = 2 ** len(self.team)
        sums = jnp.concatenate([one.reshape(size, local_rows, -1) for one in sums], axis=1)
        return lax.all_to_all(sums, self.team, split_axis=0, concat_axis=0, tiled=True)

    def total(self, value):
        for axis in reversed(self.every):
            value = value + swap(value, axis)
        return value

    def team_map(self, own, function):
        def chunk_of(piece):
            return jnp.concatenate([piece, swap(piece, self.c)], axis=0)

        by_x, by_l = swap(own, self.x), swap(own, self.l)
        chunks = [chunk_of(own)]
        results = [function(chunks[0])]
        by_x, by_l, results = together(by_x, by_l, results)
        half = own.shape[0] // 2
        both = jnp.concatenate([swap(by_x[:half], self.l), swap(by_l[half:], self.x)], axis=0)
        for piece in (by_x, by_l, both):
            chunks.append(chunk_of(piece))
            results.append(function(chunks[-1]))
        return chunks, results

    def core_sums(self, chunks):
        sums = []
        for chunk in chunks:
            rows = chunk.shape[0] // 2
            other = swap(chunk[rows:].astype(BF16), self.c)
            sums.append(chunk[:rows].astype(F32) + other.astype(F32))
        return sums

    def team_near(self, sums):
        own, by_x, by_l, both = sums
        half = own.shape[0] // 2
        both = both.astype(BF16)
        first = by_l[:half] + swap(both[:half], self.x).astype(F32)
        second = by_x[half:] + swap(both[half:], self.l).astype(F32)
        by_l = jnp.concatenate([first, by_l[half:]], axis=0).astype(BF16)
        by_x = jnp.concatenate([by_x[:half], second], axis=0).astype(BF16)
        return own, by_l, by_x

    def team_far(self, sums):
        own, by_l, by_x = sums
        return own + swap(by_l, self.l).astype(F32) + swap(by_x, self.x).astype(F32)


def product_split(left, pieces):
    width = left.shape[1] // len(pieces)
    return sum(product(left[:, i * width : (i + 1) * width], one) for i, one in enumerate(pieces))


def product_nt_split(left, pieces):
    return jnp.concatenate([product_nt(left, one) for one in pieces], axis=1)


def reorder(values, matrix):
    rows = values.shape[0]
    high = lax.reduce_precision(values, 8, 7)
    parts = jnp.concatenate([high.astype(BF16), (values - high).astype(BF16)], axis=0)
    parts = product_nt(parts, matrix)
    return parts[:rows] + parts[rows:]


def passed_along(value, axes, count, steps):
    initial, last = (max(0, -steps), min(count, count - steps))
    return lax.ppermute(value, axes, [(source, source + steps) for source in range(initial, last)])


def body(
    plan,
    tokens,
    per_layer,
    positions,
    span_start,
    cotangent,
    query_weight,
    key_weight,
    value_weight,
    output_weight,
    laurel_left,
    laurel_right,
    gate_weight,
    up_weight,
    down_weight,
    side_gate,
    side_output,
    norm_input,
    norm_attn,
    norm_laurel,
    norm_before,
    norm_after,
    norm_layer,
    norm_query,
    norm_key,
):
    batch, block, width = tokens.shape
    rows = batch * block
    head_size = norm_query.shape[0]
    heads = query_weight.shape[1] // head_size
    kv_heads = key_weight.shape[1] // head_size
    group = heads // kv_heads
    seq_count = 2 ** len(plan.seq)
    local_rows = gate_weight.shape[0]
    team_size = 2 ** len(plan.team)
    hidden_own = gate_weight.shape[1] // team_size

    kvl_widths = [
        key_weight.shape[1],
        value_weight.shape[1],
        laurel_left.shape[1],
        laurel_right.shape[1],
    ]
    rest_widths = [output_weight.shape[1], side_gate.shape[1], side_output.shape[1]]
    feed_local = jnp.concatenate(
        [
            one.reshape(local_rows, team_size, hidden_own).transpose(1, 0, 2)
            for one in (gate_weight, up_weight, down_weight)
        ],
        axis=1,
    )
    feed_team = lax.all_to_all(feed_local, plan.team, split_axis=0, concat_axis=0, tiled=True)
    feed_team = feed_team.reshape(team_size, 3, local_rows, hidden_own).transpose(1, 0, 2, 3)
    block_widths = [sum(kvl_widths), query_weight.shape[1], sum(rest_widths)]
    attn_block = jnp.concatenate(
        [key_weight, value_weight, laurel_left, laurel_right, query_weight]
        + [output_weight, side_gate, side_output],
        axis=1,
    )
    attn_block = plan.grow(attn_block, plan.far_seq)
    attn_block, feed_team = together(attn_block, feed_team)
    feed_full = lax.all_gather(feed_team.reshape(-1, hidden_own), plan.far, axis=0, tiled=True)
    attn_block = plan.grow(attn_block, (plan.l,))
    kvl_block, query_block, rest_block = split_columns(attn_block, block_widths)
    kvl_block = plan.grow(kvl_block, plan.far_dp)
    query_block = plan.grow(query_block, plan.far_dp)
    kvl_full = plan.gather_pieces(kvl_block)
    kvl_full, rest_block = together(kvl_full, rest_block)
    query_full = plan.gather_pieces(query_block)
    rest_block = plan.grow(rest_block, plan.far_dp)
    right_full = plan.far_team_rows([one[:, -kvl_widths[3] :] for one in kvl_full])
    kvl_full = [one[:, : -kvl_widths[3]] for one in kvl_full]

    places = jnp.arange(width, dtype=jnp.int32)
    far_team = plan.to_far_team(places[None])[0]
    to_far_team = (places[:, None] == far_team[None, :]).astype(BF16)
    to_spread = (places[:, None] == plan.spread_order(width)[None, :]).astype(BF16)
    gains = jnp.stack([norm_input, norm_attn, norm_laurel, norm_before, norm_after, norm_layer])
    norm_input, norm_attn, norm_laurel, norm_before, norm_after, norm_layer = plan.to_far_team(gains)
    inputs = product(tokens.reshape(rows, width), to_far_team)
    upstream = product(cotangent.reshape(rows, width), to_far_team)
    side_in = per_layer.astype(F32).reshape(rows, -1)
    normed, pre_pull = jax.vjp(rms, inputs, norm_input)
    normed_low = normed.astype(BF16)
    normed_spread = product(normed_low, to_spread).astype(BF16)
    keys, values, latent = split_columns(
        product_split(normed_spread, kvl_full), kvl_widths[:3]
    )
    queries = product_split(normed_spread, query_full).reshape(batch, block, heads, head_size)
    keys = keys.reshape(batch, block, kv_heads, head_size)
    values = values.reshape(batch, block, kv_heads, head_size)
    latent_low = latent.astype(BF16)

    def head_prep(query_in, key_in, value_in, gain_query, gain_key):
        return (
            rotate(rms(query_in, gain_query), positions),
            rotate(rms(key_in, gain_key), positions),
            rms(value_in, 1.0),
        )

    (rot_query, rot_key, rot_value), prep_pull = jax.vjp(
        head_prep, queries, keys, values, norm_query, norm_key
    )
    query_low = rot_query.astype(BF16)
    key_low = rot_key.astype(BF16)
    value_low = rot_value.astype(BF16)
    left_count = WINDOW // block
    right_count = (SPAN + block - 2) // block
    offsets = list(range(left_count, 0, -1)) + [0] + list(range(-1, -right_count - 1, -1))
    whole_sequence = seq_count <= len(offsets) + 1
    seq_index = lax.axis_index(plan.seq)
    total_length = block * seq_count
    if whole_sequence:
        key_low, value_low, rest_block = together(key_low, value_low, rest_block)
        pair_low = plan.near_far(key_low, value_low)
        keys_all, values_all = [
            one.swapaxes(0, 1).reshape(batch, total_length, kv_heads, head_size)
            for one in plan.near_gather(pair_low)
        ]
        key_blocks = plan.near_places()
    else:
        pair_low = jnp.stack([key_low, value_low])
        gathered = [
            passed_along(pair_low, plan.seq, seq_count, offset) if offset else pair_low
            for offset in offsets
        ]
        keys_all, values_all = jnp.concatenate(gathered, axis=2)
        key_blocks = seq_index - jnp.array(offsets, dtype=jnp.int32)
    key_count = keys_all.shape[1]
    rest_other = swap(rest_block, plan.order[-1])
    keys_all, values_all, rest_other = together(keys_all, values_all, rest_other)
    rest_full = plan.core_pieces(rest_block, rest_other)
    query_places = seq_index * block + jnp.arange(block, dtype=jnp.int32)
    key_places = (key_blocks[:, None] * block + jnp.arange(block, dtype=jnp.int32)).reshape(-1)
    in_query = (query_places[None, :, None] >= span_start[:, None, :]) & (
        query_places[None, :, None] < span_start[:, None, :] + SPAN
    )
    in_key = (key_places[None, :, None] >= span_start[:, None, :]) & (
        key_places[None, :, None] < span_start[:, None, :] + SPAN
    )
    same = jnp.any(in_query[:, :, None, :] & in_key[:, None, :, :], axis=-1)
    near = (key_places[None, :] <= query_places[:, None]) & (
        query_places[:, None] - key_places[None, :] < WINDOW
    )
    valid = (key_places >= 0) & (key_places < total_length)
    allowed = (valid[None, None, :] & (near[None] | same))[:, None, None]
    query_group = query_low.reshape(batch, block, kv_heads, group, head_size)
    scores = jnp.einsum("btkgd,bskd->bkgts", query_group, keys_all, preferred_element_type=F32)
    masked = jnp.where(allowed, scores, -1e30)
    top = jnp.max(masked, axis=-1, keepdims=True)
    expo = jnp.exp(masked - top)
    total = jnp.sum(expo, axis=-1, keepdims=True)
    probs = expo / total
    probs_low = probs.astype(BF16)
    attended = jnp.einsum("bkgts,bskd->btkgd", probs_low, values_all, preferred_element_type=F32)
    attended_low = attended.reshape(rows, heads * head_size).astype(BF16)
    attended_low, feed_full = together(attended_low, feed_full)
    output_full = [one[:, : rest_widths[0]] for one in rest_full]
    side_full = plan.far_team_rows([one[:, rest_widths[0] :] for one in rest_full])
    side_gate_full, side_output_full = split_columns(side_full, rest_widths[1:])
    attn_proj = reorder(product_nt_split(attended_low, output_full), to_spread)
    laurel = product_nt(latent_low, right_full)
    (resid_one, feed_in), mid_pull = jax.vjp(
        middle, inputs, normed, attn_proj, laurel, norm_attn, norm_laurel, norm_before
    )

    feed_low = feed_in.astype(BF16)
    feed_full = feed_full.reshape(-1, 3, team_size * local_rows, hidden_own)
    gate_full, up_full, down_full = [feed_full[:, at].reshape(width, hidden_own) for at in range(3)]
    pulls = []
    hidden_chunks = []

    def forward_chunk(chunk):
        hidden, pull = jax.vjp(gate_act, product(chunk, gate_full), product(chunk, up_full))
        hidden_low = hidden.astype(BF16)
        pulls.append(pull)
        hidden_chunks.append(hidden_low)
        return product_nt(hidden_low, down_full).astype(BF16)

    feed_chunks, feed_parts = plan.team_map(feed_low, forward_chunk)
    feed_out = plan.team_far(plan.team_near(plan.core_sums(feed_parts)))

    resid_two, after_pull = jax.vjp(after_feed, resid_one, feed_out, norm_after)
    resid_low = resid_two.astype(BF16)
    side_pre = product(resid_low, side_gate_full)
    side_val, side_pull = jax.vjp(side_act, side_pre, side_in)
    side_low = side_val.astype(BF16)
    side_out = product_nt(side_low, side_output_full)
    result, final_pull = jax.vjp(finish, resid_two, side_out, norm_layer)
    output = product_nt(result.astype(BF16), to_far_team).astype(BF16).reshape(batch, block, width)

    d_resid_two, d_side_out, grad_norm_layer = final_pull(upstream)
    d_side_out_low = d_side_out.astype(BF16)
    d_side = product(d_side_out_low, side_output_full)
    d_side_pre, d_side_in = side_pull(d_side)
    d_side_pre_low = d_side_pre.astype(BF16)
    d_resid_two = d_resid_two + product_nt(d_side_pre_low, side_gate_full)
    d_resid_one, d_feed_out, grad_norm_after = after_pull(d_resid_two)

    d_out_low = d_feed_out.astype(BF16)
    d_gate_chunks = []
    d_up_chunks = []

    def backward_chunk(chunk):
        d_gate, d_up = pulls[len(d_gate_chunks)](product(chunk, down_full))
        d_gate_chunks.append(d_gate.astype(BF16))
        d_up_chunks.append(d_up.astype(BF16))
        part = product_nt(d_gate_chunks[-1], gate_full) + product_nt(d_up_chunks[-1], up_full)
        return part.astype(BF16)

    d_out_chunks, d_feed_parts = plan.team_map(d_out_low, backward_chunk)
    d_feed_sums = plan.core_sums(d_feed_parts)
    d_gate_chunks, d_up_chunks, feed_chunks, d_out_chunks, hidden_chunks, d_feed_sums = together(
        d_gate_chunks, d_up_chunks, feed_chunks, d_out_chunks, hidden_chunks, d_feed_sums
    )
    feed_all = jnp.concatenate(feed_chunks, axis=0)
    d_out_all = jnp.concatenate(d_out_chunks, axis=0)
    feed_terms = jnp.stack(
        [
            product_tn(left, jnp.concatenate(right, axis=0))
            .astype(BF16)
            .reshape(-1, team_size * local_rows, hidden_own)
            for left, right in (
                (feed_all, d_gate_chunks),
                (feed_all, d_up_chunks),
                (d_out_all, hidden_chunks),
            )
        ],
        axis=1,
    )
    d_feed_in = plan.team_far(plan.team_near(d_feed_sums))
    d_feed_in, feed_terms = together(d_feed_in, feed_terms)
    feed_sum = lax.psum_scatter(
        feed_terms.reshape(-1, hidden_own), plan.far, scatter_dimension=0, tiled=True
    )
    steps = tuple(reversed(plan.order))

    (
        d_inputs,
        d_normed,
        d_attn_proj,
        d_laurel,
        grad_norm_attn,
        grad_norm_laurel,
        grad_norm_before,
    ) = mid_pull((d_resid_one, d_feed_in))
    d_attn_low = d_attn_proj.astype(BF16)
    d_laurel_low = d_laurel.astype(BF16)
    d_attn_spread = product(d_attn_low, to_spread).astype(BF16)
    d_latent_low = product(d_laurel_low, right_full).astype(BF16)
    output_sum = plan.spread_begin([(d_attn_spread, attended_low)])
    d_attn_spread, output_sum = together(d_attn_spread, output_sum)
    d_attended_low = product_split(d_attn_spread, output_full).astype(BF16)
    output_sum = plan.spread_step(output_sum, steps[:1])

    d_att = d_attended_low.reshape(batch, block, kv_heads, group, head_size)
    d_values_all = jnp.einsum("bkgts,btkgd->bskd", probs_low, d_att, preferred_element_type=F32)
    d_probs = jnp.einsum("btkgd,bskd->bkgts", d_att, values_all, preferred_element_type=F32)
    d_scores = probs * (d_probs - jnp.sum(probs * d_probs, axis=-1, keepdims=True))
    d_scores_low = d_scores.astype(BF16)
    d_query_rot = jnp.einsum("bkgts,bskd->btkgd", d_scores_low, keys_all, preferred_element_type=F32)
    d_keys_all = jnp.einsum(
        "bkgts,btkgd->bskd", d_scores_low, query_group, preferred_element_type=F32
    )
    d_keys_all, d_values_all, d_query_rot, output_sum, side_left = together(
        d_keys_all,
        d_values_all,
        d_query_rot,
        output_sum,
        jnp.concatenate([resid_low, d_side_out_low], axis=0),
    )
    side_left = product(side_left, to_spread).astype(BF16)
    side_sum = plan.spread_begin([(side_left[:rows], d_side_pre_low), (side_left[rows:], side_low)])
    side_sum = plan.spread_step(side_sum, steps[:1])
    if whole_sequence:
        d_pair_total = plan.near_sum(
            *[
                one.reshape(batch, seq_count, block, kv_heads, head_size).swapaxes(0, 1)
                for one in (d_keys_all, d_values_all)
            ]
        )
    else:
        d_pairs = jnp.stack([d_keys_all, d_values_all])
        d_pair_total = d_pairs[:, :, left_count * block : (left_count + 1) * block]
        for position, offset in enumerate(offsets):
            if offset != 0:
                piece = d_pairs[:, :, position * block : (position + 1) * block].astype(BF16)
                moved = passed_along(piece, plan.seq, seq_count, -offset)
                d_pair_total = d_pair_total + moved.astype(F32)
    d_queries, d_keys, d_values, grad_norm_query, grad_norm_key = prep_pull(
        (d_query_rot.reshape(batch, block, heads, head_size), d_pair_total[0], d_pair_total[1])
    )
    d_queries_low = d_queries.reshape(rows, -1).astype(BF16)
    query_sum = plan.spread_begin([(normed_spread, d_queries_low)])
    query_sum = plan.spread_step(query_sum, steps[:1])
    d_spread = product_nt_split(d_queries_low, query_full)
    d_keys, d_values, query_sum, output_sum, side_sum, d_spread, feed_sum = together(
        d_keys, d_values, query_sum, output_sum, side_sum, d_spread, feed_sum
    )
    output_sum = jnp.concatenate([output_sum, side_sum], axis=1)
    d_kvl_low = jnp.concatenate(
        [
            d_keys.reshape(rows, -1).astype(BF16),
            d_values.reshape(rows, -1).astype(BF16),
            d_latent_low,
        ],
        axis=1,
    )
    laurel_spread = product(d_laurel_low, to_spread).astype(BF16)
    kvl_sum = plan.spread_begin([(normed_spread, d_kvl_low), (laurel_spread, latent_low)])
    kvl_sum, d_kvl_low = together(kvl_sum, d_kvl_low)
    query_kept, query_away = plan.spread_send(query_sum, steps[1])
    output_kept, output_away = plan.spread_send(output_sum, steps[1])
    kvl_sum = plan.spread_step(kvl_sum, steps[:1])
    d_spread = d_spread + product_nt_split(d_kvl_low, kvl_full)
    kvl_sum, query_kept, output_kept, d_spread = together(
        kvl_sum, query_kept, output_kept, d_spread
    )
    feed_rows = plan.to_rows(jnp.split(feed_sum, 3), local_rows)
    query_sum = (query_kept + query_away).astype(BF16)
    output_sum = (output_kept + output_away).astype(BF16)
    kvl_sum = plan.spread_step(kvl_sum, steps[1:2])
    query_sum = plan.spread_step(query_sum, steps[2:3])
    output_sum = plan.spread_step(output_sum, steps[2:3])
    d_normed = d_normed + reorder(d_spread, to_spread)
    d_inputs_norm, grad_norm_input = pre_pull(d_normed)
    grad_tokens = reorder(d_inputs + d_inputs_norm, to_far_team).reshape(batch, block, width)
    grad_side = d_side_in.reshape(batch, block, -1)
    norm_grads = jnp.stack(
        [
            grad_norm_input,
            grad_norm_attn,
            grad_norm_laurel,
            grad_norm_before,
            grad_norm_after,
            grad_norm_layer,
        ]
    )
    gain_grads = jnp.concatenate(
        [plan.from_far_team(norm_grads).reshape(-1), grad_norm_query, grad_norm_key]
    )
    grad_query = plan.spread_step(query_sum, steps[3:])
    output_sum = plan.spread_step(output_sum, steps[3:])
    kvl_sum = plan.spread_step(kvl_sum, steps[2:3])
    gain_grads, grad_query, output_sum, kvl_sum, feed_rows = together(
        gain_grads, grad_query, output_sum, kvl_sum, feed_rows
    )
    grad_gate, grad_up, grad_down = [
        jnp.concatenate(
            [feed_rows[at, first : first + local_rows] for at in range(team_size)], axis=1
        ).astype(F32)
        for first in range(0, 3 * local_rows, local_rows)
    ]
    grad_output, grad_side_gate, grad_side_output = split_columns(output_sum, rest_widths)
    grad_key, grad_value, grad_left, grad_right = split_columns(
        plan.spread_step(kvl_sum, steps[3:]), kvl_widths
    )
    gain_grads = plan.total(gain_grads)
    gain_parts = split_columns(gain_grads, [width] * 6 + [head_size] * 2)
    return (
        output,
        grad_tokens,
        grad_side,
        grad_query,
        grad_key,
        grad_value,
        grad_output,
        grad_left,
        grad_right,
        grad_gate,
        grad_up,
        grad_down,
        grad_side_gate,
        grad_side_output,
    ) + tuple(gain_parts)


def solution(mesh):
    seq_bits = int(math.log2(mesh.shape["seq"]))
    dp_bits = int(math.log2(mesh.shape["dp"]))
    plan = Plan(seq_bits, dp_bits)
    binary = Mesh(mesh.devices.reshape((2,) * (seq_bits + dp_bits)), plan.every)
    token_spec = P(plan.dp, plan.seq, None)
    weight_spec = P(plan.every, None)

    def step(*arrays):
        return body(plan, *arrays)

    return jax.shard_map(
        step,
        mesh=binary,
        in_specs=(token_spec, token_spec, P(plan.dp, plan.seq), P(plan.dp, None), token_spec)
        + (weight_spec,) * 11
        + (P(),) * 8,
        out_specs=(token_spec,) * 3 + (weight_spec,) * 11 + (P(),) * 8,
        check_vma=False,
    )
```
